32 devices in a mesh: groups: 2 (over x), blk: 4 (over y, core), tsplit: 4 (over z).
Axes of the slice: x: 2, y: 2, z: 4, core: 2. Of those that a mesh axis runs over, the one named last changes fastest.
Arguments:
- sources: bfloat16 [2048, 512], P(('groups', 'blk')), parts along dimension 0, may hold values from -4 to 4
- targets: bfloat16 [32768, 512], P(('groups', 'blk', 'tsplit')), parts along dimension 0, may hold values from -4 to 4
- tgt_potential: float32 [32768], P(('groups', 'blk', 'tsplit')), parts along dimension 0, may hold values from -1 to 1
- src_logmass: float32 [2048], P(('groups', 'blk')), parts along dimension 0, may hold values from -9.5 to -7.5
- tgt_logmass: float32 [32768], P(('groups', 'blk', 'tsplit')), parts along dimension 0, may hold values from -12 to -10
- src_exponent: float32 [2048], P(('groups', 'blk')), parts along dimension 0, may hold values from 0.4 to 0.95
- tgt_exponent: float32 [32768], P(('groups', 'blk', 'tsplit')), parts along dimension 0, may hold values from 0.4 to 0.95
Outputs:
- src_potential: float32 [2048], P(('groups', 'blk')), parts along dimension 0
- tgt_update: float32 [32768], P(('groups', 'blk', 'tsplit')), parts along dimension 0
The draws below stay inside these ranges and needn't reach their ends.
There are 2 independent parts, one for each index of `groups`. The reference program is written for one: setup_inputs(seed, part) draws one part's arguments, and reference() takes and returns one part's arrays. A program takes and returns all parts, laid end to end along the dimension named above; each array names one. Nothing has to cross between parts.
All inputs are finite; a program needn't handle non-finite values.
Results may differ from the reference program's by a relative error of at most 0.0003.
Values may be sent and summed in bfloat16 or wider, within the bound.
No kernel may reach another device: no remote copies, remote signals or barrier semaphores. Data moves between devices by JAX's collectives and lax.ppermute only.
A program may use at most 64 MiB of HBM per device.

```python
import jax
import jax.numpy as jnp
from jax import lax

E = 512
T_BLK = 1024
NS = 1024
NT = 16384


def embed_pair(key, spread):
    key_src, key_tgt, key_srow, key_trow, key_noise, key_sign, key_mag, key_snoise = jax.random.split(key, 8)
    src_draw = 0.1 * jax.random.normal(key_src, (NS, E), jnp.float32)
    tgt_draw = 0.1 * jax.random.normal(key_tgt, (NT, E), jnp.float32)
    src_scale = jnp.exp(jnp.log(spread) * jax.random.uniform(key_srow, (NS, 1), jnp.float32))
    tgt_scale = jnp.exp(jnp.log(spread) * jax.random.uniform(key_trow, (NT, 1), jnp.float32))
    src_draw = src_draw * src_scale
    tgt_draw = tgt_draw * tgt_scale
    anchor_index = jnp.arange(16, dtype=jnp.int32) * (NT // 16)
    signs = jnp.where(jax.random.uniform(key_sign, (16, E), jnp.float32) < 0.5, -1.0, 1.0)
    direction = signs * jax.random.uniform(key_mag, (16, E), jnp.float32, 0.5, 1.0)
    direction = direction / jnp.sqrt(jnp.sum(direction * direction, axis=1, keepdims=True))
    strength = 60.0 * jnp.exp(jnp.log(400.0 / 60.0) * jnp.arange(16, dtype=jnp.float32) / 15.0)
    anchors = direction * jnp.sqrt(strength / 2.0)[:, None]
    noise_scale = (0.75 / E) ** 0.5
    nudged = anchors + noise_scale * jax.random.normal(key_noise, (16, E), jnp.float32)
    src_nudged = anchors + noise_scale * jax.random.normal(key_snoise, (16, E), jnp.float32)
    tgt_draw = tgt_draw.at[anchor_index].set(anchors)
    tgt_draw = tgt_draw.at[anchor_index + 1].set(nudged)
    src_draw = src_draw.at[:16].set(anchors)
    src_draw = src_draw.at[16:32].set(src_nudged)
    return (jnp.clip(src_draw, -4.0, 4.0), jnp.clip(tgt_draw, -4.0, 4.0))


def draw_sources(key, part):
    paired = embed_pair(key, 1.0)
    return paired[0].astype(jnp.bfloat16)


def draw_targets(key, part):
    paired = embed_pair(key, 1.0)
    return paired[1].astype(jnp.bfloat16)


def block_levels(key, extent, cuts, least, largest):
    gain = 1.0
    for axis_at, blocks in cuts:
        heights = jax.random.uniform(jax.random.fold_in(jax.random.fold_in(key, 6), axis_at), (blocks,), jnp.float32, least / len(cuts), largest / len(cuts))
        gain = gain * jnp.repeat(jnp.exp(heights), extent[axis_at] // blocks).reshape((-1,) + (1,) * (len(extent) - 1 - axis_at))
    return gain


def setup_inputs(seed: int = 0, part: int = 0) -> dict:
    key_of = jax.random.split(jax.random.key(seed), 8)
    own_keys = jax.random.split(jax.random.fold_in(key_of[7], part), 8)
    sources = draw_sources(jax.random.fold_in(jax.random.fold_in(key_of[7], part), 71), part)
    targets = draw_targets(jax.random.fold_in(jax.random.fold_in(key_of[7], part), 71), part)
    tgt_potential = jnp.clip(jax.random.uniform(own_keys[2], (NT,), jnp.float32, -1.0, 1.0) * block_levels(own_keys[2], (NT,), ((0, 16),), -0.4, 0.0), -1.0, 1.0)
    src_logmass = jnp.clip(-9.5 + 2.0 * jax.random.uniform(own_keys[3], (NS,), jnp.float32) ** block_levels(own_keys[3], (NS,), ((0, 4),), -0.2, 0.2), -9.5, -7.5)
    tgt_logmass = jnp.clip(-12.0 + 2.0 * jax.random.uniform(own_keys[4], (NT,), jnp.float32) ** block_levels(own_keys[4], (NT,), ((0, 16),), -0.2, 0.2), -12.0, -10.0)
    src_exponent = jnp.clip(0.4 + 0.54999998 * jax.random.uniform(own_keys[5], (NS,), jnp.float32) ** block_levels(own_keys[5], (NS,), ((0, 4),), -0.2, 0.2), 0.4, 0.95)
    tgt_exponent = jnp.clip(0.4 + 0.54999998 * jax.random.uniform(own_keys[6], (NT,), jnp.float32) ** block_levels(own_keys[6], (NT,), ((0, 16),), -0.2, 0.2), 0.4, 0.95)
    return {"sources": sources, "targets": targets, "tgt_potential": tgt_potential, "src_logmass": src_logmass, "tgt_logmass": tgt_logmass, "src_exponent": src_exponent, "tgt_exponent": tgt_exponent}


EPSILON = 0.5
LOGIT_SCALE = 2.0 / EPSILON


def reference(sources, targets, tgt_potential, src_logmass, tgt_logmass, src_exponent, tgt_exponent):
    src_float = sources.astype(jnp.float32)
    src_sq = jnp.sum(src_float * src_float, axis=1) / EPSILON
    tgt_float = targets.astype(jnp.float32)
    tgt_sq = jnp.sum(tgt_float * tgt_float, axis=1) / EPSILON
    tgt_offset = tgt_potential + tgt_logmass - tgt_sq
    block_count = NT // T_BLK
    tgt_blocks = targets.reshape(block_count, T_BLK, E)
    offset_blocks = tgt_offset.reshape(block_count, T_BLK)

    def row_step(state_pair, pieces):
        running_peak, running_mass = state_pair
        key_rows, offsets = pieces
        logits = LOGIT_SCALE * jnp.dot(sources, key_rows.T, preferred_element_type=jnp.float32) + offsets[None, :]
        new_peak = jnp.maximum(running_peak, jnp.max(logits, axis=1))
        running_mass = running_mass * jnp.exp(running_peak - new_peak) + jnp.sum(jnp.exp(logits - new_peak[:, None]), axis=1)
        return (new_peak, running_mass), None

    start_pair = (jnp.full((NS,), -jnp.inf, jnp.float32), jnp.zeros((NS,), jnp.float32))
    (row_peak, row_mass), _ = lax.scan(row_step, start_pair, (tgt_blocks, offset_blocks))
    row_lse = row_peak + jnp.log(row_mass) - src_sq
    src_potential = src_exponent * (src_logmass - row_lse)
    src_offset = src_potential + src_logmass - src_sq

    def column_step(unused, pieces):
        key_rows, squares = pieces
        logits = LOGIT_SCALE * jnp.dot(key_rows, sources.T, preferred_element_type=jnp.float32) + src_offset[None, :]
        column_peak = jnp.max(logits, axis=1)
        column_lse = column_peak + jnp.log(jnp.sum(jnp.exp(logits - column_peak[:, None]), axis=1)) - squares
        return unused, column_lse

    _, column_lse = lax.scan(column_step, jnp.zeros((), jnp.float32), (tgt_blocks, tgt_sq.reshape(block_count, T_BLK)))
    tgt_update = tgt_exponent * (tgt_logmass - column_lse.reshape(NT))
    return src_potential, tgt_update
```

```python
import functools

import jax
import jax.numpy as jnp
from jax import lax
from jax.experimental import pallas as pl
from jax.experimental.pallas import tpu as pltpu
from jax.sharding import PartitionSpec as P

EPSILON = 0.5
LOGIT_SCALE = 2.0 / EPSILON
LANES = 128
CHUNK = 256
VMEM = pl.BlockSpec(memory_space=pltpu.VMEM)
SMEM = pl.BlockSpec(memory_space=pltpu.SMEM)
NT_DIMS = (((1,), (1,)), ((), ()))


def diagonal():
    rows = lax.broadcasted_iota(jnp.int32, (LANES, LANES), 0)
    cols = lax.broadcasted_iota(jnp.int32, (LANES, LANES), 1)
    return rows == cols


def to_lanes(column, eye):
    return jnp.sum(jnp.where(eye, column, 0.0), axis=0, keepdims=True)


def to_column(lanes, eye):
    return jnp.sum(jnp.where(eye, lanes, 0.0), axis=1, keepdims=True)


def fold_rows(value, op):
    return op(value.reshape(value.shape[0] // 8, 8, value.shape[1]), axis=0)


def row_block(rows_ref, tgt_ref, offset_ref, logit_ref, slot):
    tgt_count = tgt_ref.shape[0]
    rows = rows_ref[...]
    peak = None
    for at in range(0, tgt_count, CHUNK):
        part = pl.ds(at, CHUNK)
        logits = LOGIT_SCALE * lax.dot_general(tgt_ref[part, :], rows, NT_DIMS, preferred_element_type=jnp.float32)
        logit_ref[slot, part, :] = logits
        high = fold_rows(logits + offset_ref[part, :1], jnp.max)
        peak = high if peak is None else jnp.maximum(peak, high)
    peak = jnp.max(peak, axis=0, keepdims=True)
    mass = None
    for at in range(0, tgt_count, CHUNK):
        part = pl.ds(at, CHUNK)
        term = jnp.exp(logit_ref[slot, part, :] + (offset_ref[part, :1] - peak))
        term = fold_rows(term, jnp.sum)
        mass = term if mass is None else mass + term
    mass = jnp.sum(mass, axis=0, keepdims=True)
    return peak + jnp.log(mass)


def near_kernel(own_ref, pair_ref, tgt_ref, pot_ref, mass_ref, logit_ref, lse_ref, offset_ref, tsq_ref, ssq_ref):
    eye = diagonal()
    tgt_count = tgt_ref.shape[0]
    for group in range(tgt_count // LANES):
        part = pl.ds(group * LANES, LANES)
        rows = tgt_ref[part, :].astype(jnp.float32)
        square = jnp.sum(rows * rows, axis=1, keepdims=True) / EPSILON
        offset = to_column(pot_ref[group : group + 1, :] + mass_ref[group : group + 1, :], eye) - square
        offset_ref[part, :] = jnp.broadcast_to(offset, (LANES, LANES))
        tsq_ref[group : group + 1, :] = to_lanes(square, eye)
    for group in range(own_ref.shape[0] // LANES):
        rows = own_ref[pl.ds(group * LANES, LANES), :].astype(jnp.float32)
        square = jnp.sum(rows * rows, axis=1, keepdims=True) / EPSILON
        ssq_ref[group : group + 1, :] = to_lanes(square, eye)
    lse_ref[0:1, :] = row_block(own_ref, tgt_ref, offset_ref, logit_ref, 0)
    lse_ref[1:2, :] = row_block(pair_ref, tgt_ref, offset_ref, logit_ref, 1)


def far_kernel(count, *refs):
    blocks = refs[:count]
    tgt_ref, offset_ref, logit_ref, lse_ref = refs[count:]
    for slot in range(count):
        lse_ref[slot : slot + 1, :] = row_block(blocks[slot], tgt_ref, offset_ref, logit_ref, slot)


def column_kernel(order_ref, near_ref, far_ref, srcoff_ref, tsq_ref, mass_ref, expo_ref, out_ref, off_ref):
    eye = diagonal()
    near = near_ref.shape[0]
    far = far_ref.shape[0]
    src_count = near_ref.shape[2]
    tgt_count = near_ref.shape[1]
    for slot in range(near + far):
        off_ref[slot : slot + 1, :] = srcoff_ref[pl.ds(order_ref[slot], 1), :]

    def logits(slot, part):
        held = near_ref[slot, part, :] if slot < near else far_ref[slot - near, part, :]
        return held + off_ref[slot : slot + 1, :]

    def fold_lanes(value, op):
        out = value[:, :LANES]
        for at in range(LANES, src_count, LANES):
            out = op(out, value[:, at : at + LANES])
        return out

    for group in range(tgt_count // LANES):
        part = pl.ds(group * LANES, LANES)
        peak = None
        for slot in range(near + far):
            high = fold_lanes(logits(slot, part), jnp.maximum)
            peak = high if peak is None else jnp.maximum(peak, high)
        peak = jnp.max(peak, axis=1, keepdims=True)
        mass = None
        for slot in range(near + far):
            term = fold_lanes(jnp.exp(logits(slot, part) - peak), jnp.add)
            mass = term if mass is None else mass + term
        mass = jnp.sum(mass, axis=1, keepdims=True)
        row = slice(group, group + 1)
        lse = to_lanes(peak, eye) + jnp.log(to_lanes(mass, eye)) - tsq_ref[row, :]
        out_ref[row, :] = expo_ref[row, :] * (mass_ref[row, :] - lse)


def f32(*shape):
    return jax.ShapeDtypeStruct(shape, jnp.float32)


def params():
    return pltpu.CompilerParams(vmem_limit_bytes=48 * 1024 * 1024)


def shards(sources, targets, tgt_potential, src_logmass, tgt_logmass, src_exponent, tgt_exponent):
    src_count, width = sources.shape
    tgt_count = targets.shape[0]
    slabs = lax.axis_size("blk")
    sets = lax.axis_size("tsplit")
    chips = slabs // 2
    groups = tgt_count // LANES
    me = lax.axis_index("blk")

    pair_way = [(i, i ^ 1) for i in range(slabs)]
    pair = lax.ppermute(sources, "blk", pair_way)
    straight = [
        lax.ppermute(sources, "blk", [(i, (i + 2 * step) % slabs) for i in range(slabs)]) for step in range(1, chips)
    ]
    crossed = [lax.ppermute(block, "blk", pair_way) for block in straight]
    far_blocks = straight + crossed
    origin = [(me + slabs - 2 * step) % slabs for step in range(1, chips)]
    order = jnp.stack([me, me ^ 1] + origin + [at ^ 1 for at in origin]).astype(jnp.int32)

    potential = tgt_potential.reshape(groups, LANES)
    logmass = tgt_logmass.reshape(groups, LANES)
    exponent = tgt_exponent.reshape(groups, LANES)

    pair_flops = 2 * src_count * tgt_count * width
    near_logits, near_lse, offset, tgt_sq, src_sq = pl.pallas_call(
        near_kernel,
        out_shape=(
            f32(2, tgt_count, src_count),
            f32(2, src_count),
            f32(tgt_count, LANES),
            f32(groups, LANES),
            f32(src_count // LANES, LANES),
        ),
        in_specs=[VMEM] * 5,
        out_specs=(VMEM,) * 5,
        compiler_params=params(),
        cost_estimate=pl.CostEstimate(
            flops=2 * pair_flops, bytes_accessed=4 * 2**20, transcendentals=2 * src_count * tgt_count
        ),
        name="near_rows",
    )(sources, pair, targets, potential, logmass)
    far = len(far_blocks)
    far_logits, far_lse = pl.pallas_call(
        functools.partial(far_kernel, far),
        out_shape=(f32(far, tgt_count, src_count), f32(far, src_count)),
        in_specs=[VMEM] * (far + 2),
        out_specs=(VMEM,) * 2,
        compiler_params=params(),
        cost_estimate=pl.CostEstimate(
            flops=far * pair_flops, bytes_accessed=4 * 2**20, transcendentals=far * src_count * tgt_count
        ),
        name="far_rows",
    )(*far_blocks, targets, offset)

    own_sq = src_sq.reshape(src_count)
    partial_lse = jnp.concatenate([near_lse, far_lse])
    placed = order[None, :, None] == jnp.arange(slabs, dtype=jnp.int32)[:, None, None]
    partial_lse = jnp.sum(jnp.where(placed, partial_lse[None], 0.0), axis=1).reshape(-1)
    shift = src_exponent * (src_logmass + own_sq) + src_logmass - own_sq
    payload = jnp.concatenate([partial_lse, src_exponent, shift])
    everyone = lax.all_gather(payload, ("blk", "tsplit"), axis=0, tiled=False)
    total = slabs * src_count
    lses = everyone[:, :total]
    peak = jnp.max(lses, axis=0)
    lse = peak + jnp.log(jnp.sum(jnp.exp(lses - peak[None, :]), axis=0))
    homes = everyone.reshape(slabs, sets, -1)[:, 0, total:]
    slopes = homes[:, :src_count].reshape(total)
    shifts = homes[:, src_count:].reshape(total)
    src_offset = (shifts - slopes * lse).reshape(slabs, src_count)
    own_lse = lax.dynamic_slice_in_dim(lse, me * src_count, src_count) - own_sq
    src_potential = src_exponent * (src_logmass - own_lse)

    tgt_update = pl.pallas_call(
        column_kernel,
        out_shape=f32(groups, LANES),
        in_specs=[SMEM] + [VMEM] * 6,
        out_specs=VMEM,
        scratch_shapes=[pltpu.VMEM((slabs, src_count), jnp.float32)],
        compiler_params=params(),
        name="columns",
    )(order, near_logits, far_logits, src_offset, tgt_sq, logmass, exponent)
    return (src_potential, tgt_update.reshape(tgt_count))


def solution(mesh):
    placed = (
        P(("groups", "blk"), None),
        P(("groups", "blk", "tsplit"), None),
        P(("groups", "blk", "tsplit")),
        P(("groups", "blk")),
        P(("groups", "blk", "tsplit")),
        P(("groups", "blk")),
        P(("groups", "blk", "tsplit")),
    )
    return jax.shard_map(
        shards,
        mesh=mesh,
        in_specs=placed,
        out_specs=(P(("groups", "blk")), P(("groups", "blk", "tsplit"))),
        check_vma=False,
    )
```

```python
import functools

import jax
import jax.numpy as jnp
from jax import lax
from jax.experimental import pallas as pl
from jax.experimental.pallas import tpu as pltpu
from jax.sharding import PartitionSpec as P

EPSILON = 0.5
LOGIT_SCALE = 2.0 / EPSILON
LANES = 128
CHUNK = 256
VMEM = pl.BlockSpec(memory_space=pltpu.VMEM)
NT_DIMS = (((1,), (1,)), ((), ()))


def diagonal():
    rows = lax.broadcasted_iota(jnp.int32, (LANES, LANES), 0)
    cols = lax.broadcasted_iota(jnp.int32, (LANES, LANES), 1)
    return rows == cols


def to_lanes(column, eye):
    return jnp.sum(jnp.where(eye, column, 0.0), axis=0, keepdims=True)


def to_column(lanes, eye):
    return jnp.sum(jnp.where(eye, lanes, 0.0), axis=1, keepdims=True)


def fold_rows(value, op):
    return op(value.reshape(value.shape[0] // 8, 8, value.shape[1]), axis=0)


def row_block(rows_ref, tgt_refs, offset_ref, z_at, lse_at, eye):
    rows = rows_ref[...] * LOGIT_SCALE
    src_count = rows.shape[0]
    tgt_count = tgt_refs[0].shape[0]
    peak = None
    for half, tgt_ref in enumerate(tgt_refs):
        for at in range(0, tgt_count, CHUNK):
            cols = slice(half * tgt_count + at, half * tgt_count + at + CHUNK)
            dots = lax.dot_general(rows, tgt_ref[at : at + CHUNK, :], NT_DIMS, preferred_element_type=jnp.float32)
            z = dots + offset_ref[:, cols]
            z_at[:, cols] = z
            for lane in range(0, CHUNK, LANES):
                part = z[:, lane : lane + LANES]
                peak = part if peak is None else jnp.maximum(peak, part)
    peak = jnp.max(peak, axis=1, keepdims=True)
    mass = None
    for at in range(0, len(tgt_refs) * tgt_count, LANES):
        term = jnp.exp(z_at[:, at : at + LANES] - peak)
        mass = term if mass is None else mass + term
    mass = jnp.sum(mass, axis=1, keepdims=True)
    for at in range(0, src_count, LANES):
        part = slice(at, at + LANES)
        lse_at[:, part] = to_lanes(peak[part], eye) + jnp.log(to_lanes(mass[part], eye))


def near_kernel(src_ref, own_ref, pair_ref, own_base_ref, pair_base_ref, z_ref, lse_ref, offset_ref):
    eye = diagonal()
    tgt_count = own_ref.shape[0]
    for half, (tgt_ref, base_ref) in enumerate(((own_ref, own_base_ref), (pair_ref, pair_base_ref))):
        for group in range(tgt_count // LANES):
            rows = tgt_ref[group * LANES : (group + 1) * LANES, :].astype(jnp.float32)
            square = jnp.sum(rows * rows, axis=1, keepdims=True) / EPSILON
            at = half * tgt_count + group * LANES
            offset_ref[:, at : at + LANES] = base_ref[group : group + 1, :] - to_lanes(square, eye)
    row_block(src_ref, (own_ref, pair_ref), offset_ref, z_ref, lse_ref, eye)


def far_kernel(count, *refs):
    eye = diagonal()
    blocks = refs[:count]
    own_ref, pair_ref, offset_ref, z_ref, lse_ref = refs[count:]
    for slot in range(count):
        row_block(
            blocks[slot], (own_ref, pair_ref), offset_ref, z_ref.at[slot], lse_ref.at[slot], eye
        )


def column_kernel(
    near_ref, far_ref, lse_ref, slope_ref, shift_ref, mass_ref, sq_ref, own_ref, pair_ref, potential_ref, off_ref
):
    eye = diagonal()
    slots, src_count = lse_ref.shape
    tgt_count = near_ref.shape[1] // 2
    lse = lse_ref[...]
    potential_ref[...] = slope_ref[0:1, :] * (mass_ref[...] - (lse[0:1, :] - sq_ref[...]))
    offset = shift_ref[...] - slope_ref[...] * lse
    for slot in range(slots):
        for at in range(0, src_count, LANES):
            column = to_column(offset[slot : slot + 1, at : at + LANES], eye)
            off_ref[slot, at : at + LANES, :] = jnp.broadcast_to(column, (LANES, LANES))

    def held(slot, cols):
        z = near_ref[:, cols] if slot == 0 else far_ref[slot - 1, :, cols]
        return z + off_ref[slot]

    for at in range(0, 2 * tgt_count, LANES):
        cols = slice(at, at + LANES)
        peak = None
        for slot in range(slots):
            high = fold_rows(held(slot, cols), jnp.max)
            peak = high if peak is None else jnp.maximum(peak, high)
        peak = jnp.max(peak, axis=0, keepdims=True)
        mass = None
        for slot in range(slots):
            term = fold_rows(jnp.exp(held(slot, cols) - peak), jnp.sum)
            mass = term if mass is None else mass + term
        mass = jnp.sum(mass, axis=0, keepdims=True)
        group = at // LANES
        if at < tgt_count:
            own_ref[group : group + 1, :] = peak + jnp.log(mass)
        else:
            group -= tgt_count // LANES
            pair_ref[group : group + 1, :] = peak + jnp.log(mass)


def f32(*shape):
    return jax.ShapeDtypeStruct(shape, jnp.float32)


def params():
    return pltpu.CompilerParams(vmem_limit_bytes=32 * 1024 * 1024)


def merge(left, right):
    peak = jnp.maximum(left, right)
    return peak + jnp.log(jnp.exp(left - peak) + jnp.exp(right - peak))


def shards(sources, targets, tgt_potential, src_logmass, tgt_logmass, src_exponent, tgt_exponent):
    src_count, width = sources.shape
    tgt_count = targets.shape[0]
    slabs = lax.axis_size("blk")
    sets = lax.axis_size("tsplit")
    chips = slabs // 2
    groups = tgt_count // LANES
    assert chips & (chips - 1) == 0 and sets & (sets - 1) == 0

    def pair(value):
        return lax.ppermute(value, "blk", [(i, i ^ 1) for i in range(slabs)])

    def across(value, chip):
        return lax.ppermute(value, "blk", [(i, i ^ (2 * chip)) for i in range(slabs)])

    def along(value, step):
        return lax.ppermute(value, "tsplit", [(i, i ^ step) for i in range(sets)])

    far_blocks = [across(sources, chip) for chip in range(1, chips)]
    pair_targets = pair(targets)
    base = (tgt_potential + tgt_logmass).reshape(groups, LANES)
    pair_base = pair(base)
    own_sq = jnp.sum(jnp.square(sources.astype(jnp.float32)), axis=1) / EPSILON
    shift = src_exponent * (src_logmass + own_sq) + src_logmass - own_sq
    line = jnp.stack([src_exponent, shift])
    lines = jnp.stack([line] + [across(line, chip) for chip in range(1, chips)])

    block_pairs = src_count * 2 * tgt_count

    def cost(blocks):
        return pl.CostEstimate(
            flops=2 * blocks * block_pairs * width, bytes_accessed=2 * 2**20, transcendentals=blocks * block_pairs
        )

    near_z, near_lse, offset = pl.pallas_call(
        near_kernel,
        out_shape=(f32(src_count, 2 * tgt_count), f32(1, src_count), f32(1, 2 * tgt_count)),
        in_specs=[VMEM] * 5,
        out_specs=(VMEM,) * 3,
        compiler_params=params(),
        cost_estimate=cost(1),
        name="near_rows",
    )(sources, targets, pair_targets, base, pair_base)
    far = chips - 1
    far_z, far_lse = pl.pallas_call(
        functools.partial(far_kernel, far),
        out_shape=(f32(far, src_count, 2 * tgt_count), f32(far, 1, src_count)),
        in_specs=[VMEM] * (far + 3),
        out_specs=(VMEM,) * 2,
        compiler_params=params(),
        cost_estimate=cost(far),
        name="far_rows",
    )(*far_blocks, targets, pair_targets, offset)

    lse = jnp.concatenate([near_lse, far_lse.reshape(far, src_count)])
    chip = 1
    while chip < chips:
        other = across(lse, chip)
        lse = merge(lse, jnp.stack([other[slot ^ chip] for slot in range(chips)]))
        chip *= 2
    step = 1
    while step < sets:
        lse = merge(lse, along(lse, step))
        step *= 2

    own_part, pair_part, src_potential = pl.pallas_call(
        column_kernel,
        out_shape=(f32(groups, LANES), f32(groups, LANES), f32(1, src_count)),
        in_specs=[VMEM] * 7,
        out_specs=(VMEM,) * 3,
        scratch_shapes=[pltpu.VMEM((chips, src_count, LANES), jnp.float32)],
        compiler_params=params(),
        cost_estimate=cost(chips),
        name="columns",
    )(near_z, far_z, lse, lines[:, 0], lines[:, 1], src_logmass.reshape(1, -1), own_sq.reshape(1, -1))
    columns = merge(own_part, pair(pair_part)).reshape(tgt_count)
    tgt_update = tgt_exponent * (2.0 * tgt_logmass + tgt_potential - columns)
    return (src_potential.reshape(src_count), tgt_update)


def solution(mesh):
    placed = (
        P(("groups", "blk"), None),
        P(("groups", "blk", "tsplit"), None),
        P(("groups", "blk", "tsplit")),
        P(("groups", "blk")),
        P(("groups", "blk", "tsplit")),
        P(("groups", "blk")),
        P(("groups", "blk", "tsplit")),
    )
    return jax.shard_map(
        shards,
        mesh=mesh,
        in_specs=placed,
        out_specs=(P(("groups", "blk")), P(("groups", "blk", "tsplit"))),
        check_vma=False,
    )
```

```python
import functools

import jax
import jax.numpy as jnp
from jax import lax
from jax.experimental import pallas as pl
from jax.experimental.pallas import tpu as pltpu
from jax.sharding import PartitionSpec as P

EPSILON = 0.5
LOGIT_SCALE = 2.0 / EPSILON
LANES = 128
CHUNK = 256
VMEM = pl.BlockSpec(memory_space=pltpu.VMEM)
SMEM = pl.BlockSpec(memory_space=pltpu.SMEM)
HBM = pl.BlockSpec(memory_space=pltpu.HBM)
NT_DIMS = (((1,), (1,)), ((), ()))


def diagonal():
    rows = lax.broadcasted_iota(jnp.int32, (LANES, LANES), 0)
    cols = lax.broadcasted_iota(jnp.int32, (LANES, LANES), 1)
    return rows == cols


def to_lanes(column, eye):
    return jnp.sum(jnp.where(eye, column, 0.0), axis=0, keepdims=True)


def to_column(lanes, eye):
    return jnp.sum(jnp.where(eye, lanes, 0.0), axis=1, keepdims=True)


def fold_rows(value, op):
    return op(value.reshape(value.shape[0] // 8, 8, value.shape[1]), axis=0)


def squares(rows_ref, at):
    rows = rows_ref[at : at + LANES, :].astype(jnp.float32)
    return jnp.sum(rows * rows, axis=1, keepdims=True) / EPSILON


def row_block(rows_ref, tgt_ref, offset_ref, z_ref, eye):
    rows = rows_ref[...] * LOGIT_SCALE
    src_count = rows.shape[0]
    tgt_count = tgt_ref.shape[0]
    peak = None
    for at in range(0, tgt_count, CHUNK):
        cols = slice(at, at + CHUNK)
        dots = lax.dot_general(rows, tgt_ref[cols, :], NT_DIMS, preferred_element_type=jnp.float32)
        z = dots + offset_ref[:, cols]
        z_ref[:, cols] = z
        for lane in range(0, CHUNK, LANES):
            part = z[:, lane : lane + LANES]
            peak = part if peak is None else jnp.maximum(peak, part)
    peak = jnp.max(peak, axis=1, keepdims=True)
    mass = None
    for at in range(0, tgt_count, LANES):
        term = jnp.exp(z_ref[:, at : at + LANES] - peak)
        mass = term if mass is None else mass + term
    mass = jnp.sum(mass, axis=1, keepdims=True)
    parts = [slice(at, at + LANES) for at in range(0, src_count, LANES)]
    return jnp.concatenate([to_lanes(peak[p], eye) + jnp.log(to_lanes(mass[p], eye)) for p in parts], axis=1)


def put_row(held, value, row):
    return jnp.where(lax.broadcasted_iota(jnp.int32, held.shape, 0) == row, value, held)


def prepare_kernel(
    core_ref, src_hbm, tgt_hbm, pot_hbm, mass_hbm, tgt_ref, offset_ref, z_ref, lse_ref, src_ref, pot_ref, mass_ref, sems
):
    copies = [
        pltpu.make_async_copy(source, target, sems.at[at])
        for at, (source, target) in enumerate(
            ((tgt_hbm, tgt_ref), (src_hbm, src_ref), (pot_hbm, pot_ref), (mass_hbm, mass_ref))
        )
    ]
    for copy in copies:
        copy.start()
    for copy in copies:
        copy.wait()
    eye = diagonal()
    for group in range(tgt_ref.shape[0] // LANES):
        at = group * LANES
        base = pot_ref[group : group + 1, :] + mass_ref[group : group + 1, :]
        offset_ref[:, at : at + LANES] = base - to_lanes(squares(tgt_ref, at), eye)
    lse = row_block(src_ref, tgt_ref, offset_ref, z_ref, eye)
    lse_ref[...] = put_row(jnp.zeros(lse_ref.shape, jnp.float32), lse, core_ref[0])


def block_kernel(slot, core_ref, rows_ref, tgt_ref, offset_ref, held_ref, z_ref, lse_ref):
    lse = row_block(rows_ref, tgt_ref, offset_ref, z_ref, diagonal())
    lse_ref[...] = put_row(held_ref[...], lse, slot ^ core_ref[0])


def squares_kernel(count, core_ref, *refs):
    eye = diagonal()
    blocks, out_ref = refs[:count], refs[count]
    out = jnp.zeros(out_ref.shape, jnp.float32)
    for slot, rows_ref in enumerate(blocks):
        row = [to_lanes(squares(rows_ref, at), eye) for at in range(0, rows_ref.shape[0], LANES)]
        out = put_row(out, jnp.concatenate(row, axis=1), slot ^ core_ref[0])
    out_ref[...] = out


def column_kernel(slots, core_ref, *refs):
    eye = diagonal()
    z_refs = refs[:slots]
    lse_ref, slope_ref, logmass_ref, sq_ref, pot_ref, mass_ref, expo_ref, potential_ref, out_ref, off_ref = refs[slots:]
    core = core_ref[0]
    src_count, tgt_count = z_refs[0].shape
    potential = slope_ref[...] * (logmass_ref[...] - (lse_ref[...] - sq_ref[...]))
    mine = lax.broadcasted_iota(jnp.int32, potential.shape, 0) == core
    potential_ref[...] = jnp.sum(jnp.where(mine, potential, 0.0), axis=0, keepdims=True)
    offset = potential + logmass_ref[...] - sq_ref[...]
    for slot in range(slots):
        row = jnp.where(core == 0, offset[slot : slot + 1, :], offset[slot ^ 1 : (slot ^ 1) + 1, :])
        for at in range(0, src_count, LANES):
            column = to_column(row[:, at : at + LANES], eye)
            off_ref[slot, at : at + LANES, :] = jnp.broadcast_to(column, (LANES, LANES))

    for at in range(0, tgt_count, LANES):
        cols = slice(at, at + LANES)
        peak = None
        for slot in range(slots):
            high = fold_rows(z_refs[slot][:, cols] + off_ref[slot], jnp.max)
            peak = high if peak is None else jnp.maximum(peak, high)
        peak = jnp.max(peak, axis=0, keepdims=True)
        mass = None
        for slot in range(slots):
            term = fold_rows(jnp.exp(z_refs[slot][:, cols] + off_ref[slot] - peak), jnp.sum)
            mass = term if mass is None else mass + term
        mass = jnp.sum(mass, axis=0, keepdims=True)
        row = slice(at // LANES, at // LANES + 1)
        out_ref[row, :] = expo_ref[row, :] * (2.0 * mass_ref[row, :] + pot_ref[row, :] - (peak + jnp.log(mass)))


def f32(*shape):
    return jax.ShapeDtypeStruct(shape, jnp.float32)


def params(mebibytes):
    return pltpu.CompilerParams(vmem_limit_bytes=mebibytes * 1024 * 1024)


def merge(*parts):
    peak = functools.reduce(jnp.maximum, parts)
    return peak + jnp.log(sum(jnp.exp(part - peak) for part in parts))


def shards(sources, targets, tgt_potential, src_logmass, tgt_logmass, src_exponent, tgt_exponent):
    src_count, width = sources.shape
    tgt_count = targets.shape[0]
    slabs = lax.axis_size("blk")
    sets = lax.axis_size("tsplit")
    chips = slabs // 2
    groups = tgt_count // LANES
    core = lax.axis_index("blk") & 1
    core_word = core.astype(jnp.int32).reshape(1)
    assert chips > 1 and sets > 1 and chips & (chips - 1) == 0 and sets & (sets - 1) == 0

    def blk(value, flip):
        return lax.ppermute(value, "blk", [(i, i ^ flip) for i in range(slabs)])

    def route(value, parity, flip, step):
        pairs = [
            (b * sets + z, (b ^ flip) * sets + (z ^ step)) for b in range(parity, slabs, 2) for z in range(sets)
        ]
        return lax.ppermute(value, ("blk", "tsplit"), pairs)

    def mirror(value, chip):
        parts = value.reshape(chips, 2, src_count)
        return jnp.concatenate([parts[k ^ chip] for k in range(chips)], axis=0)

    straight = [blk(sources, 2 * chip) for chip in range(1, chips)]
    paired = blk(sources, 1)
    blocks = [sources, paired]
    potential = tgt_potential.reshape(groups, LANES)
    logmass = tgt_logmass.reshape(groups, LANES)
    exponent = tgt_exponent.reshape(groups, LANES)
    block_pairs = src_count * tgt_count
    cost = pl.CostEstimate(flops=2 * block_pairs * width, bytes_accessed=2**20, transcendentals=block_pairs)

    held, offset, z, lse = pl.pallas_call(
        prepare_kernel,
        out_shape=(
            jax.ShapeDtypeStruct(targets.shape, targets.dtype),
            f32(1, tgt_count),
            f32(src_count, tgt_count),
            f32(slabs, src_count),
        ),
        in_specs=[SMEM] + [HBM] * 4,
        out_specs=(VMEM,) * 4,
        scratch_shapes=[
            pltpu.VMEM(sources.shape, sources.dtype),
            pltpu.VMEM((groups, LANES), jnp.float32),
            pltpu.VMEM((groups, LANES), jnp.float32),
            pltpu.SemaphoreType.DMA((4,)),
        ],
        compiler_params=params(12),
        cost_estimate=cost,
        name="prepare",
    )(core_word, *[pltpu.with_memory_space_constraint(x, pltpu.HBM) for x in (sources, targets, potential, logmass)])
    zs = [z]
    lse, src_slope, src_mass = lax.optimization_barrier((lse, src_exponent, src_logmass))
    line = jnp.stack([src_slope, src_mass])
    line = jnp.where(core == 0, jnp.stack([line, blk(line, 1)]), jnp.stack([blk(line, 1), line]))
    lines = jnp.concatenate([line] + [blk(line, 2 * chip) for chip in range(1, chips)])
    for slot in range(1, slabs):
        if slot == slabs - 1:
            lse, lines = lax.optimization_barrier((lse, lines))
        z, lse = pl.pallas_call(
            functools.partial(block_kernel, slot),
            out_shape=(f32(src_count, tgt_count), f32(slabs, src_count)),
            in_specs=[SMEM] + [VMEM] * 4,
            out_specs=(VMEM,) * 2,
            compiler_params=params(12),
            cost_estimate=cost,
            name=f"rows_{slot}",
        )(core_word, blocks[slot], held, offset, lse)
        zs.append(z)
        if slot == 1:
            lse, *straight = lax.optimization_barrier((lse, *straight))
            for block in straight:
                blocks += [block, blk(block, 1)]
    src_sq = pl.pallas_call(
        functools.partial(squares_kernel, slabs),
        out_shape=f32(slabs, src_count),
        in_specs=[SMEM] + [VMEM] * slabs,
        out_specs=VMEM,
        compiler_params=params(12),
        cost_estimate=pl.CostEstimate(flops=slabs * src_count * width, bytes_accessed=2**20, transcendentals=0),
        name="source_squares",
    )(core_word, *blocks)

    lse = merge(lse, route(lse, 0, 1, 0), mirror(route(lse, 1, 2, 0), 1), mirror(route(lse, 0, 3, 0), 1))
    chip = 2
    while chip < chips:
        lse = merge(lse, mirror(route(lse, 1, 2 * chip, 0), chip))
        chip *= 2
    step = 1
    while 2 * step < sets:
        lse = merge(lse, route(lse, 1, 0, step))
        step *= 2
    here, there, direct = route(lse, 1, 1, 0), route(lse, 1, 1, step), route(lse, 1, 0, step)
    lse = merge(jnp.where(core == 0, here, lse), jnp.where(core == 0, there, direct))

    src_potential, tgt_update = pl.pallas_call(
        functools.partial(column_kernel, slabs),
        out_shape=(f32(1, src_count), f32(groups, LANES)),
        in_specs=[SMEM] + [VMEM] * (slabs + 7),
        out_specs=(VMEM,) * 2,
        scratch_shapes=[pltpu.VMEM((slabs, src_count, LANES), jnp.float32)],
        compiler_params=params(8 + 2 * slabs),
        cost_estimate=pl.CostEstimate(
            flops=6 * slabs * block_pairs, bytes_accessed=2**20, transcendentals=slabs * block_pairs
        ),
        name="columns",
    )(core_word, *zs, lse, lines[:, 0], lines[:, 1], src_sq, potential, logmass, exponent)
    return (src_potential.reshape(src_count), tgt_update.reshape(tgt_count))


def solution(mesh):
    placed = (
        P(("groups", "blk"), None),
        P(("groups", "blk", "tsplit"), None),
        P(("groups", "blk", "tsplit")),
        P(("groups", "blk")),
        P(("groups", "blk", "tsplit")),
        P(("groups", "blk")),
        P(("groups", "blk", "tsplit")),
    )
    return jax.shard_map(
        shards,
        mesh=mesh,
        in_specs=placed,
        out_specs=(P(("groups", "blk")), P(("groups", "blk", "tsplit"))),
        check_vma=False,
    )
```

```python
import functools

import jax
import jax.numpy as jnp
from jax import lax
from jax.experimental import pallas as pl
from jax.experimental.pallas import tpu as pltpu
from jax.sharding import PartitionSpec as P

EPSILON = 0.5
LOGIT_SCALE = 2.0 / EPSILON
LANES = 128
CHUNK = 256
VMEM = pl.BlockSpec(memory_space=pltpu.VMEM)
HBM = pl.BlockSpec(memory_space=pltpu.HBM)
NT_DIMS = (((1,), (1,)), ((), ()))


def diagonal():
    rows = lax.broadcasted_iota(jnp.int32, (LANES, LANES), 0)
    cols = lax.broadcasted_iota(jnp.int32, (LANES, LANES), 1)
    return rows == cols


def to_lanes(column, eye):
    return jnp.sum(jnp.where(eye, column, 0.0), axis=0, keepdims=True)


def to_column(lanes, eye):
    return jnp.sum(jnp.where(eye, lanes, 0.0), axis=1, keepdims=True)


def fold_rows(value, op):
    return op(value.reshape(value.shape[0] // 8, 8, value.shape[1]), axis=0)


def merge(*parts):
    peak = functools.reduce(jnp.maximum, parts)
    return peak + jnp.log(sum(jnp.exp(part - peak) for part in parts))


def squares(rows_ref, at):
    rows = rows_ref[at : at + LANES, :].astype(jnp.float32)
    return jnp.sum(rows * rows, axis=1, keepdims=True) / EPSILON


def row_block(rows_ref, sides, eye):
    rows = rows_ref[...] * LOGIT_SCALE
    src_count = rows.shape[0]
    peak = None
    for tgt_ref, offset_ref, z_ref in sides:
        for at in range(0, tgt_ref.shape[0], CHUNK):
            cols = slice(at, at + CHUNK)
            dots = lax.dot_general(rows, tgt_ref[cols, :], NT_DIMS, preferred_element_type=jnp.float32)
            z = dots + offset_ref[:, cols]
            z_ref[:, cols] = z
            for lane in range(0, CHUNK, LANES):
                part = z[:, lane : lane + LANES]
                peak = part if peak is None else jnp.maximum(peak, part)
    peak = jnp.max(peak, axis=1, keepdims=True)
    mass = None
    for _, _, z_ref in sides:
        for at in range(0, z_ref.shape[1], LANES):
            term = jnp.exp(z_ref[:, at : at + LANES] - peak)
            mass = term if mass is None else mass + term
    mass = jnp.sum(mass, axis=1, keepdims=True)
    parts = [slice(at, at + LANES) for at in range(0, src_count, LANES)]
    return jnp.concatenate([to_lanes(peak[p], eye) + jnp.log(to_lanes(mass[p], eye)) for p in parts], axis=1)


def prepare_kernel(
    src_hbm, tgt_hbm, pot_hbm, mass_hbm, slope_hbm, logmass_hbm,
    tgt_ref, offset_ref, z_ref, lse_ref, line_ref, sq_ref,
    src_ref, pot_ref, mass_ref, slope_ref, logmass_ref, sems,
):
    pairs = (
        (tgt_hbm, tgt_ref), (src_hbm, src_ref), (pot_hbm, pot_ref),
        (mass_hbm, mass_ref), (slope_hbm, slope_ref), (logmass_hbm, logmass_ref),
    )
    copies = [pltpu.make_async_copy(source, target, sems.at[at]) for at, (source, target) in enumerate(pairs)]
    for copy in copies:
        copy.start()
    for copy in copies[1:]:
        copy.wait()
    eye = diagonal()
    for group in range(src_ref.shape[0] // LANES):
        cols = slice(group * LANES, (group + 1) * LANES)
        square = to_lanes(squares(src_ref, group * LANES), eye)
        slope = slope_ref[group : group + 1, :]
        logmass = logmass_ref[group : group + 1, :]
        sq_ref[:, cols] = logmass + square
        line_ref[0:1, cols] = slope
        line_ref[1:2, cols] = slope * (logmass + square) + (logmass - square)
    copies[0].wait()
    for group in range(tgt_ref.shape[0] // LANES):
        at = group * LANES
        base = pot_ref[group : group + 1, :] + mass_ref[group : group + 1, :]
        offset_ref[:, at : at + LANES] = base - to_lanes(squares(tgt_ref, at), eye)
    lse_ref[...] = row_block(src_ref, ((tgt_ref, offset_ref, z_ref),), eye)


def near_kernel(rows_ref, tgt_ref, offset_ref, held_ref, z_ref, lse_ref):
    lse_ref[...] = merge(held_ref[...], row_block(rows_ref, ((tgt_ref, offset_ref, z_ref),), diagonal()))


def far_kernel(count, *refs):
    eye = diagonal()
    blocks = refs[:count]
    own_ref, own_offset_ref, pair_ref, pair_offset_ref, own_z_ref, pair_z_ref, lse_ref = refs[count:]
    for slot in range(count):
        sides = ((own_ref, own_offset_ref, own_z_ref.at[slot]), (pair_ref, pair_offset_ref, pair_z_ref.at[slot]))
        lse_ref[slot] = row_block(blocks[slot], sides, eye)


def column_kernel(near_ref, far_ref, lse_ref, lines_ref, out_ref, off_ref):
    eye = diagonal()
    slots, src_count = lse_ref.shape
    for slot in range(slots):
        offset = lines_ref[slot, 1:2, :] - lines_ref[slot, 0:1, :] * lse_ref[slot : slot + 1, :]
        for at in range(0, src_count, LANES):
            column = to_column(offset[:, at : at + LANES], eye)
            off_ref[slot, at : at + LANES, :] = jnp.broadcast_to(column, (LANES, LANES))

    def shifted(slot, cols):
        z = near_ref[:, cols] if slot == 0 else far_ref[slot - 1, :, cols]
        return z + off_ref[slot]

    for group in range(out_ref.shape[0]):
        cols = slice(group * LANES, (group + 1) * LANES)
        peak = None
        for slot in range(slots):
            high = fold_rows(shifted(slot, cols), jnp.max)
            peak = high if peak is None else jnp.maximum(peak, high)
        peak = jnp.max(peak, axis=0, keepdims=True)
        mass = None
        for slot in range(slots):
            term = fold_rows(jnp.exp(shifted(slot, cols) - peak), jnp.sum)
            mass = term if mass is None else mass + term
        mass = jnp.sum(mass, axis=0, keepdims=True)
        out_ref[group : group + 1, :] = peak + jnp.log(mass)


def f32(*shape):
    return jax.ShapeDtypeStruct(shape, jnp.float32)


def params(mebibytes):
    return pltpu.CompilerParams(vmem_limit_bytes=mebibytes * 1024 * 1024)


def shards(sources, targets, tgt_potential, src_logmass, tgt_logmass, src_exponent, tgt_exponent):
    src_count, width = sources.shape
    tgt_count = targets.shape[0]
    slabs = lax.axis_size("blk")
    sets = lax.axis_size("tsplit")
    chips = slabs // 2
    far = chips - 1
    groups = tgt_count // LANES
    src_groups = src_count // LANES
    assert chips > 1 and chips & (chips - 1) == 0 and sets & (sets - 1) == 0

    def pair(value):
        return lax.ppermute(value, "blk", [(i, i ^ 1) for i in range(slabs)])

    def across(value, chip):
        return lax.ppermute(value, "blk", [(i, i ^ (2 * chip)) for i in range(slabs)])

    def along(value, step):
        return lax.ppermute(value, "tsplit", [(i, i ^ step) for i in range(sets)])

    def cost(blocks):
        pairs = blocks * src_count * tgt_count
        return pl.CostEstimate(flops=2 * pairs * width, bytes_accessed=2**20, transcendentals=pairs)

    far_blocks = [across(sources, chip) for chip in range(1, chips)]
    pair_targets = pair(targets)
    inputs = (
        sources,
        targets,
        tgt_potential.reshape(groups, LANES),
        tgt_logmass.reshape(groups, LANES),
        src_exponent.reshape(src_groups, LANES),
        src_logmass.reshape(src_groups, LANES),
    )
    held, offset, own_z, lse, line, src_shift = pl.pallas_call(
        prepare_kernel,
        out_shape=(
            jax.ShapeDtypeStruct(targets.shape, targets.dtype),
            f32(1, tgt_count),
            f32(src_count, tgt_count),
            f32(1, src_count),
            f32(2, src_count),
            f32(1, src_count),
        ),
        in_specs=[HBM] * 6,
        out_specs=(VMEM,) * 6,
        scratch_shapes=[pltpu.VMEM(x.shape, x.dtype) for x in (inputs[0],) + inputs[2:]]
        + [pltpu.SemaphoreType.DMA((6,))],
        compiler_params=params(12),
        cost_estimate=cost(1),
        name="prepare",
    )(*[pltpu.with_memory_space_constraint(x, pltpu.HBM) for x in inputs])
    pair_offset = pair(offset)
    lines = jnp.stack([line] + [across(line, chip) for chip in range(1, chips)])
    pair_z, lse = pl.pallas_call(
        near_kernel,
        out_shape=(f32(src_count, tgt_count), f32(1, src_count)),
        in_specs=[VMEM] * 4,
        out_specs=(VMEM,) * 2,
        compiler_params=params(12),
        cost_estimate=cost(1),
        name="near_rows",
    )(sources, pair_targets, pair_offset, lse)
    lse, lines, *far_blocks = lax.optimization_barrier((lse, lines, *far_blocks))
    own_far_z, pair_far_z, far_lse = pl.pallas_call(
        functools.partial(far_kernel, far),
        out_shape=(f32(far, src_count, tgt_count), f32(far, src_count, tgt_count), f32(far, 1, src_count)),
        in_specs=[VMEM] * (far + 4),
        out_specs=(VMEM,) * 3,
        compiler_params=params(8 + 3 * far),
        cost_estimate=cost(2 * far),
        name="far_rows",
    )(*far_blocks, held, offset, pair_targets, pair_offset)

    lse = jnp.concatenate([lse, far_lse.reshape(far, src_count)])
    chip = 1
    while chip < chips:
        other = across(lse, chip)
        lse = merge(lse, jnp.stack([other[slot ^ chip] for slot in range(chips)]))
        chip *= 2
    lse = merge(lse, *[along(lse, step) for step in range(1, sets)])

    def columns(near_z, far_z, lse):
        return pl.pallas_call(
            column_kernel,
            out_shape=f32(groups, LANES),
            in_specs=[VMEM] * 4,
            out_specs=VMEM,
            scratch_shapes=[pltpu.VMEM((chips, src_count, LANES), jnp.float32)],
            compiler_params=params(8 + 2 * chips),
            cost_estimate=pl.CostEstimate(
                flops=6 * chips * src_count * tgt_count,
                bytes_accessed=2**20,
                transcendentals=chips * src_count * tgt_count,
            ),
            name="columns",
        )(near_z, far_z, lse, lines)

    pair_part = columns(pair_z, pair_far_z, lse)
    lse, pair_part = lax.optimization_barrier((lse, pair_part))
    home = pair(pair_part)
    total = merge(columns(own_z, own_far_z, lse), home).reshape(tgt_count)
    tgt_update = tgt_exponent * (2.0 * tgt_logmass + tgt_potential - total)
    src_potential = src_exponent * (src_shift - lse[0:1]).reshape(src_count)
    return (src_potential, tgt_update)


def solution(mesh):
    placed = (
        P(("groups", "blk"), None),
        P(("groups", "blk", "tsplit"), None),
        P(("groups", "blk", "tsplit")),
        P(("groups", "blk")),
        P(("groups", "blk", "tsplit")),
        P(("groups", "blk")),
        P(("groups", "blk", "tsplit")),
    )
    return jax.shard_map(
        shards,
        mesh=mesh,
        in_specs=placed,
        out_specs=(P(("groups", "blk")), P(("groups", "blk", "tsplit"))),
        check_vma=False,
    )
```

```python
import functools

import jax
import jax.numpy as jnp
from jax import lax
from jax.experimental import pallas as pl
from jax.experimental.pallas import tpu as pltpu
from jax.sharding import PartitionSpec as P

EPSILON = 0.5
LOGIT_SCALE = 2.0 / EPSILON
LANES = 128
CHUNK = 256
VMEM = pl.BlockSpec(memory_space=pltpu.VMEM)
SMEM = pl.BlockSpec(memory_space=pltpu.SMEM)
HBM = pl.BlockSpec(memory_space=pltpu.HBM)
NT_DIMS = (((1,), (1,)), ((), ()))


def diagonal():
    rows = lax.broadcasted_iota(jnp.int32, (LANES, LANES), 0)
    cols = lax.broadcasted_iota(jnp.int32, (LANES, LANES), 1)
    return rows == cols


def to_lanes(column, eye):
    return jnp.sum(jnp.where(eye, column, 0.0), axis=0, keepdims=True)


def to_column(lanes, eye):
    return jnp.sum(jnp.where(eye, lanes, 0.0), axis=1, keepdims=True)


def fold_rows(value, op):
    return op(value.reshape(value.shape[0] // 8, 8, value.shape[1]), axis=0)


def merge(*parts):
    peak = functools.reduce(jnp.maximum, parts)
    return peak + jnp.log(sum(jnp.exp(part - peak) for part in parts))


def squares(rows_ref, at):
    rows = rows_ref[at : at + LANES, :].astype(jnp.float32)
    return jnp.sum(rows * rows, axis=1, keepdims=True) / EPSILON


def row_block(rows, sides, eye):
    rows = rows * LOGIT_SCALE
    src_count = rows.shape[0]
    peak = None
    for tgt_ref, offset_ref, z_ref in sides:
        for at in range(0, tgt_ref.shape[0], CHUNK):
            cols = slice(at, at + CHUNK)
            dots = lax.dot_general(rows, tgt_ref[cols, :], NT_DIMS, preferred_element_type=jnp.float32)
            z = dots + offset_ref[:, cols]
            z_ref[:, cols] = z
            for lane in range(0, CHUNK, LANES):
                part = z[:, lane : lane + LANES]
                peak = part if peak is None else jnp.maximum(peak, part)
    peak = jnp.max(peak, axis=1, keepdims=True)
    mass = None
    for _, _, z_ref in sides:
        for at in range(0, z_ref.shape[1], LANES):
            term = jnp.exp(z_ref[:, at : at + LANES] - peak)
            mass = term if mass is None else mass + term
    mass = jnp.sum(mass, axis=1, keepdims=True)
    parts = [slice(at, at + LANES) for at in range(0, src_count, LANES)]
    return jnp.concatenate([to_lanes(peak[p], eye) + jnp.log(to_lanes(mass[p], eye)) for p in parts], axis=1)


def prepare_kernel(
    src_hbm, tgt_hbm, pot_hbm, mass_hbm, slope_hbm, logmass_hbm,
    tgt_ref, offset_ref, z_ref, lse_ref, line_ref, sum_ref,
    src_ref, pot_ref, mass_ref, slope_ref, logmass_ref, sems,
):
    pairs = (
        (tgt_hbm, tgt_ref), (src_hbm, src_ref), (pot_hbm, pot_ref),
        (mass_hbm, mass_ref), (slope_hbm, slope_ref), (logmass_hbm, logmass_ref),
    )
    copies = [pltpu.make_async_copy(source, target, sems.at[at]) for at, (source, target) in enumerate(pairs)]
    for copy in copies:
        copy.start()
    for copy in copies[1:]:
        copy.wait()
    eye = diagonal()
    for group in range(src_ref.shape[0] // LANES):
        cols = slice(group * LANES, (group + 1) * LANES)
        square = to_lanes(squares(src_ref, group * LANES), eye)
        slope = slope_ref[group : group + 1, :]
        logmass = logmass_ref[group : group + 1, :]
        sum_ref[:, cols] = logmass + square
        line_ref[0:1, cols] = slope
        line_ref[1:2, cols] = slope * (logmass + square) + (logmass - square)
    copies[0].wait()
    for group in range(tgt_ref.shape[0] // LANES):
        at = group * LANES
        base = pot_ref[group : group + 1, :] + mass_ref[group : group + 1, :]
        offset_ref[:, at : at + LANES] = base - to_lanes(squares(tgt_ref, at), eye)
    lse_ref[...] = row_block(src_ref[...], ((tgt_ref, offset_ref, z_ref),), eye)


def near_kernel(rows_ref, tgt_ref, offset_ref, held_ref, z_ref, lse_ref):
    lse_ref[...] = merge(held_ref[...], row_block(rows_ref[...], ((tgt_ref, offset_ref, z_ref),), diagonal()))


def far_kernel(count, core_ref, *refs):
    eye = diagonal()
    early, late = refs[:count], refs[count : 2 * count]
    own_ref, own_offset_ref, pair_ref, pair_offset_ref, held_ref, line_ref = refs[2 * count : 2 * count + 6]
    own_z_ref, pair_z_ref, out_ref = refs[2 * count + 6 :]
    slots = count + 1
    out_ref[0:1, :] = held_ref[...]
    out_ref[slots : slots + 2, :] = line_ref[...]
    for slot in range(count):
        rows = jnp.where(core_ref[0] == 0, early[slot][...], late[slot][...])
        sides = ((own_ref, own_offset_ref, own_z_ref.at[slot]), (pair_ref, pair_offset_ref, pair_z_ref.at[slot]))
        out_ref[slot + 1 : slot + 2, :] = row_block(rows, sides, eye)


def sum_columns(near_ref, far_ref, offset, off_ref, out_ref):
    eye = diagonal()
    slots, src_count = offset.shape
    for slot in range(slots):
        for at in range(0, src_count, LANES):
            column = to_column(offset[slot : slot + 1, at : at + LANES], eye)
            off_ref[slot, at : at + LANES, :] = jnp.broadcast_to(column, (LANES, LANES))

    def shifted(slot, cols):
        z = near_ref[:, cols] if slot == 0 else far_ref[slot - 1, :, cols]
        return z + off_ref[slot]

    for group in range(out_ref.shape[0]):
        cols = slice(group * LANES, (group + 1) * LANES)
        peak = None
        for slot in range(slots):
            high = fold_rows(shifted(slot, cols), jnp.max)
            peak = high if peak is None else jnp.maximum(peak, high)
        peak = jnp.max(peak, axis=0, keepdims=True)
        mass = None
        for slot in range(slots):
            term = fold_rows(jnp.exp(shifted(slot, cols) - peak), jnp.sum)
            mass = term if mass is None else mass + term
        mass = jnp.sum(mass, axis=0, keepdims=True)
        out_ref[group : group + 1, :] = peak + jnp.log(mass)


def pair_kernel(near_ref, far_ref, lse_ref, slope_ref, shift_ref, out_ref, off_ref):
    sum_columns(near_ref, far_ref, shift_ref[...] - slope_ref[...] * lse_ref[...], off_ref, out_ref)


def own_kernel(near_ref, far_ref, lse_ref, slope_ref, shift_ref, sum_ref, out_ref, potential_ref, off_ref):
    lse, slope = lse_ref[...], slope_ref[...]
    potential_ref[...] = slope[0:1, :] * (sum_ref[...] - lse[0:1, :])
    sum_columns(near_ref, far_ref, shift_ref[...] - slope * lse, off_ref, out_ref)


def f32(*shape):
    return jax.ShapeDtypeStruct(shape, jnp.float32)


def params(mebibytes):
    return pltpu.CompilerParams(vmem_limit_bytes=mebibytes * 1024 * 1024)


def shards(sources, targets, tgt_potential, src_logmass, tgt_logmass, src_exponent, tgt_exponent):
    src_count, width = sources.shape
    tgt_count = targets.shape[0]
    slabs = lax.axis_size("blk")
    sets = lax.axis_size("tsplit")
    chips = slabs // 2
    far = chips - 1
    groups = tgt_count // LANES
    src_groups = src_count // LANES
    assert chips > 1 and chips & (chips - 1) == 0 and sets & (sets - 1) == 0

    def pair(value):
        return lax.ppermute(value, "blk", [(i, i ^ 1) for i in range(slabs)])

    def across(value, chip):
        return lax.ppermute(value, "blk", [(i, i ^ (2 * chip)) for i in range(slabs)])

    def along(value, step):
        return lax.ppermute(value, "tsplit", [(i, i ^ step) for i in range(sets)])

    def cost(blocks):
        pairs = blocks * src_count * tgt_count
        return pl.CostEstimate(flops=2 * pairs * width, bytes_accessed=2**20, transcendentals=pairs)

    core = lax.axis_index("blk") & 1
    core_word = core.astype(jnp.int32).reshape(1)

    def across_one(value, chip, parity):
        return lax.ppermute(value, "blk", [(i, i ^ (2 * chip) if i & 1 == parity else i) for i in range(slabs)])

    early = [across_one(sources, chip, 0) for chip in range(1, chips)]
    pair_targets = pair(targets)
    inputs = (
        sources,
        targets,
        tgt_potential.reshape(groups, LANES),
        tgt_logmass.reshape(groups, LANES),
        src_exponent.reshape(src_groups, LANES),
        src_logmass.reshape(src_groups, LANES),
    )
    held, offset, own_z, lse, line, src_sum = pl.pallas_call(
        prepare_kernel,
        out_shape=(
            jax.ShapeDtypeStruct(targets.shape, targets.dtype),
            f32(1, tgt_count),
            f32(src_count, tgt_count),
            f32(1, src_count),
            f32(2, src_count),
            f32(1, src_count),
        ),
        in_specs=[HBM] * 6,
        out_specs=(VMEM,) * 6,
        scratch_shapes=[pltpu.VMEM(x.shape, x.dtype) for x in (inputs[0],) + inputs[2:]]
        + [pltpu.SemaphoreType.DMA((6,))],
        compiler_params=params(12),
        cost_estimate=cost(1),
        name="prepare",
    )(*[pltpu.with_memory_space_constraint(x, pltpu.HBM) for x in inputs])
    lse, late_sources = lax.optimization_barrier((lse, sources))
    late = [across_one(late_sources, chip, 1) for chip in range(1, chips)]
    pair_offset = pair(offset)
    lse, *early = lax.optimization_barrier((lse, *early))
    pair_z, lse = pl.pallas_call(
        near_kernel,
        out_shape=(f32(src_count, tgt_count), f32(1, src_count)),
        in_specs=[VMEM] * 4,
        out_specs=(VMEM,) * 2,
        compiler_params=params(12),
        cost_estimate=cost(1),
        name="near_rows",
    )(sources, pair_targets, pair_offset, lse)
    far_lines = [across(line, chip) for chip in range(2, chips)]
    lse, *moved = lax.optimization_barrier((lse, *early, *late, *far_lines))
    own_far_z, pair_far_z, payload = pl.pallas_call(
        functools.partial(far_kernel, far),
        out_shape=(f32(far, src_count, tgt_count), f32(far, src_count, tgt_count), f32(chips + 2, src_count)),
        in_specs=[SMEM] + [VMEM] * (2 * far + 6),
        out_specs=(VMEM,) * 3,
        compiler_params=params(8 + 3 * far),
        cost_estimate=cost(2 * far),
        name="far_rows",
    )(core_word, *moved[: 2 * far], held, offset, pair_targets, pair_offset, lse, line)

    other = across(payload, 1)
    lines = jnp.stack([line, other[chips:]] + moved[2 * far :], axis=1)
    lse = merge(payload[:chips], jnp.stack([other[slot ^ 1] for slot in range(chips)]))
    chip = 2
    while chip < chips:
        other = across(lse, chip)
        lse = merge(lse, jnp.stack([other[slot ^ chip] for slot in range(chips)]))
        chip *= 2
    step = 1
    while step < sets:
        lse = merge(lse, along(lse, step))
        step *= 2

    def columns(kernel, near_z, far_z, *more):
        outs = (f32(groups, LANES), f32(1, src_count))[: 1 + len(more)]
        return pl.pallas_call(
            kernel,
            out_shape=outs,
            in_specs=[VMEM] * (5 + len(more)),
            out_specs=(VMEM,) * len(outs),
            scratch_shapes=[pltpu.VMEM((chips, src_count, LANES), jnp.float32)],
            compiler_params=params(8 + 2 * chips),
            cost_estimate=pl.CostEstimate(
                flops=6 * chips * src_count * tgt_count,
                bytes_accessed=2**20,
                transcendentals=chips * src_count * tgt_count,
            ),
            name="columns",
        )(near_z, far_z, lse, lines[0], lines[1], *more)

    (pair_part,) = columns(pair_kernel, pair_z, pair_far_z)
    lse, pair_part = lax.optimization_barrier((lse, pair_part))
    home = pair(pair_part)
    own_part, src_potential = columns(own_kernel, own_z, own_far_z, src_sum)
    total = merge(own_part, home).reshape(tgt_count)
    tgt_update = tgt_exponent * (2.0 * tgt_logmass + tgt_potential - total)
    return (src_potential.reshape(src_count), tgt_update)


def solution(mesh):
    placed = (
        P(("groups", "blk"), None),
        P(("groups", "blk", "tsplit"), None),
        P(("groups", "blk", "tsplit")),
        P(("groups", "blk")),
        P(("groups", "blk", "tsplit")),
        P(("groups", "blk")),
        P(("groups", "blk", "tsplit")),
    )
    return jax.shard_map(
        shards,
        mesh=mesh,
        in_specs=placed,
        out_specs=(P(("groups", "blk")), P(("groups", "blk", "tsplit"))),
        check_vma=False,
    )
```

```python
import functools

import jax
import jax.numpy as jnp
from jax import lax
from jax.experimental import pallas as pl
from jax.experimental.pallas import tpu as pltpu
from jax.sharding import PartitionSpec as P

EPSILON = 0.5
LOGIT_SCALE = 2.0 / EPSILON
LANES = 128
CHUNK = 256
VMEM = pl.BlockSpec(memory_space=pltpu.VMEM)
HBM = pl.BlockSpec(memory_space=pltpu.HBM)
NT_DIMS = (((1,), (1,)), ((), ()))


def diagonal():
    rows = lax.broadcasted_iota(jnp.int32, (LANES, LANES), 0)
    cols = lax.broadcasted_iota(jnp.int32, (LANES, LANES), 1)
    return rows == cols


def to_lanes(column, eye):
    return jnp.sum(jnp.where(eye, column, 0.0), axis=0, keepdims=True)


def to_column(lanes, eye):
    return jnp.sum(jnp.where(eye, lanes, 0.0), axis=1, keepdims=True)


def fold_rows(value, op):
    return op(value.reshape(value.shape[0] // 8, 8, value.shape[1]), axis=0)


def merge(*parts):
    peak = functools.reduce(jnp.maximum, parts)
    return peak + jnp.log(sum(jnp.exp(part - peak) for part in parts))


def squares(rows_ref, at):
    rows = rows_ref[at : at + LANES, :].astype(jnp.float32)
    return jnp.sum(rows * rows, axis=1, keepdims=True) / EPSILON


def row_block(rows, sides, eye):
    rows = rows * LOGIT_SCALE
    src_count = rows.shape[0]
    peak = None
    for tgt_ref, offset_ref, z_ref in sides:
        for at in range(0, tgt_ref.shape[0], CHUNK):
            cols = slice(at, at + CHUNK)
            dots = lax.dot_general(rows, tgt_ref[cols, :], NT_DIMS, preferred_element_type=jnp.float32)
            z = dots + offset_ref[:, cols]
            z_ref[:, cols] = z
            for lane in range(0, CHUNK, LANES):
                part = z[:, lane : lane + LANES]
                peak = part if peak is None else jnp.maximum(peak, part)
    peak = jnp.max(peak, axis=1, keepdims=True)
    mass = None
    for _, _, z_ref in sides:
        for at in range(0, z_ref.shape[1], LANES):
            term = jnp.exp(z_ref[:, at : at + LANES] - peak)
            mass = term if mass is None else mass + term
    mass = jnp.sum(mass, axis=1, keepdims=True)
    parts = [slice(at, at + LANES) for at in range(0, src_count, LANES)]
    return jnp.concatenate([to_lanes(peak[p], eye) + jnp.log(to_lanes(mass[p], eye)) for p in parts], axis=1)


def prepare_kernel(
    src_hbm, tgt_hbm, pot_hbm, mass_hbm, slope_hbm, logmass_hbm,
    tgt_ref, offset_ref, z_ref, lse_ref, line_ref, sum_ref,
    src_ref, pot_ref, mass_ref, slope_ref, logmass_ref, sems,
):
    pairs = (
        (tgt_hbm, tgt_ref), (src_hbm, src_ref), (pot_hbm, pot_ref),
        (mass_hbm, mass_ref), (slope_hbm, slope_ref), (logmass_hbm, logmass_ref),
    )
    copies = [pltpu.make_async_copy(source, target, sems.at[at]) for at, (source, target) in enumerate(pairs)]
    for copy in copies:
        copy.start()
    for copy in copies[1:]:
        copy.wait()
    eye = diagonal()
    for group in range(src_ref.shape[0] // LANES):
        cols = slice(group * LANES, (group + 1) * LANES)
        square = to_lanes(squares(src_ref, group * LANES), eye)
        slope = slope_ref[group : group + 1, :]
        logmass = logmass_ref[group : group + 1, :]
        sum_ref[:, cols] = logmass + square
        line_ref[0:1, cols] = slope
        line_ref[1:2, cols] = slope * (logmass + square) + (logmass - square)
    copies[0].wait()
    for group in range(tgt_ref.shape[0] // LANES):
        at = group * LANES
        base = pot_ref[group : group + 1, :] + mass_ref[group : group + 1, :]
        offset_ref[:, at : at + LANES] = base - to_lanes(squares(tgt_ref, at), eye)
    lse_ref[...] = row_block(src_ref[...], ((tgt_ref, offset_ref, z_ref),), eye)


def near_kernel(rows_ref, tgt_ref, offset_ref, held_ref, z_ref, lse_ref):
    lse_ref[...] = merge(held_ref[...], row_block(rows_ref[...], ((tgt_ref, offset_ref, z_ref),), diagonal()))


def far_kernel(count, *refs):
    eye = diagonal()
    own_ref, own_offset_ref, pair_ref, pair_offset_ref, held_ref, line_ref = refs[count : count + 6]
    own_z_ref, pair_z_ref, out_ref = refs[count + 6 :]
    slots = count + 1
    out_ref[0:1, :] = held_ref[...]
    out_ref[slots : slots + 2, :] = line_ref[...]
    for slot in range(count):
        sides = ((own_ref, own_offset_ref, own_z_ref.at[slot]), (pair_ref, pair_offset_ref, pair_z_ref.at[slot]))
        out_ref[slot + 1 : slot + 2, :] = row_block(refs[slot][...], sides, eye)


def sum_columns(near_ref, far_ref, offset, off_ref, out_ref):
    eye = diagonal()
    slots, src_count = offset.shape
    for slot in range(slots):
        for at in range(0, src_count, LANES):
            column = to_column(offset[slot : slot + 1, at : at + LANES], eye)
            off_ref[slot, at : at + LANES, :] = jnp.broadcast_to(column, (LANES, LANES))

    def shifted(slot, cols):
        z = near_ref[:, cols] if slot == 0 else far_ref[slot - 1, :, cols]
        return z + off_ref[slot]

    for group in range(out_ref.shape[0]):
        cols = slice(group * LANES, (group + 1) * LANES)
        peak = None
        for slot in range(slots):
            high = fold_rows(shifted(slot, cols), jnp.max)
            peak = high if peak is None else jnp.maximum(peak, high)
        peak = jnp.max(peak, axis=0, keepdims=True)
        mass = None
        for slot in range(slots):
            term = fold_rows(jnp.exp(shifted(slot, cols) - peak), jnp.sum)
            mass = term if mass is None else mass + term
        mass = jnp.sum(mass, axis=0, keepdims=True)
        out_ref[group : group + 1, :] = peak + jnp.log(mass)


def pair_kernel(near_ref, far_ref, lse_ref, slope_ref, shift_ref, out_ref, off_ref):
    sum_columns(near_ref, far_ref, shift_ref[...] - slope_ref[...] * lse_ref[...], off_ref, out_ref)


def own_kernel(near_ref, far_ref, lse_ref, slope_ref, shift_ref, sum_ref, out_ref, potential_ref, off_ref):
    lse, slope = lse_ref[...], slope_ref[...]
    potential_ref[...] = slope[0:1, :] * (sum_ref[...] - lse[0:1, :])
    sum_columns(near_ref, far_ref, shift_ref[...] - slope * lse, off_ref, out_ref)


def f32(*shape):
    return jax.ShapeDtypeStruct(shape, jnp.float32)


def params(mebibytes):
    return pltpu.CompilerParams(vmem_limit_bytes=mebibytes * 1024 * 1024)


def shards(sources, targets, tgt_potential, src_logmass, tgt_logmass, src_exponent, tgt_exponent):
    src_count, width = sources.shape
    tgt_count = targets.shape[0]
    slabs = lax.axis_size("blk")
    sets = lax.axis_size("tsplit")
    chips = slabs // 2
    far = chips - 1
    groups = tgt_count // LANES
    src_groups = src_count // LANES
    assert chips > 1 and chips & (chips - 1) == 0 and sets & (sets - 1) == 0

    def pair(value):
        return lax.ppermute(value, "blk", [(i, i ^ 1) for i in range(slabs)])

    def across(value, chip):
        return lax.ppermute(value, "blk", [(i, i ^ (2 * chip)) for i in range(slabs)])

    def along(value, step):
        return lax.ppermute(value, "tsplit", [(i, i ^ step) for i in range(sets)])

    def cost(blocks):
        pairs = blocks * src_count * tgt_count
        return pl.CostEstimate(flops=2 * pairs * width, bytes_accessed=2**20, transcendentals=pairs)

    far_blocks = [across(sources, chip) for chip in range(1, chips)]
    pair_targets = pair(targets)
    inputs = (
        sources,
        targets,
        tgt_potential.reshape(groups, LANES),
        tgt_logmass.reshape(groups, LANES),
        src_exponent.reshape(src_groups, LANES),
        src_logmass.reshape(src_groups, LANES),
    )
    held, offset, own_z, lse, line, src_sum = pl.pallas_call(
        prepare_kernel,
        out_shape=(
            jax.ShapeDtypeStruct(targets.shape, targets.dtype),
            f32(1, tgt_count),
            f32(src_count, tgt_count),
            f32(1, src_count),
            f32(2, src_count),
            f32(1, src_count),
        ),
        in_specs=[HBM] * 6,
        out_specs=(VMEM,) * 6,
        scratch_shapes=[pltpu.VMEM(x.shape, x.dtype) for x in (inputs[0],) + inputs[2:]]
        + [pltpu.SemaphoreType.DMA((6,))],
        compiler_params=params(12),
        cost_estimate=cost(1),
        name="prepare",
    )(*[pltpu.with_memory_space_constraint(x, pltpu.HBM) for x in inputs])
    pair_offset = pair(offset)
    pair_z, lse = pl.pallas_call(
        near_kernel,
        out_shape=(f32(src_count, tgt_count), f32(1, src_count)),
        in_specs=[VMEM] * 4,
        out_specs=(VMEM,) * 2,
        compiler_params=params(12),
        cost_estimate=cost(1),
        name="near_rows",
    )(sources, pair_targets, pair_offset, lse)
    far_lines = [across(line, chip) for chip in range(2, chips)]
    lse, *moved = lax.optimization_barrier((lse, *far_blocks, *far_lines))
    own_far_z, pair_far_z, payload = pl.pallas_call(
        functools.partial(far_kernel, far),
        out_shape=(f32(far, src_count, tgt_count), f32(far, src_count, tgt_count), f32(chips + 2, src_count)),
        in_specs=[VMEM] * (far + 6),
        out_specs=(VMEM,) * 3,
        compiler_params=params(8 + 3 * far),
        cost_estimate=cost(2 * far),
        name="far_rows",
    )(*moved[:far], held, offset, pair_targets, pair_offset, lse, line)

    other = across(payload, 1)
    lines = jnp.stack([line, other[chips:]] + moved[far:], axis=1)
    lse = merge(payload[:chips], jnp.stack([other[slot ^ 1] for slot in range(chips)]))
    chip = 2
    while chip < chips:
        other = across(lse, chip)
        lse = merge(lse, jnp.stack([other[slot ^ chip] for slot in range(chips)]))
        chip *= 2
    step = 1
    while step < sets:
        lse = merge(lse, along(lse, step))
        step *= 2

    def columns(kernel, near_z, far_z, *more):
        outs = (f32(groups, LANES), f32(1, src_count))[: 1 + len(more)]
        return pl.pallas_call(
            kernel,
            out_shape=outs,
            in_specs=[VMEM] * (5 + len(more)),
            out_specs=(VMEM,) * len(outs),
            scratch_shapes=[pltpu.VMEM((chips, src_count, LANES), jnp.float32)],
            compiler_params=params(8 + 2 * chips),
            cost_estimate=pl.CostEstimate(
                flops=6 * chips * src_count * tgt_count,
                bytes_accessed=2**20,
                transcendentals=chips * src_count * tgt_count,
            ),
            name="columns",
        )(near_z, far_z, lse, lines[0], lines[1], *more)

    (pair_part,) = columns(pair_kernel, pair_z, pair_far_z)
    lse, pair_part = lax.optimization_barrier((lse, pair_part))
    home = pair(pair_part)
    own_part, src_potential = columns(own_kernel, own_z, own_far_z, src_sum)
    total = merge(own_part, home).reshape(tgt_count)
    tgt_update = tgt_exponent * (2.0 * tgt_logmass + tgt_potential - total)
    return (src_potential.reshape(src_count), tgt_update)


def solution(mesh):
    placed = (
        P(("groups", "blk"), None),
        P(("groups", "blk", "tsplit"), None),
        P(("groups", "blk", "tsplit")),
        P(("groups", "blk")),
        P(("groups", "blk", "tsplit")),
        P(("groups", "blk")),
        P(("groups", "blk", "tsplit")),
    )
    return jax.shard_map(
        shards,
        mesh=mesh,
        in_specs=placed,
        out_specs=(P(("groups", "blk")), P(("groups", "blk", "tsplit"))),
        check_vma=False,
    )
```

```python
import functools

import jax
import jax.numpy as jnp
from jax import lax
from jax.experimental import pallas as pl
from jax.experimental.pallas import tpu as pltpu
from jax.sharding import PartitionSpec as P

EPSILON = 0.5
LOGIT_SCALE = 2.0 / EPSILON
LANES = 128
CHUNK = 256
VMEM = pl.BlockSpec(memory_space=pltpu.VMEM)
SMEM = pl.BlockSpec(memory_space=pltpu.SMEM)
HBM = pl.BlockSpec(memory_space=pltpu.HBM)
NT_DIMS = (((1,), (1,)), ((), ()))


def diagonal():
    rows = lax.broadcasted_iota(jnp.int32, (LANES, LANES), 0)
    cols = lax.broadcasted_iota(jnp.int32, (LANES, LANES), 1)
    return rows == cols


def to_lanes(column, eye):
    return jnp.sum(jnp.where(eye, column, 0.0), axis=0, keepdims=True)


def to_column(lanes, eye):
    return jnp.sum(jnp.where(eye, lanes, 0.0), axis=1, keepdims=True)


def fold_rows(value, op):
    return op(value.reshape(value.shape[0] // 8, 8, value.shape[1]), axis=0)


def merge(*parts):
    peak = functools.reduce(jnp.maximum, parts)
    return peak + jnp.log(sum(jnp.exp(part - peak) for part in parts))


def squares(rows_ref, at):
    rows = rows_ref[at : at + LANES, :].astype(jnp.float32)
    return jnp.sum(rows * rows, axis=1, keepdims=True) / EPSILON


def row_block(rows, sides, eye):
    rows = rows * LOGIT_SCALE
    src_count = rows.shape[0]
    peak = None
    for tgt_ref, offset_ref, z_ref in sides:
        for at in range(0, tgt_ref.shape[0], CHUNK):
            cols = slice(at, at + CHUNK)
            dots = lax.dot_general(rows, tgt_ref[cols, :], NT_DIMS, preferred_element_type=jnp.float32)
            z = dots + offset_ref[:, cols]
            z_ref[:, cols] = z
            for lane in range(0, CHUNK, LANES):
                part = z[:, lane : lane + LANES]
                peak = part if peak is None else jnp.maximum(peak, part)
    peak = jnp.max(peak, axis=1, keepdims=True)
    mass = None
    for _, _, z_ref in sides:
        for at in range(0, z_ref.shape[1], LANES):
            term = jnp.exp(z_ref[:, at : at + LANES] - peak)
            mass = term if mass is None else mass + term
    mass = jnp.sum(mass, axis=1, keepdims=True)
    parts = [slice(at, at + LANES) for at in range(0, src_count, LANES)]
    return jnp.concatenate([to_lanes(peak[p], eye) + jnp.log(to_lanes(mass[p], eye)) for p in parts], axis=1)


def prepare_kernel(turn, core_ref, *refs):
    inputs, refs = refs[:6], refs[6:]
    earlier, refs = refs[: 6 * (1 - turn)], refs[6 * (1 - turn) :]
    outs, scratch = refs[:6], refs[6:]

    @pl.when(core_ref[0] == turn)
    def work():
        prepare(*inputs, *outs, *scratch)

    if earlier:

        @pl.when(core_ref[0] != turn)
        def hand_on():
            for source, target in zip(earlier, outs):
                target[...] = source[...]


def prepare(
    src_hbm, tgt_hbm, pot_hbm, mass_hbm, slope_hbm, logmass_hbm,
    tgt_ref, offset_ref, z_ref, lse_ref, line_ref, sum_ref,
    src_ref, pot_ref, mass_ref, slope_ref, logmass_ref, sems,
):
    pairs = (
        (tgt_hbm, tgt_ref), (src_hbm, src_ref), (pot_hbm, pot_ref),
        (mass_hbm, mass_ref), (slope_hbm, slope_ref), (logmass_hbm, logmass_ref),
    )
    copies = [pltpu.make_async_copy(source, target, sems.at[at]) for at, (source, target) in enumerate(pairs)]
    for copy in copies:
        copy.start()
    for copy in copies[1:]:
        copy.wait()
    eye = diagonal()
    for group in range(src_ref.shape[0] // LANES):
        cols = slice(group * LANES, (group + 1) * LANES)
        square = to_lanes(squares(src_ref, group * LANES), eye)
        slope = slope_ref[group : group + 1, :]
        logmass = logmass_ref[group : group + 1, :]
        sum_ref[:, cols] = logmass + square
        line_ref[0:1, cols] = slope
        line_ref[1:2, cols] = slope * (logmass + square) + (logmass - square)
    copies[0].wait()
    for group in range(tgt_ref.shape[0] // LANES):
        at = group * LANES
        base = pot_ref[group : group + 1, :] + mass_ref[group : group + 1, :]
        offset_ref[:, at : at + LANES] = base - to_lanes(squares(tgt_ref, at), eye)
    lse_ref[...] = row_block(src_ref[...], ((tgt_ref, offset_ref, z_ref),), eye)


def near_kernel(rows_ref, tgt_ref, offset_ref, held_ref, z_ref, lse_ref):
    lse_ref[...] = merge(held_ref[...], row_block(rows_ref[...], ((tgt_ref, offset_ref, z_ref),), diagonal()))


def far_kernel(count, *refs):
    eye = diagonal()
    own_ref, own_offset_ref, pair_ref, pair_offset_ref, held_ref, line_ref = refs[count : count + 6]
    own_z_ref, pair_z_ref, out_ref = refs[count + 6 :]
    slots = count + 1
    out_ref[0:1, :] = held_ref[...]
    out_ref[slots : slots + 2, :] = line_ref[...]
    for slot in range(count):
        sides = ((own_ref, own_offset_ref, own_z_ref.at[slot]), (pair_ref, pair_offset_ref, pair_z_ref.at[slot]))
        out_ref[slot + 1 : slot + 2, :] = row_block(refs[slot][...], sides, eye)


def sum_columns(near_ref, far_ref, offset, off_ref, out_ref):
    eye = diagonal()
    slots, src_count = offset.shape
    for slot in range(slots):
        for at in range(0, src_count, LANES):
            column = to_column(offset[slot : slot + 1, at : at + LANES], eye)
            off_ref[slot, at : at + LANES, :] = jnp.broadcast_to(column, (LANES, LANES))

    def shifted(slot, cols):
        z = near_ref[:, cols] if slot == 0 else far_ref[slot - 1, :, cols]
        return z + off_ref[slot]

    for group in range(out_ref.shape[0]):
        cols = slice(group * LANES, (group + 1) * LANES)
        peak = None
        for slot in range(slots):
            high = fold_rows(shifted(slot, cols), jnp.max)
            peak = high if peak is None else jnp.maximum(peak, high)
        peak = jnp.max(peak, axis=0, keepdims=True)
        mass = None
        for slot in range(slots):
            term = fold_rows(jnp.exp(shifted(slot, cols) - peak), jnp.sum)
            mass = term if mass is None else mass + term
        mass = jnp.sum(mass, axis=0, keepdims=True)
        out_ref[group : group + 1, :] = peak + jnp.log(mass)


def pair_kernel(near_ref, far_ref, lse_ref, slope_ref, shift_ref, out_ref, off_ref):
    sum_columns(near_ref, far_ref, shift_ref[...] - slope_ref[...] * lse_ref[...], off_ref, out_ref)


def own_kernel(near_ref, far_ref, lse_ref, slope_ref, shift_ref, sum_ref, out_ref, potential_ref, off_ref):
    lse, slope = lse_ref[...], slope_ref[...]
    potential_ref[...] = slope[0:1, :] * (sum_ref[...] - lse[0:1, :])
    sum_columns(near_ref, far_ref, shift_ref[...] - slope * lse, off_ref, out_ref)


def f32(*shape):
    return jax.ShapeDtypeStruct(shape, jnp.float32)


def params(mebibytes):
    return pltpu.CompilerParams(vmem_limit_bytes=mebibytes * 1024 * 1024)


def shards(sources, targets, tgt_potential, src_logmass, tgt_logmass, src_exponent, tgt_exponent):
    src_count, width = sources.shape
    tgt_count = targets.shape[0]
    slabs = lax.axis_size("blk")
    sets = lax.axis_size("tsplit")
    chips = slabs // 2
    far = chips - 1
    groups = tgt_count // LANES
    src_groups = src_count // LANES
    assert chips > 1 and chips & (chips - 1) == 0 and sets & (sets - 1) == 0

    def pair(value):
        return lax.ppermute(value, "blk", [(i, i ^ 1) for i in range(slabs)])

    def across(value, chip):
        return lax.ppermute(value, "blk", [(i, i ^ (2 * chip)) for i in range(slabs)])

    def along(value, step):
        return lax.ppermute(value, "tsplit", [(i, i ^ step) for i in range(sets)])

    def cost(blocks):
        pairs = blocks * src_count * tgt_count
        return pl.CostEstimate(flops=2 * pairs * width, bytes_accessed=2**20, transcendentals=pairs)

    core = lax.axis_index("blk") & 1
    core_word = core.astype(jnp.int32).reshape(1)
    pair_targets = pair(targets)
    inputs = (
        sources,
        targets,
        tgt_potential.reshape(groups, LANES),
        tgt_logmass.reshape(groups, LANES),
        src_exponent.reshape(src_groups, LANES),
        src_logmass.reshape(src_groups, LANES),
    )
    inputs = [pltpu.with_memory_space_constraint(x, pltpu.HBM) for x in inputs]

    def prepare_on(turn, *earlier):
        return pl.pallas_call(
            functools.partial(prepare_kernel, turn),
            out_shape=(
                jax.ShapeDtypeStruct(targets.shape, targets.dtype),
                f32(1, tgt_count),
                f32(src_count, tgt_count),
                f32(1, src_count),
                f32(2, src_count),
                f32(1, src_count),
            ),
            in_specs=[SMEM] + [HBM] * 6 + [VMEM] * len(earlier),
            out_specs=(VMEM,) * 6,
            scratch_shapes=[pltpu.VMEM(x.shape, x.dtype) for x in (inputs[0], *inputs[2:])]
            + [pltpu.SemaphoreType.DMA((6,))],
            compiler_params=params(12),
            cost_estimate=cost(1),
            name=f"prepare_{turn}",
        )(core_word, *inputs, *earlier)

    earlier = prepare_on(1)
    first, sent = lax.optimization_barrier((earlier[5], sources))
    far_blocks = [across(sent, chip) for chip in range(1, chips)]
    held, offset, own_z, lse, line, src_sum = prepare_on(0, *earlier[:5], first)
    pair_offset = pair(offset)
    pair_z, lse = pl.pallas_call(
        near_kernel,
        out_shape=(f32(src_count, tgt_count), f32(1, src_count)),
        in_specs=[VMEM] * 4,
        out_specs=(VMEM,) * 2,
        compiler_params=params(12),
        cost_estimate=cost(1),
        name="near_rows",
    )(sources, pair_targets, pair_offset, lse)
    far_lines = [across(line, chip) for chip in range(2, chips)]
    lse, *moved = lax.optimization_barrier((lse, *far_blocks, *far_lines))
    own_far_z, pair_far_z, payload = pl.pallas_call(
        functools.partial(far_kernel, far),
        out_shape=(f32(far, src_count, tgt_count), f32(far, src_count, tgt_count), f32(chips + 2, src_count)),
        in_specs=[VMEM] * (far + 6),
        out_specs=(VMEM,) * 3,
        compiler_params=params(8 + 3 * far),
        cost_estimate=cost(2 * far),
        name="far_rows",
    )(*moved[:far], held, offset, pair_targets, pair_offset, lse, line)

    other = across(payload, 1)
    lines = jnp.stack([line, other[chips:]] + moved[far:], axis=1)
    lse = merge(payload[:chips], jnp.stack([other[slot ^ 1] for slot in range(chips)]))
    chip = 2
    while chip < chips:
        other = across(lse, chip)
        lse = merge(lse, jnp.stack([other[slot ^ chip] for slot in range(chips)]))
        chip *= 2
    step = 1
    while step < sets:
        lse = merge(lse, along(lse, step))
        step *= 2

    def columns(kernel, near_z, far_z, *more):
        outs = (f32(groups, LANES), f32(1, src_count))[: 1 + len(more)]
        return pl.pallas_call(
            kernel,
            out_shape=outs,
            in_specs=[VMEM] * (5 + len(more)),
            out_specs=(VMEM,) * len(outs),
            scratch_shapes=[pltpu.VMEM((chips, src_count, LANES), jnp.float32)],
            compiler_params=params(8 + 2 * chips),
            cost_estimate=pl.CostEstimate(
                flops=6 * chips * src_count * tgt_count,
                bytes_accessed=2**20,
                transcendentals=chips * src_count * tgt_count,
            ),
            name="columns",
        )(near_z, far_z, lse, lines[0], lines[1], *more)

    (pair_part,) = columns(pair_kernel, pair_z, pair_far_z)
    lse, pair_part = lax.optimization_barrier((lse, pair_part))
    home = pair(pair_part)
    own_part, src_potential = columns(own_kernel, own_z, own_far_z, src_sum)
    total = merge(own_part, home).reshape(tgt_count)
    tgt_update = tgt_exponent * (2.0 * tgt_logmass + tgt_potential - total)
    return (src_potential.reshape(src_count), tgt_update)


def solution(mesh):
    placed = (
        P(("groups", "blk"), None),
        P(("groups", "blk", "tsplit"), None),
        P(("groups", "blk", "tsplit")),
        P(("groups", "blk")),
        P(("groups", "blk", "tsplit")),
        P(("groups", "blk")),
        P(("groups", "blk", "tsplit")),
    )
    return jax.shard_map(
        shards,
        mesh=mesh,
        in_specs=placed,
        out_specs=(P(("groups", "blk")), P(("groups", "blk", "tsplit"))),
        check_vma=False,
    )
```

```python
import functools

import jax
import jax.numpy as jnp
from jax import lax
from jax.experimental import pallas as pl
from jax.experimental.pallas import tpu as pltpu
from jax.sharding import PartitionSpec as P

EPSILON = 0.5
LOGIT_SCALE = 2.0 / EPSILON
LANES = 128
CHUNK = 256
VMEM = pl.BlockSpec(memory_space=pltpu.VMEM)
SMEM = pl.BlockSpec(memory_space=pltpu.SMEM)
HBM = pl.BlockSpec(memory_space=pltpu.HBM)
NT_DIMS = (((1,), (1,)), ((), ()))


def diagonal():
    rows = lax.broadcasted_iota(jnp.int32, (LANES, LANES), 0)
    cols = lax.broadcasted_iota(jnp.int32, (LANES, LANES), 1)
    return rows == cols


def to_lanes(column, eye):
    return jnp.sum(jnp.where(eye, column, 0.0), axis=0, keepdims=True)


def to_column(lanes, eye):
    return jnp.sum(jnp.where(eye, lanes, 0.0), axis=1, keepdims=True)


def fold_rows(value, op):
    return op(value.reshape(value.shape[0] // 8, 8, value.shape[1]), axis=0)


def merge(*parts):
    peak = functools.reduce(jnp.maximum, parts)
    return peak + jnp.log(sum(jnp.exp(part - peak) for part in parts))


def squares(rows_ref, at):
    rows = rows_ref[at : at + LANES, :].astype(jnp.float32)
    return jnp.sum(rows * rows, axis=1, keepdims=True) / EPSILON


def row_block(rows, sides, eye):
    rows = rows * LOGIT_SCALE
    src_count = rows.shape[0]
    peak = None
    for tgt_ref, offset_ref, z_ref in sides:
        for at in range(0, tgt_ref.shape[0], CHUNK):
            cols = slice(at, at + CHUNK)
            dots = lax.dot_general(rows, tgt_ref[cols, :], NT_DIMS, preferred_element_type=jnp.float32)
            z = dots + offset_ref[:, cols]
            z_ref[:, cols] = z
            for lane in range(0, CHUNK, LANES):
                part = z[:, lane : lane + LANES]
                peak = part if peak is None else jnp.maximum(peak, part)
    peak = jnp.max(peak, axis=1, keepdims=True)
    mass = None
    for _, _, z_ref in sides:
        for at in range(0, z_ref.shape[1], LANES):
            term = jnp.exp(z_ref[:, at : at + LANES] - peak)
            mass = term if mass is None else mass + term
    mass = jnp.sum(mass, axis=1, keepdims=True)
    parts = [slice(at, at + LANES) for at in range(0, src_count, LANES)]
    return jnp.concatenate([to_lanes(peak[p], eye) + jnp.log(to_lanes(mass[p], eye)) for p in parts], axis=1)


def prepare_kernel(turn, core_ref, *refs):
    inputs, refs = refs[:6], refs[6:]
    earlier, refs = refs[: 7 * (1 - turn)], refs[7 * (1 - turn) :]
    outs, scratch = refs[:7], refs[7:]

    @pl.when(core_ref[0] == turn)
    def work():
        prepare(*inputs, *outs, *scratch)

    if earlier:

        @pl.when(core_ref[0] != turn)
        def hand_on():
            for source, target in zip(earlier, outs):
                target[...] = source[...]


def prepare(
    src_hbm, tgt_hbm, pot_hbm, mass_hbm, slope_hbm, logmass_hbm,
    tgt_ref, src_ref, offset_ref, z_ref, lse_ref, line_ref, sum_ref,
    pot_ref, mass_ref, slope_ref, logmass_ref, sems,
):
    pairs = (
        (tgt_hbm, tgt_ref), (src_hbm, src_ref), (pot_hbm, pot_ref),
        (mass_hbm, mass_ref), (slope_hbm, slope_ref), (logmass_hbm, logmass_ref),
    )
    copies = [pltpu.make_async_copy(source, target, sems.at[at]) for at, (source, target) in enumerate(pairs)]
    for copy in copies:
        copy.start()
    for copy in copies[1:]:
        copy.wait()
    eye = diagonal()
    for group in range(src_ref.shape[0] // LANES):
        cols = slice(group * LANES, (group + 1) * LANES)
        square = to_lanes(squares(src_ref, group * LANES), eye)
        slope = slope_ref[group : group + 1, :]
        logmass = logmass_ref[group : group + 1, :]
        sum_ref[:, cols] = logmass + square
        line_ref[0:1, cols] = slope
        line_ref[1:2, cols] = slope * (logmass + square) + (logmass - square)
    copies[0].wait()
    for group in range(tgt_ref.shape[0] // LANES):
        at = group * LANES
        base = pot_ref[group : group + 1, :] + mass_ref[group : group + 1, :]
        offset_ref[:, at : at + LANES] = base - to_lanes(squares(tgt_ref, at), eye)
    lse_ref[...] = row_block(src_ref[...], ((tgt_ref, offset_ref, z_ref),), eye)


def near_kernel(rows_ref, tgt_ref, offset_ref, held_ref, z_ref, lse_ref):
    lse_ref[...] = merge(held_ref[...], row_block(rows_ref[...], ((tgt_ref, offset_ref, z_ref),), diagonal()))


def far_kernel(count, *refs):
    eye = diagonal()
    own_ref, own_offset_ref, pair_ref, pair_offset_ref, held_ref, line_ref = refs[count : count + 6]
    own_z_ref, pair_z_ref, out_ref = refs[count + 6 :]
    slots = count + 1
    out_ref[0:1, :] = held_ref[...]
    out_ref[slots : slots + 2, :] = line_ref[...]
    for slot in range(count):
        sides = ((own_ref, own_offset_ref, own_z_ref.at[slot]), (pair_ref, pair_offset_ref, pair_z_ref.at[slot]))
        out_ref[slot + 1 : slot + 2, :] = row_block(refs[slot][...], sides, eye)


def sum_columns(near_ref, far_ref, offset, off_ref, out_ref):
    eye = diagonal()
    slots, src_count = offset.shape
    for slot in range(slots):
        for at in range(0, src_count, LANES):
            column = to_column(offset[slot : slot + 1, at : at + LANES], eye)
            off_ref[slot, at : at + LANES, :] = jnp.broadcast_to(column, (LANES, LANES))

    def shifted(slot, cols):
        z = near_ref[:, cols] if slot == 0 else far_ref[slot - 1, :, cols]
        return z + off_ref[slot]

    for group in range(out_ref.shape[0]):
        cols = slice(group * LANES, (group + 1) * LANES)
        peak = None
        for slot in range(slots):
            high = fold_rows(shifted(slot, cols), jnp.max)
            peak = high if peak is None else jnp.maximum(peak, high)
        peak = jnp.max(peak, axis=0, keepdims=True)
        mass = None
        for slot in range(slots):
            term = fold_rows(jnp.exp(shifted(slot, cols) - peak), jnp.sum)
            mass = term if mass is None else mass + term
        mass = jnp.sum(mass, axis=0, keepdims=True)
        out_ref[group : group + 1, :] = peak + jnp.log(mass)


def pair_kernel(near_ref, far_ref, lse_ref, slope_ref, shift_ref, out_ref, off_ref):
    sum_columns(near_ref, far_ref, shift_ref[...] - slope_ref[...] * lse_ref[...], off_ref, out_ref)


def own_kernel(near_ref, far_ref, lse_ref, slope_ref, shift_ref, sum_ref, out_ref, potential_ref, off_ref):
    lse, slope = lse_ref[...], slope_ref[...]
    potential_ref[...] = slope[0:1, :] * (sum_ref[...] - lse[0:1, :])
    sum_columns(near_ref, far_ref, shift_ref[...] - slope * lse, off_ref, out_ref)


def f32(*shape):
    return jax.ShapeDtypeStruct(shape, jnp.float32)


def params(mebibytes):
    return pltpu.CompilerParams(vmem_limit_bytes=mebibytes * 1024 * 1024)


def shards(sources, targets, tgt_potential, src_logmass, tgt_logmass, src_exponent, tgt_exponent):
    src_count, width = sources.shape
    tgt_count = targets.shape[0]
    slabs = lax.axis_size("blk")
    sets = lax.axis_size("tsplit")
    chips = slabs // 2
    far = chips - 1
    groups = tgt_count // LANES
    src_groups = src_count // LANES
    assert chips > 1 and chips & (chips - 1) == 0 and sets & (sets - 1) == 0

    def pair(value):
        return lax.ppermute(value, "blk", [(i, i ^ 1) for i in range(slabs)])

    def across(value, chip):
        return lax.ppermute(value, "blk", [(i, i ^ (2 * chip)) for i in range(slabs)])

    def along(value, step):
        return lax.ppermute(value, "tsplit", [(i, i ^ step) for i in range(sets)])

    def cost(blocks):
        pairs = blocks * src_count * tgt_count
        return pl.CostEstimate(flops=2 * pairs * width, bytes_accessed=2**20, transcendentals=pairs)

    core = lax.axis_index("blk") & 1
    core_word = core.astype(jnp.int32).reshape(1)
    pair_targets = pair(targets)
    inputs = (
        sources,
        targets,
        tgt_potential.reshape(groups, LANES),
        tgt_logmass.reshape(groups, LANES),
        src_exponent.reshape(src_groups, LANES),
        src_logmass.reshape(src_groups, LANES),
    )
    inputs = [pltpu.with_memory_space_constraint(x, pltpu.HBM) for x in inputs]

    def prepare_on(turn, *earlier):
        return pl.pallas_call(
            functools.partial(prepare_kernel, turn),
            out_shape=(
                jax.ShapeDtypeStruct(targets.shape, targets.dtype),
                jax.ShapeDtypeStruct(sources.shape, sources.dtype),
                f32(1, tgt_count),
                f32(src_count, tgt_count),
                f32(1, src_count),
                f32(2, src_count),
                f32(1, src_count),
            ),
            in_specs=[SMEM] + [HBM] * 6 + [VMEM] * len(earlier),
            out_specs=(VMEM,) * 7,
            scratch_shapes=[pltpu.VMEM(x.shape, x.dtype) for x in inputs[2:]]
            + [pltpu.SemaphoreType.DMA((6,))],
            compiler_params=params(12),
            cost_estimate=cost(1),
            name=f"prepare_{turn}",
        )(core_word, *inputs, *earlier)

    earlier = prepare_on(1)
    first, sent = lax.optimization_barrier((earlier[6], sources))
    far_blocks = [across(sent, chip) for chip in range(1, chips)]
    held, held_sources, offset, own_z, lse, line, src_sum = prepare_on(0, *earlier[:6], first)
    pair_offset = pair(offset)
    pair_z, lse = pl.pallas_call(
        near_kernel,
        out_shape=(f32(src_count, tgt_count), f32(1, src_count)),
        in_specs=[VMEM] * 4,
        out_specs=(VMEM,) * 2,
        compiler_params=params(12),
        cost_estimate=cost(1),
        name="near_rows",
    )(held_sources, pair_targets, pair_offset, lse)
    far_lines = [across(line, chip) for chip in range(2, chips)]
    lse, *moved = lax.optimization_barrier((lse, *far_blocks, *far_lines))
    own_far_z, pair_far_z, payload = pl.pallas_call(
        functools.partial(far_kernel, far),
        out_shape=(f32(far, src_count, tgt_count), f32(far, src_count, tgt_count), f32(chips + 2, src_count)),
        in_specs=[VMEM] * (far + 6),
        out_specs=(VMEM,) * 3,
        compiler_params=params(8 + 3 * far),
        cost_estimate=cost(2 * far),
        name="far_rows",
    )(*moved[:far], held, offset, pair_targets, pair_offset, lse, line)

    other = across(payload, 1)
    lines = jnp.stack([line, other[chips:]] + moved[far:], axis=1)
    lse = merge(payload[:chips], jnp.stack([other[slot ^ 1] for slot in range(chips)]))
    chip = 2
    while chip < chips:
        other = across(lse, chip)
        lse = merge(lse, jnp.stack([other[slot ^ chip] for slot in range(chips)]))
        chip *= 2
    around = lax.all_gather(lse, "tsplit")
    lse = merge(*[around[z] for z in range(sets)])

    def columns(kernel, near_z, far_z, *more):
        outs = (f32(groups, LANES), f32(1, src_count))[: 1 + len(more)]
        return pl.pallas_call(
            kernel,
            out_shape=outs,
            in_specs=[VMEM] * (5 + len(more)),
            out_specs=(VMEM,) * len(outs),
            scratch_shapes=[pltpu.VMEM((chips, src_count, LANES), jnp.float32)],
            compiler_params=params(8 + 2 * chips),
            cost_estimate=pl.CostEstimate(
                flops=6 * chips * src_count * tgt_count,
                bytes_accessed=2**20,
                transcendentals=chips * src_count * tgt_count,
            ),
            name="columns",
        )(near_z, far_z, lse, lines[0], lines[1], *more)

    (pair_part,) = columns(pair_kernel, pair_z, pair_far_z)
    lse, pair_part = lax.optimization_barrier((lse, pair_part))
    home = pair(pair_part)
    own_part, src_potential = columns(own_kernel, own_z, own_far_z, src_sum)
    total = merge(own_part, home).reshape(tgt_count)
    tgt_update = tgt_exponent * (2.0 * tgt_logmass + tgt_potential - total)
    return (src_potential.reshape(src_count), tgt_update)


def solution(mesh):
    placed = (
        P(("groups", "blk"), None),
        P(("groups", "blk", "tsplit"), None),
        P(("groups", "blk", "tsplit")),
        P(("groups", "blk")),
        P(("groups", "blk", "tsplit")),
        P(("groups", "blk")),
        P(("groups", "blk", "tsplit")),
    )
    return jax.shard_map(
        shards,
        mesh=mesh,
        in_specs=placed,
        out_specs=(P(("groups", "blk")), P(("groups", "blk", "tsplit"))),
        check_vma=False,
    )
```

```python
import functools

import jax
import jax.numpy as jnp
from jax import lax
from jax.experimental import pallas as pl
from jax.experimental.pallas import tpu as pltpu
from jax.sharding import PartitionSpec as P

EPSILON = 0.5
LOGIT_SCALE = 2.0 / EPSILON
LANES = 128
CHUNK = 256
VMEM = pl.BlockSpec(memory_space=pltpu.VMEM)
SMEM = pl.BlockSpec(memory_space=pltpu.SMEM)
HBM = pl.BlockSpec(memory_space=pltpu.HBM)
NT_DIMS = (((1,), (1,)), ((), ()))


def diagonal():
    rows = lax.broadcasted_iota(jnp.int32, (LANES, LANES), 0)
    cols = lax.broadcasted_iota(jnp.int32, (LANES, LANES), 1)
    return rows == cols


def to_lanes(column, eye):
    return jnp.sum(jnp.where(eye, column, 0.0), axis=0, keepdims=True)


def to_column(lanes, eye):
    return jnp.sum(jnp.where(eye, lanes, 0.0), axis=1, keepdims=True)


def fold_rows(value, op):
    return op(value.reshape(value.shape[0] // 8, 8, value.shape[1]), axis=0)


def merge(*parts):
    peak = functools.reduce(jnp.maximum, parts)
    return peak + jnp.log(sum(jnp.exp(part - peak) for part in parts))


def squares(rows_ref, at):
    rows = rows_ref[at : at + LANES, :].astype(jnp.float32)
    return jnp.sum(rows * rows, axis=1, keepdims=True) / EPSILON


def row_block(rows, sides, eye):
    rows = rows * LOGIT_SCALE
    src_count = rows.shape[0]
    peak = None
    for tgt_ref, offset_ref, z_ref in sides:
        for at in range(0, tgt_ref.shape[0], CHUNK):
            cols = slice(at, at + CHUNK)
            dots = lax.dot_general(rows, tgt_ref[cols, :], NT_DIMS, preferred_element_type=jnp.float32)
            z = dots + offset_ref[:, cols]
            z_ref[:, cols] = z
            for lane in range(0, CHUNK, LANES):
                part = z[:, lane : lane + LANES]
                peak = part if peak is None else jnp.maximum(peak, part)
    peak = jnp.max(peak, axis=1, keepdims=True)
    mass = None
    for _, _, z_ref in sides:
        for at in range(0, z_ref.shape[1], LANES):
            term = jnp.exp(z_ref[:, at : at + LANES] - peak)
            mass = term if mass is None else mass + term
    mass = jnp.sum(mass, axis=1, keepdims=True)
    parts = [slice(at, at + LANES) for at in range(0, src_count, LANES)]
    return jnp.concatenate([to_lanes(peak[p], eye) + jnp.log(to_lanes(mass[p], eye)) for p in parts], axis=1)


def prepare_kernel(turn, core_ref, *refs):
    inputs, refs = refs[:6], refs[6:]
    earlier, refs = refs[: 6 * (1 - turn)], refs[6 * (1 - turn) :]
    outs, scratch = refs[:6], refs[6:]

    @pl.when(core_ref[0] == turn)
    def work():
        prepare(*inputs, *outs, *scratch)

    if earlier:

        @pl.when(core_ref[0] != turn)
        def hand_on():
            for source, target in zip(earlier, outs):
                target[...] = source[...]


def prepare(
    src_hbm, tgt_hbm, pot_hbm, mass_hbm, slope_hbm, logmass_hbm,
    tgt_ref, offset_ref, z_ref, lse_ref, line_ref, sum_ref,
    src_ref, pot_ref, mass_ref, slope_ref, logmass_ref, sems,
):
    pairs = (
        (tgt_hbm, tgt_ref), (src_hbm, src_ref), (pot_hbm, pot_ref),
        (mass_hbm, mass_ref), (slope_hbm, slope_ref), (logmass_hbm, logmass_ref),
    )
    copies = [pltpu.make_async_copy(source, target, sems.at[at]) for at, (source, target) in enumerate(pairs)]
    for copy in copies:
        copy.start()
    for copy in copies[1:]:
        copy.wait()
    eye = diagonal()
    for group in range(src_ref.shape[0] // LANES):
        cols = slice(group * LANES, (group + 1) * LANES)
        square = to_lanes(squares(src_ref, group * LANES), eye)
        slope = slope_ref[group : group + 1, :]
        logmass = logmass_ref[group : group + 1, :]
        sum_ref[:, cols] = logmass + square
        line_ref[0:1, cols] = slope
        line_ref[1:2, cols] = slope * (logmass + square) + (logmass - square)
    copies[0].wait()
    for group in range(tgt_ref.shape[0] // LANES):
        at = group * LANES
        base = pot_ref[group : group + 1, :] + mass_ref[group : group + 1, :]
        offset_ref[:, at : at + LANES] = base - to_lanes(squares(tgt_ref, at), eye)
    lse_ref[...] = row_block(src_ref[...], ((tgt_ref, offset_ref, z_ref),), eye)


def near_kernel(rows_ref, tgt_ref, offset_ref, held_ref, z_ref, lse_ref):
    lse_ref[...] = merge(held_ref[...], row_block(rows_ref[...], ((tgt_ref, offset_ref, z_ref),), diagonal()))


def far_kernel(count, *refs):
    eye = diagonal()
    own_ref, own_offset_ref, pair_ref, pair_offset_ref, held_ref, line_ref = refs[count : count + 6]
    own_z_ref, pair_z_ref, out_ref = refs[count + 6 :]
    slots = count + 1
    out_ref[0:1, :] = held_ref[...]
    out_ref[slots : slots + 2, :] = line_ref[...]
    for slot in range(count):
        sides = ((own_ref, own_offset_ref, own_z_ref.at[slot]), (pair_ref, pair_offset_ref, pair_z_ref.at[slot]))
        out_ref[slot + 1 : slot + 2, :] = row_block(refs[slot][...], sides, eye)


def sum_columns(near_ref, far_ref, offset, off_ref, out_ref):
    eye = diagonal()
    slots, src_count = offset.shape
    for slot in range(slots):
        for at in range(0, src_count, LANES):
            column = to_column(offset[slot : slot + 1, at : at + LANES], eye)
            off_ref[slot, at : at + LANES, :] = jnp.broadcast_to(column, (LANES, LANES))

    def shifted(slot, cols):
        z = near_ref[:, cols] if slot == 0 else far_ref[slot - 1, :, cols]
        return z + off_ref[slot]

    for group in range(out_ref.shape[0]):
        cols = slice(group * LANES, (group + 1) * LANES)
        peak = None
        for slot in range(slots):
            high = fold_rows(shifted(slot, cols), jnp.max)
            peak = high if peak is None else jnp.maximum(peak, high)
        peak = jnp.max(peak, axis=0, keepdims=True)
        mass = None
        for slot in range(slots):
            term = fold_rows(jnp.exp(shifted(slot, cols) - peak), jnp.sum)
            mass = term if mass is None else mass + term
        mass = jnp.sum(mass, axis=0, keepdims=True)
        out_ref[group : group + 1, :] = peak + jnp.log(mass)


def pair_kernel(near_ref, far_ref, lse_ref, slope_ref, shift_ref, out_ref, off_ref):
    sum_columns(near_ref, far_ref, shift_ref[...] - slope_ref[...] * lse_ref[...], off_ref, out_ref)


def own_kernel(near_ref, far_ref, lse_ref, slope_ref, shift_ref, sum_ref, out_ref, potential_ref, off_ref):
    lse, slope = lse_ref[...], slope_ref[...]
    potential_ref[...] = slope[0:1, :] * (sum_ref[...] - lse[0:1, :])
    sum_columns(near_ref, far_ref, shift_ref[...] - slope * lse, off_ref, out_ref)


def f32(*shape):
    return jax.ShapeDtypeStruct(shape, jnp.float32)


def params(mebibytes):
    return pltpu.CompilerParams(vmem_limit_bytes=mebibytes * 1024 * 1024)


def shards(sources, targets, tgt_potential, src_logmass, tgt_logmass, src_exponent, tgt_exponent):
    src_count, width = sources.shape
    tgt_count = targets.shape[0]
    slabs = lax.axis_size("blk")
    sets = lax.axis_size("tsplit")
    chips = slabs // 2
    far = chips - 1
    groups = tgt_count // LANES
    src_groups = src_count // LANES
    assert chips > 1 and chips & (chips - 1) == 0 and sets & (sets - 1) == 0

    def pair(value):
        return lax.ppermute(value, "blk", [(i, i ^ 1) for i in range(slabs)])

    def across(value, chip):
        return lax.ppermute(value, "blk", [(i, i ^ (2 * chip)) for i in range(slabs)])

    def along(value, step):
        return lax.ppermute(value, "tsplit", [(i, i ^ step) for i in range(sets)])

    def cost(blocks):
        pairs = blocks * src_count * tgt_count
        return pl.CostEstimate(flops=2 * pairs * width, bytes_accessed=2**20, transcendentals=pairs)

    core = lax.axis_index("blk") & 1
    core_word = core.astype(jnp.int32).reshape(1)
    pair_targets = pair(targets)
    inputs = (
        sources,
        targets,
        tgt_potential.reshape(groups, LANES),
        tgt_logmass.reshape(groups, LANES),
        src_exponent.reshape(src_groups, LANES),
        src_logmass.reshape(src_groups, LANES),
    )
    inputs = [pltpu.with_memory_space_constraint(x, pltpu.HBM) for x in inputs]

    def prepare_on(turn, *earlier):
        return pl.pallas_call(
            functools.partial(prepare_kernel, turn),
            out_shape=(
                jax.ShapeDtypeStruct(targets.shape, targets.dtype),
                f32(1, tgt_count),
                f32(src_count, tgt_count),
                f32(1, src_count),
                f32(2, src_count),
                f32(1, src_count),
            ),
            in_specs=[SMEM] + [HBM] * 6 + [VMEM] * len(earlier),
            out_specs=(VMEM,) * 6,
            scratch_shapes=[pltpu.VMEM(x.shape, x.dtype) for x in (inputs[0], *inputs[2:])]
            + [pltpu.SemaphoreType.DMA((6,))],
            compiler_params=params(12),
            cost_estimate=cost(1),
            name=f"prepare_{turn}",
        )(core_word, *inputs, *earlier)

    earlier = prepare_on(1)
    first, sent = lax.optimization_barrier((earlier[5], sources))
    far_blocks = [across(sent, chip) for chip in range(1, chips)]
    held, offset, own_z, lse, line, src_sum = prepare_on(0, *earlier[:5], first)
    pair_offset = pair(offset)
    pair_z, lse = pl.pallas_call(
        near_kernel,
        out_shape=(f32(src_count, tgt_count), f32(1, src_count)),
        in_specs=[VMEM] * 4,
        out_specs=(VMEM,) * 2,
        compiler_params=params(12),
        cost_estimate=cost(1),
        name="near_rows",
    )(sources, pair_targets, pair_offset, lse)
    far_lines = [across(line, chip) for chip in range(2, chips)]
    lse, *moved = lax.optimization_barrier((lse, *far_blocks, *far_lines))
    own_far_z, pair_far_z, payload = pl.pallas_call(
        functools.partial(far_kernel, far),
        out_shape=(f32(far, src_count, tgt_count), f32(far, src_count, tgt_count), f32(chips + 2, src_count)),
        in_specs=[VMEM] * (far + 6),
        out_specs=(VMEM,) * 3,
        compiler_params=params(8 + 3 * far),
        cost_estimate=cost(2 * far),
        name="far_rows",
    )(*moved[:far], held, offset, pair_targets, pair_offset, lse, line)

    other = across(payload, 1)
    lines = jnp.stack([line, other[chips:]] + moved[far:], axis=1)
    lse = merge(payload[:chips], jnp.stack([other[slot ^ 1] for slot in range(chips)]))
    chip = 2
    while chip < chips:
        other = across(lse, chip)
        lse = merge(lse, jnp.stack([other[slot ^ chip] for slot in range(chips)]))
        chip *= 2
    lse = merge(lse, *[along(lse, step) for step in range(sets - 1, 0, -1)])

    def columns(kernel, near_z, far_z, *more):
        outs = (f32(groups, LANES), f32(1, src_count))[: 1 + len(more)]
        return pl.pallas_call(
            kernel,
            out_shape=outs,
            in_specs=[VMEM] * (5 + len(more)),
            out_specs=(VMEM,) * len(outs),
            scratch_shapes=[pltpu.VMEM((chips, src_count, LANES), jnp.float32)],
            compiler_params=params(8 + 2 * chips),
            cost_estimate=pl.CostEstimate(
                flops=6 * chips * src_count * tgt_count,
                bytes_accessed=2**20,
                transcendentals=chips * src_count * tgt_count,
            ),
            name="columns",
        )(near_z, far_z, lse, lines[0], lines[1], *more)

    (pair_part,) = columns(pair_kernel, pair_z, pair_far_z)
    lse, pair_part = lax.optimization_barrier((lse, pair_part))
    home = pair(pair_part)
    own_part, src_potential = columns(own_kernel, own_z, own_far_z, src_sum)
    total = merge(own_part, home).reshape(tgt_count)
    tgt_update = tgt_exponent * (2.0 * tgt_logmass + tgt_potential - total)
    return (src_potential.reshape(src_count), tgt_update)


def solution(mesh):
    placed = (
        P(("groups", "blk"), None),
        P(("groups", "blk", "tsplit"), None),
        P(("groups", "blk", "tsplit")),
        P(("groups", "blk")),
        P(("groups", "blk", "tsplit")),
        P(("groups", "blk")),
        P(("groups", "blk", "tsplit")),
    )
    return jax.shard_map(
        shards,
        mesh=mesh,
        in_specs=placed,
        out_specs=(P(("groups", "blk")), P(("groups", "blk", "tsplit"))),
        check_vma=False,
    )
```

```python
import functools
import math

import jax
import jax.numpy as jnp
from jax import lax
from jax.experimental import pallas as pl
from jax.experimental.pallas import tpu as pltpu
from jax.sharding import PartitionSpec as P

EPSILON = 0.5
LOGIT_SCALE = 2.0 / EPSILON
LOG2_E = math.log2(math.e)
LOG_2 = math.log(2.0)
LANES = 128
CHUNK = 256
VMEM = pl.BlockSpec(memory_space=pltpu.VMEM)
SMEM = pl.BlockSpec(memory_space=pltpu.SMEM)
HBM = pl.BlockSpec(memory_space=pltpu.HBM)
NT_DIMS = (((1,), (1,)), ((), ()))


def diagonal():
    rows = lax.broadcasted_iota(jnp.int32, (LANES, LANES), 0)
    cols = lax.broadcasted_iota(jnp.int32, (LANES, LANES), 1)
    return rows == cols


def to_lanes(column, eye):
    return jnp.sum(jnp.where(eye, column, 0.0), axis=0, keepdims=True)


def to_column(lanes, eye):
    return jnp.sum(jnp.where(eye, lanes, 0.0), axis=1, keepdims=True)


def merge(*parts):
    peak = functools.reduce(jnp.maximum, parts)
    return peak + jnp.log(sum(jnp.exp(part - peak) for part in parts))


def squares(rows_ref, at):
    rows = rows_ref[at : at + LANES, :].astype(jnp.float32)
    return jnp.sum(rows * rows, axis=1, keepdims=True) / EPSILON


def row_block(rows, sides, eye):
    rows = rows * LOGIT_SCALE
    src_count = rows.shape[0]

    def product(side, at):
        tgt_ref, offset_ref, z_ref = sides[side]
        cols = slice(at, at + CHUNK)
        dots = lax.dot_general(rows, tgt_ref[cols, :], NT_DIMS, preferred_element_type=jnp.float32)
        z = (dots + offset_ref[:, cols]) * LOG2_E
        z_ref[:, cols] = z
        high = z[:, :LANES]
        for lane in range(LANES, CHUNK, LANES):
            high = jnp.maximum(high, z[:, lane : lane + LANES])
        return high

    def raise_to(side, at, peak):
        z_ref = sides[side][2]
        return sum(jnp.exp2(z_ref[:, lane : lane + LANES] - peak) for lane in range(at, at + CHUNK, LANES))

    steps = range(0, sides[0][0].shape[0], CHUNK)
    peaks, masses = [], []
    for side in range(len(sides) + 1):
        peak = mass = None
        for at in steps:
            if side < len(sides):
                high = product(side, at)
                peak = high if peak is None else jnp.maximum(peak, high)
            if side > 0:
                term = raise_to(side - 1, at, peaks[-1])
                mass = term if mass is None else mass + term
        if side < len(sides):
            peaks.append(peak)
        if side > 0:
            masses.append(mass)
    peak = jnp.max(functools.reduce(jnp.maximum, peaks), axis=1, keepdims=True)
    mass = sum(mass * jnp.exp2(high - peak) for high, mass in zip(peaks, masses))
    mass = jnp.sum(mass, axis=1, keepdims=True)
    parts = [slice(at, at + LANES) for at in range(0, src_count, LANES)]
    return jnp.concatenate([to_lanes(peak[p], eye) * LOG_2 + jnp.log(to_lanes(mass[p], eye)) for p in parts], axis=1)


def prepare_kernel(turn, core_ref, *refs):
    inputs, refs = refs[:6], refs[6:]
    earlier, refs = refs[: 6 * (1 - turn)], refs[6 * (1 - turn) :]
    outs, scratch = refs[:6], refs[6:]

    @pl.when(core_ref[0] == turn)
    def work():
        prepare(*inputs, *outs, *scratch)

    if earlier:

        @pl.when(core_ref[0] != turn)
        def hand_on():
            for source, target in zip(earlier, outs):
                target[...] = source[...]


def prepare(
    src_hbm, tgt_hbm, pot_hbm, mass_hbm, slope_hbm, logmass_hbm,
    tgt_ref, offset_ref, z_ref, lse_ref, line_ref, sum_ref,
    src_ref, pot_ref, mass_ref, slope_ref, logmass_ref, sems,
):
    pairs = (
        (tgt_hbm, tgt_ref), (src_hbm, src_ref), (pot_hbm, pot_ref),
        (mass_hbm, mass_ref), (slope_hbm, slope_ref), (logmass_hbm, logmass_ref),
    )
    copies = [pltpu.make_async_copy(source, target, sems.at[at]) for at, (source, target) in enumerate(pairs)]
    for copy in copies:
        copy.start()
    for copy in copies[1:]:
        copy.wait()
    eye = diagonal()
    for group in range(src_ref.shape[0] // LANES):
        cols = slice(group * LANES, (group + 1) * LANES)
        square = to_lanes(squares(src_ref, group * LANES), eye)
        slope = slope_ref[group : group + 1, :]
        logmass = logmass_ref[group : group + 1, :]
        sum_ref[:, cols] = logmass + square
        line_ref[0:1, cols] = slope
        line_ref[1:2, cols] = slope * (logmass + square) + (logmass - square)
    copies[0].wait()
    for group in range(tgt_ref.shape[0] // LANES):
        at = group * LANES
        base = pot_ref[group : group + 1, :] + mass_ref[group : group + 1, :]
        offset_ref[:, at : at + LANES] = base - to_lanes(squares(tgt_ref, at), eye)
    lse_ref[...] = row_block(src_ref[...], ((tgt_ref, offset_ref, z_ref),), eye)


def near_kernel(rows_ref, tgt_ref, offset_ref, held_ref, z_ref, lse_ref):
    lse_ref[...] = merge(held_ref[...], row_block(rows_ref[...], ((tgt_ref, offset_ref, z_ref),), diagonal()))


def far_kernel(count, *refs):
    eye = diagonal()
    own_ref, own_offset_ref, pair_ref, pair_offset_ref, held_ref, line_ref = refs[count : count + 6]
    own_z_ref, pair_z_ref, out_ref = refs[count + 6 :]
    slots = count + 1
    out_ref[0:1, :] = held_ref[...]
    out_ref[slots : slots + 2, :] = line_ref[...]
    for slot in range(count):
        sides = ((own_ref, own_offset_ref, own_z_ref.at[slot]), (pair_ref, pair_offset_ref, pair_z_ref.at[slot]))
        out_ref[slot + 1 : slot + 2, :] = row_block(refs[slot][...], sides, eye)


def sum_columns(near_ref, far_ref, offset, off_ref, out_ref):
    eye = diagonal()
    slots, src_count = offset.shape
    for slot in range(slots):
        for at in range(0, src_count, LANES):
            column = to_column(offset[slot : slot + 1, at : at + LANES] * LOG2_E, eye)
            off_ref[slot, at : at + LANES, :] = jnp.broadcast_to(column, (LANES, LANES))

    for group in range(out_ref.shape[0]):
        cols = slice(group * LANES, (group + 1) * LANES)
        peaks, masses = [], []
        for slot in range(slots):
            z = near_ref[:, cols] if slot == 0 else far_ref[slot - 1, :, cols]
            z = (z + off_ref[slot]).reshape(src_count // 8, 8, LANES)
            peaks.append(jnp.max(z, axis=0))
            masses.append(jnp.sum(jnp.exp2(z - peaks[-1]), axis=0))
        peak = jnp.max(functools.reduce(jnp.maximum, peaks), axis=0, keepdims=True)
        mass = sum(mass * jnp.exp2(high - peak) for high, mass in zip(peaks, masses))
        mass = jnp.sum(mass, axis=0, keepdims=True)
        out_ref[group : group + 1, :] = peak * LOG_2 + jnp.log(mass)


def pair_kernel(near_ref, far_ref, lse_ref, slope_ref, shift_ref, out_ref, off_ref):
    sum_columns(near_ref, far_ref, shift_ref[...] - slope_ref[...] * lse_ref[...], off_ref, out_ref)


def own_kernel(near_ref, far_ref, lse_ref, slope_ref, shift_ref, sum_ref, out_ref, potential_ref, off_ref):
    lse, slope = lse_ref[...], slope_ref[...]
    potential_ref[...] = slope[0:1, :] * (sum_ref[...] - lse[0:1, :])
    sum_columns(near_ref, far_ref, shift_ref[...] - slope * lse, off_ref, out_ref)


def f32(*shape):
    return jax.ShapeDtypeStruct(shape, jnp.float32)


def params(mebibytes):
    return pltpu.CompilerParams(vmem_limit_bytes=mebibytes * 1024 * 1024)


def shards(sources, targets, tgt_potential, src_logmass, tgt_logmass, src_exponent, tgt_exponent):
    src_count, width = sources.shape
    tgt_count = targets.shape[0]
    slabs = lax.axis_size("blk")
    sets = lax.axis_size("tsplit")
    chips = slabs // 2
    far = chips - 1
    groups = tgt_count // LANES
    src_groups = src_count // LANES
    assert chips > 1 and sets > 1 and chips & (chips - 1) == 0 and sets & (sets - 1) == 0

    def pair(value):
        return lax.ppermute(value, "blk", [(i, i ^ 1) for i in range(slabs)])

    def across(value, chip):
        return lax.ppermute(value, "blk", [(i, i ^ (2 * chip)) for i in range(slabs)])

    def along(value, step):
        return lax.ppermute(value, "tsplit", [(i, i ^ step) for i in range(sets)])

    def cost(blocks):
        pairs = blocks * src_count * tgt_count
        return pl.CostEstimate(flops=2 * pairs * width, bytes_accessed=2**20, transcendentals=pairs)

    core = lax.axis_index("blk") & 1
    core_word = core.astype(jnp.int32).reshape(1)
    pair_targets = pair(targets)
    inputs = (
        sources,
        targets,
        tgt_potential.reshape(groups, LANES),
        tgt_logmass.reshape(groups, LANES),
        src_exponent.reshape(src_groups, LANES),
        src_logmass.reshape(src_groups, LANES),
    )
    inputs = [pltpu.with_memory_space_constraint(x, pltpu.HBM) for x in inputs]

    def prepare_on(turn, *earlier):
        return pl.pallas_call(
            functools.partial(prepare_kernel, turn),
            out_shape=(
                jax.ShapeDtypeStruct(targets.shape, targets.dtype),
                f32(1, tgt_count),
                f32(src_count, tgt_count),
                f32(1, src_count),
                f32(2, src_count),
                f32(1, src_count),
            ),
            in_specs=[SMEM] + [HBM] * 6 + [VMEM] * len(earlier),
            out_specs=(VMEM,) * 6,
            scratch_shapes=[pltpu.VMEM(x.shape, x.dtype) for x in (inputs[0], *inputs[2:])]
            + [pltpu.SemaphoreType.DMA((6,))],
            compiler_params=params(12),
            cost_estimate=cost(1),
            name=f"prepare_{turn}",
        )(core_word, *inputs, *earlier)

    earlier = prepare_on(1)
    first, sent = lax.optimization_barrier((earlier[5], sources))
    far_blocks = [across(sent, chip) for chip in range(1, chips)]
    held, offset, own_z, lse, line, src_sum = prepare_on(0, *earlier[:5], first)
    pair_offset = pair(offset)
    pair_z, lse = pl.pallas_call(
        near_kernel,
        out_shape=(f32(src_count, tgt_count), f32(1, src_count)),
        in_specs=[VMEM] * 4,
        out_specs=(VMEM,) * 2,
        compiler_params=params(12),
        cost_estimate=cost(1),
        name="near_rows",
    )(sources, pair_targets, pair_offset, lse)
    far_lines = [across(line, chip) for chip in range(2, chips)]
    lse, *moved = lax.optimization_barrier((lse, *far_blocks, *far_lines))
    own_far_z, pair_far_z, payload = pl.pallas_call(
        functools.partial(far_kernel, far),
        out_shape=(f32(far, src_count, tgt_count), f32(far, src_count, tgt_count), f32(chips + 2, src_count)),
        in_specs=[VMEM] * (far + 6),
        out_specs=(VMEM,) * 3,
        compiler_params=params(8 + 3 * far),
        cost_estimate=cost(2 * far),
        name="far_rows",
    )(*moved[:far], held, offset, pair_targets, pair_offset, lse, line)

    def mirror(value, chip):
        return jnp.stack([value[slot ^ chip] for slot in range(chips)])

    joined = lax.ppermute(
        payload,
        ("blk", "tsplit"),
        [(b * sets + z, (b ^ 2) * sets + (z ^ 1)) for b in range(slabs) for z in range(sets)],
    )
    beside = along(payload, 1)
    other = across(payload, 1)
    lines = jnp.stack([line, other[chips:]] + moved[far:], axis=1)
    lse = merge(payload[:chips], mirror(joined, 1), beside[:chips], mirror(other, 1))
    chip = 2
    while chip < chips:
        lse = merge(lse, mirror(across(lse, chip), chip))
        chip *= 2
    step = 2
    while step < sets:
        lse = merge(lse, along(lse, step))
        step *= 2

    def columns(kernel, near_z, far_z, *more):
        outs = (f32(groups, LANES), f32(1, src_count))[: 1 + len(more)]
        return pl.pallas_call(
            kernel,
            out_shape=outs,
            in_specs=[VMEM] * (5 + len(more)),
            out_specs=(VMEM,) * len(outs),
            scratch_shapes=[pltpu.VMEM((chips, src_count, LANES), jnp.float32)],
            compiler_params=params(8 + 2 * chips),
            cost_estimate=pl.CostEstimate(
                flops=6 * chips * src_count * tgt_count,
                bytes_accessed=2**20,
                transcendentals=chips * src_count * tgt_count,
            ),
            name="columns",
        )(near_z, far_z, lse, lines[0], lines[1], *more)

    (pair_part,) = columns(pair_kernel, pair_z, pair_far_z)
    lse, pair_part = lax.optimization_barrier((lse, pair_part))
    home = pair(pair_part)
    own_part, src_potential = columns(own_kernel, own_z, own_far_z, src_sum)
    total = merge(own_part, home).reshape(tgt_count)
    tgt_update = tgt_exponent * (2.0 * tgt_logmass + tgt_potential - total)
    return (src_potential.reshape(src_count), tgt_update)


def solution(mesh):
    placed = (
        P(("groups", "blk"), None),
        P(("groups", "blk", "tsplit"), None),
        P(("groups", "blk", "tsplit")),
        P(("groups", "blk")),
        P(("groups", "blk", "tsplit")),
        P(("groups", "blk")),
        P(("groups", "blk", "tsplit")),
    )
    return jax.shard_map(
        shards,
        mesh=mesh,
        in_specs=placed,
        out_specs=(P(("groups", "blk")), P(("groups", "blk", "tsplit"))),
        check_vma=False,
    )
```

```python
import functools
import math

import jax
import jax.numpy as jnp
from jax import lax
from jax.experimental import pallas as pl
from jax.experimental.pallas import tpu as pltpu
from jax.sharding import PartitionSpec as P

EPSILON = 0.5
LOGIT_SCALE = 2.0 / EPSILON
LOG2_E = math.log2(math.e)
LOG_2 = math.log(2.0)
LANES = 128
CHUNK = 256
PIECE = 512
VMEM = pl.BlockSpec(memory_space=pltpu.VMEM)
SMEM = pl.BlockSpec(memory_space=pltpu.SMEM)
HBM = pl.BlockSpec(memory_space=pltpu.HBM)
NT_DIMS = (((1,), (1,)), ((), ()))


def diagonal():
    rows = lax.broadcasted_iota(jnp.int32, (LANES, LANES), 0)
    cols = lax.broadcasted_iota(jnp.int32, (LANES, LANES), 1)
    return rows == cols


def to_lanes(column, eye):
    return jnp.sum(jnp.where(eye, column, 0.0), axis=0, keepdims=True)


def to_column(lanes, eye):
    return jnp.sum(jnp.where(eye, lanes, 0.0), axis=1, keepdims=True)


def merge(*parts):
    peak = functools.reduce(jnp.maximum, parts)
    return peak + jnp.log(sum(jnp.exp(part - peak) for part in parts))


def squares(rows_ref, at):
    rows = rows_ref[at : at + LANES, :].astype(jnp.float32)
    return jnp.sum(rows * rows, axis=1, keepdims=True) / EPSILON


def row_sums(rows, sides, z_ref):
    rows = rows * LOGIT_SCALE
    pieces = [(side, at) for side, (tgt_ref, _) in enumerate(sides) for at in range(0, tgt_ref.shape[0], PIECE)]

    def product(index):
        side, at = pieces[index]
        part = sides[side][0][at : at + PIECE, :]
        z_ref[index % 2] = lax.dot_general(part, rows, NT_DIMS, preferred_element_type=jnp.float32)

    def absorb(index, state):
        side, at = pieces[index]
        for inner in range(0, PIECE, LANES):
            offset = sides[side][1][at + inner : at + inner + LANES, :]
            offset = jnp.concatenate([offset] * (rows.shape[0] // LANES), axis=1)
            z = z_ref[index % 2, inner : inner + LANES, :] * LOG2_E + offset
            z = z.reshape(LANES // 8, 8, rows.shape[0])
            high = jnp.max(z, axis=0)
            peak = high if state is None else jnp.maximum(state[0], high)
            mass = jnp.sum(jnp.exp2(z - peak), axis=0)
            if state is not None:
                mass = mass + state[1] * jnp.exp2(state[0] - peak)
            state = (peak, mass)
        return state

    state = None
    product(0)
    for index in range(len(pieces)):
        if index + 1 < len(pieces):
            product(index + 1)
        state = absorb(index, state)
    high, mass = state
    peak = jnp.max(high, axis=0, keepdims=True)
    mass = jnp.sum(mass * jnp.exp2(high - peak), axis=0, keepdims=True)
    return peak * LOG_2 + jnp.log(mass)


def put_offsets(offset_ref, column_ref, eye):
    for at in range(0, offset_ref.shape[1], LANES):
        column = to_column(offset_ref[:, at : at + LANES] * LOG2_E, eye)
        column_ref[at : at + LANES, :] = jnp.broadcast_to(column, (LANES, LANES))


def logits_kernel(rows_ref, own_ref, own_offset_ref, pair_ref, pair_offset_ref, own_z_ref, pair_z_ref):
    rows = rows_ref[...] * LOGIT_SCALE
    for tgt_ref, offset_ref, z_ref in ((own_ref, own_offset_ref, own_z_ref), (pair_ref, pair_offset_ref, pair_z_ref)):
        for at in range(0, tgt_ref.shape[0], CHUNK):
            cols = slice(at, at + CHUNK)
            dots = lax.dot_general(rows, tgt_ref[cols, :], NT_DIMS, preferred_element_type=jnp.float32)
            z_ref[:, cols] = (dots + offset_ref[:, cols]) * LOG2_E


def prepare_kernel(turn, core_ref, *refs):
    inputs, refs = refs[:6], refs[6:]
    earlier, refs = refs[: 6 * (1 - turn)], refs[6 * (1 - turn) :]
    outs, scratch = refs[:6], refs[6:]

    @pl.when(core_ref[0] == turn)
    def work():
        prepare(*inputs, *outs, *scratch)

    if earlier:

        @pl.when(core_ref[0] != turn)
        def hand_on():
            for source, target in zip(earlier, outs):
                target[...] = source[...]


def prepare(
    src_hbm, tgt_hbm, pot_hbm, mass_hbm, slope_hbm, logmass_hbm,
    tgt_ref, offset_ref, column_ref, lse_ref, line_ref, sum_ref,
    src_ref, pot_ref, mass_ref, slope_ref, logmass_ref, z_ref, sems,
):
    pairs = (
        (tgt_hbm, tgt_ref), (src_hbm, src_ref), (pot_hbm, pot_ref),
        (mass_hbm, mass_ref), (slope_hbm, slope_ref), (logmass_hbm, logmass_ref),
    )
    copies = [pltpu.make_async_copy(source, target, sems.at[at]) for at, (source, target) in enumerate(pairs)]
    for copy in copies:
        copy.start()
    for copy in copies[1:]:
        copy.wait()
    eye = diagonal()
    for group in range(src_ref.shape[0] // LANES):
        cols = slice(group * LANES, (group + 1) * LANES)
        square = to_lanes(squares(src_ref, group * LANES), eye)
        slope = slope_ref[group : group + 1, :]
        logmass = logmass_ref[group : group + 1, :]
        sum_ref[:, cols] = logmass + square
        line_ref[0:1, cols] = slope
        line_ref[1:2, cols] = slope * (logmass + square) + (logmass - square)
    copies[0].wait()
    for group in range(tgt_ref.shape[0] // LANES):
        at = group * LANES
        base = pot_ref[group : group + 1, :] + mass_ref[group : group + 1, :]
        offset_ref[:, at : at + LANES] = base - to_lanes(squares(tgt_ref, at), eye)
    put_offsets(offset_ref, column_ref, eye)
    lse_ref[...] = row_sums(src_ref[...], ((tgt_ref, column_ref),), z_ref)


def near_kernel(rows_ref, tgt_ref, offset_ref, held_ref, column_ref, lse_ref, z_ref):
    put_offsets(offset_ref, column_ref, diagonal())
    lse_ref[...] = merge(held_ref[...], row_sums(rows_ref[...], ((tgt_ref, column_ref),), z_ref))


def far_kernel(count, *refs):
    own_ref, own_column_ref, pair_ref, pair_column_ref, held_ref, line_ref = refs[count : count + 6]
    out_ref, z_ref = refs[count + 6 :]
    slots = count + 1
    out_ref[0:1, :] = held_ref[...]
    out_ref[slots : slots + 2, :] = line_ref[...]
    for slot in range(count):
        sides = ((own_ref, own_column_ref), (pair_ref, pair_column_ref))
        out_ref[slot + 1 : slot + 2, :] = row_sums(refs[slot][...], sides, z_ref)


def sum_columns(z_refs, offset, off_ref, out_ref):
    eye = diagonal()
    slots, src_count = offset.shape
    for slot in range(slots):
        for at in range(0, src_count, LANES):
            column = to_column(offset[slot : slot + 1, at : at + LANES] * LOG2_E, eye)
            off_ref[slot, at : at + LANES, :] = jnp.broadcast_to(column, (LANES, LANES))

    for group in range(out_ref.shape[0]):
        cols = slice(group * LANES, (group + 1) * LANES)
        peaks, masses = [], []
        for slot in range(slots):
            z = (z_refs[slot][:, cols] + off_ref[slot]).reshape(src_count // 8, 8, LANES)
            peaks.append(jnp.max(z, axis=0))
            masses.append(jnp.sum(jnp.exp2(z - peaks[-1]), axis=0))
        peak = jnp.max(functools.reduce(jnp.maximum, peaks), axis=0, keepdims=True)
        mass = sum(mass * jnp.exp2(high - peak) for high, mass in zip(peaks, masses))
        mass = jnp.sum(mass, axis=0, keepdims=True)
        out_ref[group : group + 1, :] = peak * LOG_2 + jnp.log(mass)


def pair_kernel(slots, *refs):
    lse_ref, slope_ref, shift_ref, out_ref, off_ref = refs[slots:]
    sum_columns(refs[:slots], shift_ref[...] - slope_ref[...] * lse_ref[...], off_ref, out_ref)


def own_kernel(slots, *refs):
    lse_ref, slope_ref, shift_ref, sum_ref, out_ref, potential_ref, off_ref = refs[slots:]
    lse, slope = lse_ref[...], slope_ref[...]
    potential_ref[...] = slope[0:1, :] * (sum_ref[...] - lse[0:1, :])
    sum_columns(refs[:slots], shift_ref[...] - slope * lse, off_ref, out_ref)


def f32(*shape):
    return jax.ShapeDtypeStruct(shape, jnp.float32)


def params(mebibytes):
    return pltpu.CompilerParams(vmem_limit_bytes=mebibytes * 1024 * 1024)


def shards(sources, targets, tgt_potential, src_logmass, tgt_logmass, src_exponent, tgt_exponent):
    src_count, width = sources.shape
    tgt_count = targets.shape[0]
    slabs = lax.axis_size("blk")
    sets = lax.axis_size("tsplit")
    chips = slabs // 2
    far = chips - 1
    groups = tgt_count // LANES
    src_groups = src_count // LANES
    assert chips > 1 and sets > 1 and chips & (chips - 1) == 0 and sets & (sets - 1) == 0

    def pair(value):
        return lax.ppermute(value, "blk", [(i, i ^ 1) for i in range(slabs)])

    def across(value, chip):
        return lax.ppermute(value, "blk", [(i, i ^ (2 * chip)) for i in range(slabs)])

    def along(value, step):
        return lax.ppermute(value, "tsplit", [(i, i ^ step) for i in range(sets)])

    def cost(blocks):
        pairs = blocks * src_count * tgt_count
        return pl.CostEstimate(flops=2 * pairs * width, bytes_accessed=2**20, transcendentals=pairs)

    core = lax.axis_index("blk") & 1
    core_word = core.astype(jnp.int32).reshape(1)
    pair_targets = pair(targets)
    inputs = (
        sources,
        targets,
        tgt_potential.reshape(groups, LANES),
        tgt_logmass.reshape(groups, LANES),
        src_exponent.reshape(src_groups, LANES),
        src_logmass.reshape(src_groups, LANES),
    )
    inputs = [pltpu.with_memory_space_constraint(x, pltpu.HBM) for x in inputs]

    product_space = pltpu.VMEM((2, PIECE, src_count), jnp.float32)

    def prepare_on(turn, *earlier):
        return pl.pallas_call(
            functools.partial(prepare_kernel, turn),
            out_shape=(
                jax.ShapeDtypeStruct(targets.shape, targets.dtype),
                f32(1, tgt_count),
                f32(tgt_count, LANES),
                f32(1, src_count),
                f32(2, src_count),
                f32(1, src_count),
            ),
            in_specs=[SMEM] + [HBM] * 6 + [VMEM] * len(earlier),
            out_specs=(VMEM,) * 6,
            scratch_shapes=[pltpu.VMEM(x.shape, x.dtype) for x in (inputs[0], *inputs[2:])]
            + [product_space, pltpu.SemaphoreType.DMA((6,))],
            compiler_params=params(12),
            cost_estimate=cost(1),
            name=f"prepare_{turn}",
        )(core_word, *inputs, *earlier)

    earlier = prepare_on(1)
    first, sent = lax.optimization_barrier((earlier[5], sources))
    far_blocks = [across(sent, chip) for chip in range(1, chips)]
    held, offset, column, lse, line, src_sum = prepare_on(0, *earlier[:5], first)
    pair_offset = pair(offset)
    pair_column, lse = pl.pallas_call(
        near_kernel,
        out_shape=(f32(tgt_count, LANES), f32(1, src_count)),
        in_specs=[VMEM] * 4,
        out_specs=(VMEM,) * 2,
        scratch_shapes=[product_space],
        compiler_params=params(12),
        cost_estimate=cost(1),
        name="near_rows",
    )(sources, pair_targets, pair_offset, lse)
    far_lines = [across(line, chip) for chip in range(2, chips)]
    lse, *moved = lax.optimization_barrier((lse, *far_blocks, *far_lines))
    payload = pl.pallas_call(
        functools.partial(far_kernel, far),
        out_shape=f32(chips + 2, src_count),
        in_specs=[VMEM] * (far + 6),
        out_specs=VMEM,
        scratch_shapes=[product_space],
        compiler_params=params(12 + far),
        cost_estimate=cost(2 * far),
        name="far_rows",
    )(*moved[:far], held, column, pair_targets, pair_column, lse, line)

    payload, *blocks = lax.optimization_barrier((payload, sources, *moved[:far]))
    own_zs, pair_zs = [], []
    for block in blocks:
        own_z, pair_z = pl.pallas_call(
            logits_kernel,
            out_shape=(f32(src_count, tgt_count), f32(src_count, tgt_count)),
            in_specs=[VMEM] * 5,
            out_specs=(VMEM,) * 2,
            compiler_params=params(12),
            cost_estimate=cost(2),
            name="logits",
        )(block, held, offset, pair_targets, pair_offset)
        own_zs.append(own_z)
        pair_zs.append(pair_z)

    def mirror(value, chip):
        return jnp.stack([value[slot ^ chip] for slot in range(chips)])

    joined = lax.ppermute(
        payload,
        ("blk", "tsplit"),
        [(b * sets + z, (b ^ 2) * sets + (z ^ 1)) for b in range(slabs) for z in range(sets)],
    )
    beside = along(payload, 1)
    other = across(payload, 1)
    lines = jnp.stack([line, other[chips:]] + moved[far:], axis=1)
    lse = merge(payload[:chips], mirror(joined, 1), beside[:chips], mirror(other, 1))
    chip = 2
    while chip < chips:
        lse = merge(lse, mirror(across(lse, chip), chip))
        chip *= 2
    step = 2
    while step < sets:
        lse = merge(lse, along(lse, step))
        step *= 2

    def columns(kernel, zs, *more):
        outs = (f32(groups, LANES), f32(1, src_count))[: 1 + len(more)]
        return pl.pallas_call(
            functools.partial(kernel, chips),
            out_shape=outs,
            in_specs=[VMEM] * (chips + 3 + len(more)),
            out_specs=(VMEM,) * len(outs),
            scratch_shapes=[pltpu.VMEM((chips, src_count, LANES), jnp.float32)],
            compiler_params=params(8 + 2 * chips),
            cost_estimate=pl.CostEstimate(
                flops=6 * chips * src_count * tgt_count,
                bytes_accessed=2**20,
                transcendentals=chips * src_count * tgt_count,
            ),
            name="columns",
        )(*zs, lse, lines[0], lines[1], *more)

    (pair_part,) = columns(pair_kernel, pair_zs)
    lse, pair_part = lax.optimization_barrier((lse, pair_part))
    home = pair(pair_part)
    own_part, src_potential = columns(own_kernel, own_zs, src_sum)
    total = merge(own_part, home).reshape(tgt_count)
    tgt_update = tgt_exponent * (2.0 * tgt_logmass + tgt_potential - total)
    return (src_potential.reshape(src_count), tgt_update)


def solution(mesh):
    placed = (
        P(("groups", "blk"), None),
        P(("groups", "blk", "tsplit"), None),
        P(("groups", "blk", "tsplit")),
        P(("groups", "blk")),
        P(("groups", "blk", "tsplit")),
        P(("groups", "blk")),
        P(("groups", "blk", "tsplit")),
    )
    return jax.shard_map(
        shards,
        mesh=mesh,
        in_specs=placed,
        out_specs=(P(("groups", "blk")), P(("groups", "blk", "tsplit"))),
        check_vma=False,
    )
```

```python
import functools
import math

import jax
import jax.numpy as jnp
from jax import lax
from jax.experimental import pallas as pl
from jax.experimental.pallas import tpu as pltpu
from jax.sharding import PartitionSpec as P

EPSILON = 0.5
LOGIT_SCALE = 2.0 / EPSILON
LOG2_E = math.log2(math.e)
LOG_2 = math.log(2.0)
LANES = 128
CHUNK = 256
PIECE = 512
VMEM = pl.BlockSpec(memory_space=pltpu.VMEM)
SMEM = pl.BlockSpec(memory_space=pltpu.SMEM)
HBM = pl.BlockSpec(memory_space=pltpu.HBM)
NT_DIMS = (((1,), (1,)), ((), ()))


def diagonal():
    rows = lax.broadcasted_iota(jnp.int32, (LANES, LANES), 0)
    cols = lax.broadcasted_iota(jnp.int32, (LANES, LANES), 1)
    return rows == cols


def to_lanes(column, eye):
    return jnp.sum(jnp.where(eye, column, 0.0), axis=0, keepdims=True)


def to_column(lanes, eye):
    return jnp.sum(jnp.where(eye, lanes, 0.0), axis=1, keepdims=True)


def merge(*parts):
    peak = functools.reduce(jnp.maximum, parts)
    return peak + jnp.log(sum(jnp.exp(part - peak) for part in parts))


def squares(rows_ref, at):
    rows = rows_ref[at : at + LANES, :].astype(jnp.float32)
    return jnp.sum(rows * rows, axis=1, keepdims=True) / EPSILON


def row_sums(rows, sides, z_ref):
    rows = rows * LOGIT_SCALE
    pieces = [(side, at) for side, (tgt_ref, _) in enumerate(sides) for at in range(0, tgt_ref.shape[0], PIECE)]

    def product(index):
        side, at = pieces[index]
        part = sides[side][0][at : at + PIECE, :]
        z_ref[index % 2] = lax.dot_general(part, rows, NT_DIMS, preferred_element_type=jnp.float32)

    def absorb(index, state):
        side, at = pieces[index]
        for inner in range(0, PIECE, LANES):
            offset = sides[side][1][at + inner : at + inner + LANES, :]
            offset = jnp.concatenate([offset] * (rows.shape[0] // LANES), axis=1)
            z = z_ref[index % 2, inner : inner + LANES, :] * LOG2_E + offset
            z = z.reshape(LANES // 8, 8, rows.shape[0])
            high = jnp.max(z, axis=0)
            peak = high if state is None else jnp.maximum(state[0], high)
            mass = jnp.sum(jnp.exp2(z - peak), axis=0)
            if state is not None:
                mass = mass + state[1] * jnp.exp2(state[0] - peak)
            state = (peak, mass)
        return state

    state = None
    product(0)
    for index in range(len(pieces)):
        if index + 1 < len(pieces):
            product(index + 1)
        state = absorb(index, state)
    high, mass = state
    peak = jnp.max(high, axis=0, keepdims=True)
    mass = jnp.sum(mass * jnp.exp2(high - peak), axis=0, keepdims=True)
    return peak * LOG_2 + jnp.log(mass)


def put_offsets(offset_ref, column_ref, eye):
    for at in range(0, offset_ref.shape[1], LANES):
        column = to_column(offset_ref[:, at : at + LANES] * LOG2_E, eye)
        column_ref[at : at + LANES, :] = jnp.broadcast_to(column, (LANES, LANES))


def logits_kernel(rows_ref, own_ref, own_offset_ref, pair_ref, pair_offset_ref, own_z_ref, pair_z_ref):
    rows = rows_ref[...] * LOGIT_SCALE
    for tgt_ref, offset_ref, z_ref in ((own_ref, own_offset_ref, own_z_ref), (pair_ref, pair_offset_ref, pair_z_ref)):
        for at in range(0, tgt_ref.shape[0], CHUNK):
            cols = slice(at, at + CHUNK)
            dots = lax.dot_general(rows, tgt_ref[cols, :], NT_DIMS, preferred_element_type=jnp.float32)
            z_ref[:, cols] = (dots + offset_ref[:, cols]) * LOG2_E


def prepare_kernel(turn, core_ref, *refs):
    inputs, refs = refs[:6], refs[6:]
    earlier, refs = refs[: 6 * (1 - turn)], refs[6 * (1 - turn) :]
    outs, scratch = refs[:6], refs[6:]

    @pl.when(core_ref[0] == turn)
    def work():
        prepare(*inputs, *outs, *scratch)

    if earlier:

        @pl.when(core_ref[0] != turn)
        def hand_on():
            for source, target in zip(earlier, outs):
                target[...] = source[...]


def prepare(
    src_hbm, tgt_hbm, pot_hbm, mass_hbm, slope_hbm, logmass_hbm,
    tgt_ref, offset_ref, column_ref, lse_ref, line_ref, sum_ref,
    src_ref, pot_ref, mass_ref, slope_ref, logmass_ref, z_ref, sems,
):
    pairs = (
        (tgt_hbm, tgt_ref), (src_hbm, src_ref), (pot_hbm, pot_ref),
        (mass_hbm, mass_ref), (slope_hbm, slope_ref), (logmass_hbm, logmass_ref),
    )
    copies = [pltpu.make_async_copy(source, target, sems.at[at]) for at, (source, target) in enumerate(pairs)]
    for copy in copies:
        copy.start()
    for copy in copies[1:]:
        copy.wait()
    eye = diagonal()
    for group in range(src_ref.shape[0] // LANES):
        cols = slice(group * LANES, (group + 1) * LANES)
        square = to_lanes(squares(src_ref, group * LANES), eye)
        slope = slope_ref[group : group + 1, :]
        logmass = logmass_ref[group : group + 1, :]
        sum_ref[:, cols] = logmass + square
        line_ref[0:1, cols] = slope
        line_ref[1:2, cols] = slope * (logmass + square) + (logmass - square)
    copies[0].wait()
    for group in range(tgt_ref.shape[0] // LANES):
        at = group * LANES
        base = pot_ref[group : group + 1, :] + mass_ref[group : group + 1, :]
        offset_ref[:, at : at + LANES] = base - to_lanes(squares(tgt_ref, at), eye)
    put_offsets(offset_ref, column_ref, eye)
    lse_ref[...] = row_sums(src_ref[...], ((tgt_ref, column_ref),), z_ref)


def far_kernel(count, *refs):
    own_ref, column_ref, out_ref, z_ref = refs[count:]
    for slot in range(count):
        out_ref[slot : slot + 1, :] = row_sums(refs[slot][...], ((own_ref, column_ref),), z_ref)


def pair_rows_kernel(count, *refs):
    blocks, refs = refs[:count], refs[count:]
    src_hbm, tgt_ref, offset_ref, near_ref, far_ref, line_ref, out_ref, src_ref, column_ref, z_ref, sem = refs
    copy = pltpu.make_async_copy(src_hbm, src_ref, sem)
    copy.start()
    put_offsets(offset_ref, column_ref, diagonal())
    slots = count + 1
    out_ref[slots : slots + 2, :] = line_ref[...]
    sides = ((tgt_ref, column_ref),)
    for slot in range(count):
        held = far_ref[slot : slot + 1, :]
        out_ref[slot + 1 : slot + 2, :] = merge(held, row_sums(blocks[slot][...], sides, z_ref))
    copy.wait()
    out_ref[0:1, :] = merge(near_ref[...], row_sums(src_ref[...], sides, z_ref))


def sum_columns(z_refs, offset, off_ref, out_ref):
    eye = diagonal()
    slots, src_count = offset.shape
    for slot in range(slots):
        for at in range(0, src_count, LANES):
            column = to_column(offset[slot : slot + 1, at : at + LANES] * LOG2_E, eye)
            off_ref[slot, at : at + LANES, :] = jnp.broadcast_to(column, (LANES, LANES))

    for group in range(out_ref.shape[0]):
        cols = slice(group * LANES, (group + 1) * LANES)
        peaks, masses = [], []
        for slot in range(slots):
            z = (z_refs[slot][:, cols] + off_ref[slot]).reshape(src_count // 8, 8, LANES)
            peaks.append(jnp.max(z, axis=0))
            masses.append(jnp.sum(jnp.exp2(z - peaks[-1]), axis=0))
        peak = jnp.max(functools.reduce(jnp.maximum, peaks), axis=0, keepdims=True)
        mass = sum(mass * jnp.exp2(high - peak) for high, mass in zip(peaks, masses))
        mass = jnp.sum(mass, axis=0, keepdims=True)
        out_ref[group : group + 1, :] = peak * LOG_2 + jnp.log(mass)


def pair_kernel(slots, *refs):
    lse_ref, slope_ref, shift_ref, out_ref, off_ref = refs[slots:]
    sum_columns(refs[:slots], shift_ref[...] - slope_ref[...] * lse_ref[...], off_ref, out_ref)


def own_kernel(slots, *refs):
    lse_ref, slope_ref, shift_ref, sum_ref, out_ref, potential_ref, off_ref = refs[slots:]
    lse, slope = lse_ref[...], slope_ref[...]
    potential_ref[...] = slope[0:1, :] * (sum_ref[...] - lse[0:1, :])
    sum_columns(refs[:slots], shift_ref[...] - slope * lse, off_ref, out_ref)


def f32(*shape):
    return jax.ShapeDtypeStruct(shape, jnp.float32)


def params(mebibytes):
    return pltpu.CompilerParams(vmem_limit_bytes=mebibytes * 1024 * 1024)


def shards(sources, targets, tgt_potential, src_logmass, tgt_logmass, src_exponent, tgt_exponent):
    src_count, width = sources.shape
    tgt_count = targets.shape[0]
    slabs = lax.axis_size("blk")
    sets = lax.axis_size("tsplit")
    chips = slabs // 2
    far = chips - 1
    groups = tgt_count // LANES
    src_groups = src_count // LANES
    assert chips > 1 and sets > 1 and chips & (chips - 1) == 0 and sets & (sets - 1) == 0

    def pair(value):
        return lax.ppermute(value, "blk", [(i, i ^ 1) for i in range(slabs)])

    def across(value, chip):
        return lax.ppermute(value, "blk", [(i, i ^ (2 * chip)) for i in range(slabs)])

    def along(value, step):
        return lax.ppermute(value, "tsplit", [(i, i ^ step) for i in range(sets)])

    def cost(blocks):
        pairs = blocks * src_count * tgt_count
        return pl.CostEstimate(flops=2 * pairs * width, bytes_accessed=2**20, transcendentals=pairs)

    core = lax.axis_index("blk") & 1
    core_word = core.astype(jnp.int32).reshape(1)
    inputs = (
        sources,
        targets,
        tgt_potential.reshape(groups, LANES),
        tgt_logmass.reshape(groups, LANES),
        src_exponent.reshape(src_groups, LANES),
        src_logmass.reshape(src_groups, LANES),
    )
    inputs = [pltpu.with_memory_space_constraint(x, pltpu.HBM) for x in inputs]

    product_space = pltpu.VMEM((2, PIECE, src_count), jnp.float32)

    def prepare_on(turn, *earlier):
        return pl.pallas_call(
            functools.partial(prepare_kernel, turn),
            out_shape=(
                jax.ShapeDtypeStruct(targets.shape, targets.dtype),
                f32(1, tgt_count),
                f32(tgt_count, LANES),
                f32(1, src_count),
                f32(2, src_count),
                f32(1, src_count),
            ),
            in_specs=[SMEM] + [HBM] * 6 + [VMEM] * len(earlier),
            out_specs=(VMEM,) * 6,
            scratch_shapes=[pltpu.VMEM(x.shape, x.dtype) for x in (inputs[0], *inputs[2:])]
            + [product_space, pltpu.SemaphoreType.DMA((6,))],
            compiler_params=params(12),
            cost_estimate=cost(1),
            name=f"prepare_{turn}",
        )(core_word, *inputs, *earlier)

    earlier = prepare_on(1)
    first, sent = lax.optimization_barrier((earlier[5], sources))
    far_blocks = [across(sent, chip) for chip in range(1, chips)]
    held, offset, column, lse, line, src_sum = prepare_on(0, *earlier[:5], first)
    pair_offset = pair(offset)
    pair_targets = pair(held)
    far_lines = [across(line, chip) for chip in range(2, chips)]
    far_own = pl.pallas_call(
        functools.partial(far_kernel, far),
        out_shape=f32(far, src_count),
        in_specs=[VMEM] * (far + 2),
        out_specs=VMEM,
        scratch_shapes=[product_space],
        compiler_params=params(12 + far),
        cost_estimate=cost(100 * far),
        name="far_own_rows",
    )(*far_blocks, held, column)
    far_own, pair_targets, pair_offset = lax.optimization_barrier((far_own, pair_targets, pair_offset))
    payload, held_sources = pl.pallas_call(
        functools.partial(pair_rows_kernel, far),
        out_shape=(f32(chips + 2, src_count), jax.ShapeDtypeStruct(sources.shape, sources.dtype)),
        in_specs=[VMEM] * far + [HBM] + [VMEM] * 5,
        out_specs=(VMEM,) * 2,
        scratch_shapes=[pltpu.VMEM((tgt_count, LANES), jnp.float32), product_space, pltpu.SemaphoreType.DMA(())],
        compiler_params=params(12 + far),
        cost_estimate=cost(chips),
        name="pair_rows",
    )(*far_blocks, inputs[0], pair_targets, pair_offset, lse, far_own, line)

    payload, *blocks = lax.optimization_barrier((payload, held_sources, *far_blocks))
    own_zs, pair_zs = [], []
    for block in blocks:
        own_z, pair_z = pl.pallas_call(
            logits_kernel,
            out_shape=(f32(src_count, tgt_count), f32(src_count, tgt_count)),
            in_specs=[VMEM] * 5,
            out_specs=(VMEM,) * 2,
            compiler_params=params(12),
            cost_estimate=cost(2),
            name="logits",
        )(block, held, offset, pair_targets, pair_offset)
        own_zs.append(own_z)
        pair_zs.append(pair_z)

    def mirror(value, chip):
        return jnp.stack([value[slot ^ chip] for slot in range(chips)])

    joined = lax.ppermute(
        payload,
        ("blk", "tsplit"),
        [(b * sets + z, (b ^ 2) * sets + (z ^ 1)) for b in range(slabs) for z in range(sets)],
    )
    beside = along(payload, 1)
    other = across(payload, 1)
    lines = jnp.stack([line, other[chips:]] + far_lines, axis=1)
    lse = merge(payload[:chips], mirror(joined, 1), beside[:chips], mirror(other, 1))
    chip = 2
    while chip < chips:
        lse = merge(lse, mirror(across(lse, chip), chip))
        chip *= 2
    step = 2
    while step < sets:
        lse = merge(lse, along(lse, step))
        step *= 2

    def columns(kernel, zs, *more):
        outs = (f32(groups, LANES), f32(1, src_count))[: 1 + len(more)]
        return pl.pallas_call(
            functools.partial(kernel, chips),
            out_shape=outs,
            in_specs=[VMEM] * (chips + 3 + len(more)),
            out_specs=(VMEM,) * len(outs),
            scratch_shapes=[pltpu.VMEM((chips, src_count, LANES), jnp.float32)],
            compiler_params=params(8 + 2 * chips),
            cost_estimate=pl.CostEstimate(
                flops=6 * chips * src_count * tgt_count,
                bytes_accessed=2**20,
                transcendentals=chips * src_count * tgt_count,
            ),
            name="columns",
        )(*zs, lse, lines[0], lines[1], *more)

    (pair_part,) = columns(pair_kernel, pair_zs)
    lse, pair_part = lax.optimization_barrier((lse, pair_part))
    home = pair(pair_part)
    own_part, src_potential = columns(own_kernel, own_zs, src_sum)
    total = merge(own_part, home).reshape(tgt_count)
    tgt_update = tgt_exponent * (2.0 * tgt_logmass + tgt_potential - total)
    return (src_potential.reshape(src_count), tgt_update)


def solution(mesh):
    placed = (
        P(("groups", "blk"), None),
        P(("groups", "blk", "tsplit"), None),
        P(("groups", "blk", "tsplit")),
        P(("groups", "blk")),
        P(("groups", "blk", "tsplit")),
        P(("groups", "blk")),
        P(("groups", "blk", "tsplit")),
    )
    return jax.shard_map(
        shards,
        mesh=mesh,
        in_specs=placed,
        out_specs=(P(("groups", "blk")), P(("groups", "blk", "tsplit"))),
        check_vma=False,
    )
```

```python
import functools
import math

import jax
import jax.numpy as jnp
from jax import lax
from jax.experimental import pallas as pl
from jax.experimental.pallas import tpu as pltpu
from jax.sharding import PartitionSpec as P

EPSILON = 0.5
LOGIT_SCALE = 2.0 / EPSILON
LOG2_E = math.log2(math.e)
LOG_2 = math.log(2.0)
LANES = 128
CHUNK = 256
PIECE = 512
VMEM = pl.BlockSpec(memory_space=pltpu.VMEM)
SMEM = pl.BlockSpec(memory_space=pltpu.SMEM)
HBM = pl.BlockSpec(memory_space=pltpu.HBM)
NT_DIMS = (((1,), (1,)), ((), ()))


def diagonal():
    rows = lax.broadcasted_iota(jnp.int32, (LANES, LANES), 0)
    cols = lax.broadcasted_iota(jnp.int32, (LANES, LANES), 1)
    return rows == cols


def to_lanes(column, eye):
    return jnp.sum(jnp.where(eye, column, 0.0), axis=0, keepdims=True)


def to_column(lanes, eye):
    return jnp.sum(jnp.where(eye, lanes, 0.0), axis=1, keepdims=True)


def merge(*parts):
    peak = functools.reduce(jnp.maximum, parts)
    return peak + jnp.log(sum(jnp.exp(part - peak) for part in parts))


def squares(rows_ref, at):
    rows = rows_ref[at : at + LANES, :].astype(jnp.float32)
    return jnp.sum(rows * rows, axis=1, keepdims=True) / EPSILON


def row_sums(rows, sides, z_ref):
    rows = rows * LOGIT_SCALE
    pieces = [(side, at) for side, (tgt_ref, _) in enumerate(sides) for at in range(0, tgt_ref.shape[0], PIECE)]

    def product(index):
        side, at = pieces[index]
        part = sides[side][0][at : at + PIECE, :]
        z_ref[index % 2] = lax.dot_general(part, rows, NT_DIMS, preferred_element_type=jnp.float32)

    def absorb(index, state):
        side, at = pieces[index]
        for inner in range(0, PIECE, LANES):
            offset = sides[side][1][at + inner : at + inner + LANES, :]
            offset = jnp.concatenate([offset] * (rows.shape[0] // LANES), axis=1)
            z = z_ref[index % 2, inner : inner + LANES, :] * LOG2_E + offset
            z = z.reshape(LANES // 8, 8, rows.shape[0])
            high = jnp.max(z, axis=0)
            peak = high if state is None else jnp.maximum(state[0], high)
            mass = jnp.sum(jnp.exp2(z - peak), axis=0)
            if state is not None:
                mass = mass + state[1] * jnp.exp2(state[0] - peak)
            state = (peak, mass)
        return state

    state = None
    product(0)
    for index in range(len(pieces)):
        if index + 1 < len(pieces):
            product(index + 1)
        state = absorb(index, state)
    high, mass = state
    peak = jnp.max(high, axis=0, keepdims=True)
    mass = jnp.sum(mass * jnp.exp2(high - peak), axis=0, keepdims=True)
    return peak * LOG_2 + jnp.log(mass)


def put_offsets(offset_ref, column_ref, eye):
    for at in range(0, offset_ref.shape[1], LANES):
        column = to_column(offset_ref[:, at : at + LANES] * LOG2_E, eye)
        column_ref[at : at + LANES, :] = jnp.broadcast_to(column, (LANES, LANES))


def make_logits(rows, tgt_ref, offset_ref, z_ref):
    rows = rows * LOGIT_SCALE
    for at in range(0, tgt_ref.shape[0], CHUNK):
        cols = slice(at, at + CHUNK)
        dots = lax.dot_general(rows, tgt_ref[cols, :], NT_DIMS, preferred_element_type=jnp.float32)
        z_ref[:, cols] = (dots + offset_ref[:, cols]) * LOG2_E


def logits_kernel(sides, rows_ref, *refs):
    for side in range(sides):
        make_logits(rows_ref[...], refs[2 * side], refs[2 * side + 1], refs[2 * sides + side])


def prepare_kernel(turn, core_ref, *refs):
    inputs, refs = refs[:6], refs[6:]
    earlier, refs = refs[: 7 * (1 - turn)], refs[7 * (1 - turn) :]
    outs, scratch = refs[:7], refs[7:]

    @pl.when(core_ref[0] == turn)
    def work():
        prepare(*inputs, *outs, *scratch)

    if earlier:

        @pl.when(core_ref[0] != turn)
        def hand_on():
            for source, target in zip(earlier, outs):
                target[...] = source[...]


def prepare(
    src_hbm, tgt_hbm, pot_hbm, mass_hbm, slope_hbm, logmass_hbm,
    tgt_ref, offset_ref, column_ref, own_z_ref, lse_ref, line_ref, sum_ref,
    src_ref, pot_ref, mass_ref, slope_ref, logmass_ref, z_ref, sems,
):
    pairs = (
        (tgt_hbm, tgt_ref), (src_hbm, src_ref), (pot_hbm, pot_ref),
        (mass_hbm, mass_ref), (slope_hbm, slope_ref), (logmass_hbm, logmass_ref),
    )
    copies = [pltpu.make_async_copy(source, target, sems.at[at]) for at, (source, target) in enumerate(pairs)]
    for copy in copies:
        copy.start()
    for copy in copies[1:]:
        copy.wait()
    eye = diagonal()
    for group in range(src_ref.shape[0] // LANES):
        cols = slice(group * LANES, (group + 1) * LANES)
        square = to_lanes(squares(src_ref, group * LANES), eye)
        slope = slope_ref[group : group + 1, :]
        logmass = logmass_ref[group : group + 1, :]
        sum_ref[:, cols] = logmass + square
        line_ref[0:1, cols] = slope
        line_ref[1:2, cols] = slope * (logmass + square) + (logmass - square)
    copies[0].wait()
    for group in range(tgt_ref.shape[0] // LANES):
        at = group * LANES
        base = pot_ref[group : group + 1, :] + mass_ref[group : group + 1, :]
        offset_ref[:, at : at + LANES] = base - to_lanes(squares(tgt_ref, at), eye)
    put_offsets(offset_ref, column_ref, eye)
    lse_ref[...] = row_sums(src_ref[...], ((tgt_ref, column_ref),), z_ref)
    make_logits(src_ref[...], tgt_ref, offset_ref, own_z_ref)


def near_kernel(rows_ref, tgt_ref, offset_ref, held_ref, column_ref, lse_ref, z_ref):
    put_offsets(offset_ref, column_ref, diagonal())
    lse_ref[...] = merge(held_ref[...], row_sums(rows_ref[...], ((tgt_ref, column_ref),), z_ref))


def far_kernel(count, *refs):
    own_ref, own_column_ref, pair_ref, pair_column_ref, held_ref, line_ref = refs[count : count + 6]
    out_ref, z_ref = refs[count + 6 :]
    slots = count + 1
    out_ref[0:1, :] = held_ref[...]
    out_ref[slots : slots + 2, :] = line_ref[...]
    for slot in range(count):
        sides = ((own_ref, own_column_ref), (pair_ref, pair_column_ref))
        out_ref[slot + 1 : slot + 2, :] = row_sums(refs[slot][...], sides, z_ref)


def sum_columns(z_refs, offset, off_ref, out_ref):
    eye = diagonal()
    slots, src_count = offset.shape
    for slot in range(slots):
        for at in range(0, src_count, LANES):
            column = to_column(offset[slot : slot + 1, at : at + LANES] * LOG2_E, eye)
            off_ref[slot, at : at + LANES, :] = jnp.broadcast_to(column, (LANES, LANES))

    for group in range(out_ref.shape[0]):
        cols = slice(group * LANES, (group + 1) * LANES)
        peaks, masses = [], []
        for slot in range(slots):
            z = (z_refs[slot][:, cols] + off_ref[slot]).reshape(src_count // 8, 8, LANES)
            peaks.append(jnp.max(z, axis=0))
            masses.append(jnp.sum(jnp.exp2(z - peaks[-1]), axis=0))
        peak = jnp.max(functools.reduce(jnp.maximum, peaks), axis=0, keepdims=True)
        mass = sum(mass * jnp.exp2(high - peak) for high, mass in zip(peaks, masses))
        mass = jnp.sum(mass, axis=0, keepdims=True)
        out_ref[group : group + 1, :] = peak * LOG_2 + jnp.log(mass)


def pair_kernel(slots, *refs):
    lse_ref, slope_ref, shift_ref, out_ref, off_ref = refs[slots:]
    sum_columns(refs[:slots], shift_ref[...] - slope_ref[...] * lse_ref[...], off_ref, out_ref)


def own_kernel(slots, *refs):
    lse_ref, slope_ref, shift_ref, sum_ref, out_ref, potential_ref, off_ref = refs[slots:]
    lse, slope = lse_ref[...], slope_ref[...]
    potential_ref[...] = slope[0:1, :] * (sum_ref[...] - lse[0:1, :])
    sum_columns(refs[:slots], shift_ref[...] - slope * lse, off_ref, out_ref)


def f32(*shape):
    return jax.ShapeDtypeStruct(shape, jnp.float32)


def params(mebibytes):
    return pltpu.CompilerParams(vmem_limit_bytes=mebibytes * 1024 * 1024)


def shards(sources, targets, tgt_potential, src_logmass, tgt_logmass, src_exponent, tgt_exponent):
    src_count, width = sources.shape
    tgt_count = targets.shape[0]
    slabs = lax.axis_size("blk")
    sets = lax.axis_size("tsplit")
    chips = slabs // 2
    far = chips - 1
    groups = tgt_count // LANES
    src_groups = src_count // LANES
    assert chips > 1 and sets > 1 and chips & (chips - 1) == 0 and sets & (sets - 1) == 0

    def pair(value):
        return lax.ppermute(value, "blk", [(i, i ^ 1) for i in range(slabs)])

    def across(value, chip):
        return lax.ppermute(value, "blk", [(i, i ^ (2 * chip)) for i in range(slabs)])

    def along(value, step):
        return lax.ppermute(value, "tsplit", [(i, i ^ step) for i in range(sets)])

    def cost(blocks):
        pairs = blocks * src_count * tgt_count
        return pl.CostEstimate(flops=2 * pairs * width, bytes_accessed=2**20, transcendentals=pairs)

    core = lax.axis_index("blk") & 1
    core_word = core.astype(jnp.int32).reshape(1)
    pair_targets = pair(targets)
    inputs = (
        sources,
        targets,
        tgt_potential.reshape(groups, LANES),
        tgt_logmass.reshape(groups, LANES),
        src_exponent.reshape(src_groups, LANES),
        src_logmass.reshape(src_groups, LANES),
    )
    inputs = [pltpu.with_memory_space_constraint(x, pltpu.HBM) for x in inputs]

    product_space = pltpu.VMEM((2, PIECE, src_count), jnp.float32)

    def prepare_on(turn, *earlier):
        return pl.pallas_call(
            functools.partial(prepare_kernel, turn),
            out_shape=(
                jax.ShapeDtypeStruct(targets.shape, targets.dtype),
                f32(1, tgt_count),
                f32(tgt_count, LANES),
                f32(src_count, tgt_count),
                f32(1, src_count),
                f32(2, src_count),
                f32(1, src_count),
            ),
            in_specs=[SMEM] + [HBM] * 6 + [VMEM] * len(earlier),
            out_specs=(VMEM,) * 7,
            scratch_shapes=[pltpu.VMEM(x.shape, x.dtype) for x in (inputs[0], *inputs[2:])]
            + [product_space, pltpu.SemaphoreType.DMA((6,))],
            compiler_params=params(12),
            cost_estimate=cost(1),
            name=f"prepare_{turn}",
        )(core_word, *inputs, *earlier)

    earlier = prepare_on(1)
    first, sent = lax.optimization_barrier((earlier[6], sources))
    far_blocks = [across(sent, chip) for chip in range(1, chips)]
    held, offset, column, own_z, lse, line, src_sum = prepare_on(0, *earlier[:6], first)
    pair_offset = pair(offset)
    pair_column, lse = pl.pallas_call(
        near_kernel,
        out_shape=(f32(tgt_count, LANES), f32(1, src_count)),
        in_specs=[VMEM] * 4,
        out_specs=(VMEM,) * 2,
        scratch_shapes=[product_space],
        compiler_params=params(12),
        cost_estimate=cost(1),
        name="near_rows",
    )(sources, pair_targets, pair_offset, lse)
    far_lines = [across(line, chip) for chip in range(2, chips)]
    lse, *moved = lax.optimization_barrier((lse, *far_blocks, *far_lines))
    payload = pl.pallas_call(
        functools.partial(far_kernel, far),
        out_shape=f32(chips + 2, src_count),
        in_specs=[VMEM] * (far + 6),
        out_specs=VMEM,
        scratch_shapes=[product_space],
        compiler_params=params(12 + far),
        cost_estimate=cost(2 * far),
        name="far_rows",
    )(*moved[:far], held, column, pair_targets, pair_column, lse, line)

    payload, *blocks = lax.optimization_barrier((payload, sources, *moved[:far]))
    def logits(block, *sides):
        return pl.pallas_call(
            functools.partial(logits_kernel, len(sides) // 2),
            out_shape=(f32(src_count, tgt_count),) * (len(sides) // 2),
            in_specs=[VMEM] * (1 + len(sides)),
            out_specs=(VMEM,) * (len(sides) // 2),
            compiler_params=params(12),
            cost_estimate=cost(len(sides) // 2),
            name="logits",
        )(block, *sides)

    own_zs, pair_zs = [own_z], list(logits(blocks[0], pair_targets, pair_offset))
    for block in blocks[1:]:
        own_z, pair_z = logits(block, held, offset, pair_targets, pair_offset)
        own_zs.append(own_z)
        pair_zs.append(pair_z)

    def mirror(value, chip):
        return jnp.stack([value[slot ^ chip] for slot in range(chips)])

    other = across(payload, 1)
    beside = along(payload, 1)
    joined = lax.ppermute(
        payload,
        ("blk", "tsplit"),
        [(b * sets + z, (b ^ 2) * sets + (z ^ 1)) for b in range(slabs) for z in range(sets)],
    )
    lines = jnp.stack([line, other[chips:]] + moved[far:], axis=1)
    lse = merge(payload[:chips], mirror(other, 1), beside[:chips], mirror(joined, 1))
    chip = 2
    while chip < chips:
        lse = merge(lse, mirror(across(lse, chip), chip))
        chip *= 2
    step = 2
    while step < sets:
        lse = merge(lse, along(lse, step))
        step *= 2

    def columns(kernel, zs, *more):
        outs = (f32(groups, LANES), f32(1, src_count))[: 1 + len(more)]
        return pl.pallas_call(
            functools.partial(kernel, chips),
            out_shape=outs,
            in_specs=[VMEM] * (chips + 3 + len(more)),
            out_specs=(VMEM,) * len(outs),
            scratch_shapes=[pltpu.VMEM((chips, src_count, LANES), jnp.float32)],
            compiler_params=params(8 + 2 * chips),
            cost_estimate=pl.CostEstimate(
                flops=6 * chips * src_count * tgt_count,
                bytes_accessed=2**20,
                transcendentals=chips * src_count * tgt_count,
            ),
            name="columns",
        )(*zs, lse, lines[0], lines[1], *more)

    (pair_part,) = columns(pair_kernel, pair_zs)
    lse, pair_part = lax.optimization_barrier((lse, pair_part))
    home = pair(pair_part)
    own_part, src_potential = columns(own_kernel, own_zs, src_sum)
    total = merge(own_part, home).reshape(tgt_count)
    tgt_update = tgt_exponent * (2.0 * tgt_logmass + tgt_potential - total)
    return (src_potential.reshape(src_count), tgt_update)


def solution(mesh):
    placed = (
        P(("groups", "blk"), None),
        P(("groups", "blk", "tsplit"), None),
        P(("groups", "blk", "tsplit")),
        P(("groups", "blk")),
        P(("groups", "blk", "tsplit")),
        P(("groups", "blk")),
        P(("groups", "blk", "tsplit")),
    )
    return jax.shard_map(
        shards,
        mesh=mesh,
        in_specs=placed,
        out_specs=(P(("groups", "blk")), P(("groups", "blk", "tsplit"))),
        check_vma=False,
    )
```

```python
import functools
import math

import jax
import jax.numpy as jnp
from jax import lax
from jax.experimental import pallas as pl
from jax.experimental.pallas import tpu as pltpu
from jax.sharding import PartitionSpec as P

EPSILON = 0.5
LOGIT_SCALE = 2.0 / EPSILON
LOG2_E = math.log2(math.e)
LOG_2 = math.log(2.0)
LANES = 128
CHUNK = 256
PIECE = 512
VMEM = pl.BlockSpec(memory_space=pltpu.VMEM)
SMEM = pl.BlockSpec(memory_space=pltpu.SMEM)
HBM = pl.BlockSpec(memory_space=pltpu.HBM)
NT_DIMS = (((1,), (1,)), ((), ()))


def diagonal():
    rows = lax.broadcasted_iota(jnp.int32, (LANES, LANES), 0)
    cols = lax.broadcasted_iota(jnp.int32, (LANES, LANES), 1)
    return rows == cols


def to_lanes(column, eye):
    return jnp.sum(jnp.where(eye, column, 0.0), axis=0, keepdims=True)


def to_column(lanes, eye):
    return jnp.sum(jnp.where(eye, lanes, 0.0), axis=1, keepdims=True)


def merge(*parts):
    peak = functools.reduce(jnp.maximum, parts)
    return peak + jnp.log(sum(jnp.exp(part - peak) for part in parts))


def squares(rows_ref, at):
    rows = rows_ref[at : at + LANES, :].astype(jnp.float32)
    return jnp.sum(rows * rows, axis=1, keepdims=True) / EPSILON


def row_sums(rows, sides, z_ref):
    rows = rows * LOGIT_SCALE
    pieces = [(side, at) for side, (tgt_ref, _) in enumerate(sides) for at in range(0, tgt_ref.shape[0], PIECE)]

    def product(index):
        side, at = pieces[index]
        part = sides[side][0][at : at + PIECE, :]
        z_ref[index % 2] = lax.dot_general(part, rows, NT_DIMS, preferred_element_type=jnp.float32)

    def absorb(index, state):
        side, at = pieces[index]
        for inner in range(0, PIECE, LANES):
            offset = sides[side][1][at + inner : at + inner + LANES, :]
            offset = jnp.concatenate([offset] * (rows.shape[0] // LANES), axis=1)
            z = z_ref[index % 2, inner : inner + LANES, :] * LOG2_E + offset
            z = z.reshape(LANES // 8, 8, rows.shape[0])
            high = jnp.max(z, axis=0)
            peak = high if state is None else jnp.maximum(state[0], high)
            mass = jnp.sum(jnp.exp2(z - peak), axis=0)
            if state is not None:
                mass = mass + state[1] * jnp.exp2(state[0] - peak)
            state = (peak, mass)
        return state

    state = None
    product(0)
    for index in range(len(pieces)):
        if index + 1 < len(pieces):
            product(index + 1)
        state = absorb(index, state)
    high, mass = state
    peak = jnp.max(high, axis=0, keepdims=True)
    mass = jnp.sum(mass * jnp.exp2(high - peak), axis=0, keepdims=True)
    return peak * LOG_2 + jnp.log(mass)


def put_offsets(offset_ref, column_ref, eye):
    for at in range(0, offset_ref.shape[1], LANES):
        column = to_column(offset_ref[:, at : at + LANES] * LOG2_E, eye)
        column_ref[at : at + LANES, :] = jnp.broadcast_to(column, (LANES, LANES))


def make_logits(rows, tgt_ref, offset_ref, z_ref):
    rows = rows * LOGIT_SCALE
    for at in range(0, tgt_ref.shape[0], CHUNK):
        cols = slice(at, at + CHUNK)
        dots = lax.dot_general(rows, tgt_ref[cols, :], NT_DIMS, preferred_element_type=jnp.float32)
        z_ref[:, cols] = (dots + offset_ref[:, cols]) * LOG2_E


def logits_kernel(sides, rows_ref, *refs):
    for side in range(sides):
        make_logits(rows_ref[...], refs[2 * side], refs[2 * side + 1], refs[2 * sides + side])


def prepare_kernel(turn, word_ref, *refs):
    inputs, refs = refs[:6], refs[6:]
    earlier, refs = refs[: 7 * (1 - turn)], refs[7 * (1 - turn) :]
    outs, scratch = refs[:7], refs[7:]

    @pl.when(word_ref[0] == turn)
    def work():
        prepare(*inputs, *outs, *scratch)

    if earlier:

        @pl.when(word_ref[0] != turn)
        def hand_on():
            for source, target in zip(earlier, outs):
                target[...] = source[...]


def prepare(
    src_hbm, tgt_hbm, pot_hbm, mass_hbm, slope_hbm, logmass_hbm,
    tgt_ref, offset_ref, column_ref, own_z_ref, lse_ref, line_ref, sum_ref,
    src_ref, pot_ref, mass_ref, slope_ref, logmass_ref, z_ref, sems,
):
    pairs = (
        (tgt_hbm, tgt_ref), (src_hbm, src_ref), (pot_hbm, pot_ref),
        (mass_hbm, mass_ref), (slope_hbm, slope_ref), (logmass_hbm, logmass_ref),
    )
    copies = [pltpu.make_async_copy(source, target, sems.at[at]) for at, (source, target) in enumerate(pairs)]
    for copy in copies:
        copy.start()
    for copy in copies[1:]:
        copy.wait()
    eye = diagonal()
    for group in range(src_ref.shape[0] // LANES):
        cols = slice(group * LANES, (group + 1) * LANES)
        square = to_lanes(squares(src_ref, group * LANES), eye)
        slope = slope_ref[group : group + 1, :]
        logmass = logmass_ref[group : group + 1, :]
        sum_ref[:, cols] = logmass + square
        line_ref[0:1, cols] = slope
        line_ref[1:2, cols] = slope * (logmass + square) + (logmass - square)
    copies[0].wait()
    for group in range(tgt_ref.shape[0] // LANES):
        at = group * LANES
        base = pot_ref[group : group + 1, :] + mass_ref[group : group + 1, :]
        offset_ref[:, at : at + LANES] = base - to_lanes(squares(tgt_ref, at), eye)
    put_offsets(offset_ref, column_ref, eye)
    lse_ref[...] = row_sums(src_ref[...], ((tgt_ref, column_ref),), z_ref)
    make_logits(src_ref[...], tgt_ref, offset_ref, own_z_ref)


def near_kernel(rows_ref, tgt_ref, offset_ref, held_ref, line_ref, column_ref, out_ref, z_ref):
    put_offsets(offset_ref, column_ref, diagonal())
    out_ref[0:1, :] = merge(held_ref[...], row_sums(rows_ref[...], ((tgt_ref, column_ref),), z_ref))
    out_ref[1:3, :] = line_ref[...]


def far_kernel(count, *refs):
    own_ref, own_column_ref, pair_ref, pair_column_ref, out_ref, z_ref = refs[count:]
    for slot in range(count):
        sides = ((own_ref, own_column_ref), (pair_ref, pair_column_ref))
        out_ref[slot : slot + 1, :] = row_sums(refs[slot][...], sides, z_ref)


def near_logits_kernel(
    word_ref, own_rows_ref, pair_rows_ref, held_ref, own_ref, own_offset_ref, pair_ref, pair_offset_ref,
    own_z_ref, pair_z_ref,
):
    @pl.when(word_ref[1] == 0)
    def straight():
        own_z_ref[...] = held_ref[...]
        make_logits(own_rows_ref[...], pair_ref, pair_offset_ref, pair_z_ref)

    @pl.when(word_ref[1] != 0)
    def flipped():
        make_logits(pair_rows_ref[...], own_ref, own_offset_ref, own_z_ref)
        make_logits(pair_rows_ref[...], pair_ref, pair_offset_ref, pair_z_ref)


def sum_columns(z_refs, offset, off_ref, out_ref):
    eye = diagonal()
    slots, src_count = offset.shape
    for slot in range(slots):
        for at in range(0, src_count, LANES):
            column = to_column(offset[slot : slot + 1, at : at + LANES] * LOG2_E, eye)
            off_ref[slot, at : at + LANES, :] = jnp.broadcast_to(column, (LANES, LANES))

    for group in range(out_ref.shape[0]):
        cols = slice(group * LANES, (group + 1) * LANES)
        peaks, masses = [], []
        for slot in range(slots):
            z = (z_refs[slot][:, cols] + off_ref[slot]).reshape(src_count // 8, 8, LANES)
            peaks.append(jnp.max(z, axis=0))
            masses.append(jnp.sum(jnp.exp2(z - peaks[-1]), axis=0))
        peak = jnp.max(functools.reduce(jnp.maximum, peaks), axis=0, keepdims=True)
        mass = sum(mass * jnp.exp2(high - peak) for high, mass in zip(peaks, masses))
        mass = jnp.sum(mass, axis=0, keepdims=True)
        out_ref[group : group + 1, :] = peak * LOG_2 + jnp.log(mass)


def pair_kernel(slots, *refs):
    lse_ref, slope_ref, shift_ref, out_ref, off_ref = refs[slots:]
    groups = refs[0].shape[1] // LANES
    sum_columns(refs[:slots], shift_ref[...] - slope_ref[...] * lse_ref[...], off_ref, out_ref.at[:groups])
    for at in range(0, lse_ref.shape[1], LANES):
        row = groups + at // LANES
        out_ref[row : row + 1, :] = lse_ref[0:1, at : at + LANES]


def own_kernel(slots, *refs):
    lse_ref, slope_ref, shift_ref, out_ref, off_ref = refs[slots:]
    sum_columns(refs[:slots], shift_ref[...] - slope_ref[...] * lse_ref[...], off_ref, out_ref)


def final_kernel(
    word_ref, own_ref, home_ref, lse_ref, line_ref, sum_ref, pot_ref, mass_ref, expo_ref, update_ref, potential_ref
):
    groups = own_ref.shape[0]
    total = merge(own_ref[...], home_ref[:groups, :])
    update_ref[...] = expo_ref[...] * (2.0 * mass_ref[...] + pot_ref[...] - total)
    away = jnp.concatenate([home_ref[row : row + 1, :] for row in range(groups, home_ref.shape[0])], axis=1)
    lse = jnp.where(word_ref[1] == 0, lse_ref[0:1, :], away)
    potential_ref[...] = line_ref[0:1, :] * (sum_ref[...] - lse)


def f32(*shape):
    return jax.ShapeDtypeStruct(shape, jnp.float32)


def params(mebibytes):
    return pltpu.CompilerParams(vmem_limit_bytes=mebibytes * 1024 * 1024)


def shards(sources, targets, tgt_potential, src_logmass, tgt_logmass, src_exponent, tgt_exponent):
    src_count, width = sources.shape
    tgt_count = targets.shape[0]
    slabs = lax.axis_size("blk")
    sets = lax.axis_size("tsplit")
    chips = slabs // 2
    far = chips - 1
    groups = tgt_count // LANES
    src_groups = src_count // LANES
    assert chips > 1 and sets > 2 and chips & (chips - 1) == 0 and sets & (sets - 1) == 0

    def pair(value):
        return lax.ppermute(value, "blk", [(i, i ^ 1) for i in range(slabs)])

    def across(value, chip):
        return lax.ppermute(value, "blk", [(i, i ^ (2 * chip)) for i in range(slabs)])

    def along(value, step):
        return lax.ppermute(value, "tsplit", [(i, i ^ step) for i in range(sets)])

    def cost(blocks):
        pairs = blocks * src_count * tgt_count
        return pl.CostEstimate(flops=2 * pairs * width, bytes_accessed=2**20, transcendentals=pairs)

    half = sets // 2
    core = lax.axis_index("blk") & 1
    flip = lax.axis_index("tsplit") // half
    word = jnp.stack([core ^ flip, flip]).astype(jnp.int32)

    def crossed(value, chip, core_flip, step):
        ways = [
            (b * sets + z, (b ^ (2 * chip) ^ core_flip(z)) * sets + (z ^ step))
            for b in range(slabs)
            for z in range(sets)
        ]
        return lax.ppermute(value, ("blk", "tsplit"), ways)

    pair_targets = pair(targets)
    pair_sources = pair(sources)
    potential = tgt_potential.reshape(groups, LANES)
    logmass = tgt_logmass.reshape(groups, LANES)
    exponent = tgt_exponent.reshape(groups, LANES)
    inputs = (
        sources,
        targets,
        potential,
        logmass,
        src_exponent.reshape(src_groups, LANES),
        src_logmass.reshape(src_groups, LANES),
    )
    inputs = [pltpu.with_memory_space_constraint(x, pltpu.HBM) for x in inputs]

    product_space = pltpu.VMEM((2, PIECE, src_count), jnp.float32)

    def prepare_on(turn, *earlier):
        return pl.pallas_call(
            functools.partial(prepare_kernel, turn),
            out_shape=(
                jax.ShapeDtypeStruct(targets.shape, targets.dtype),
                f32(1, tgt_count),
                f32(tgt_count, LANES),
                f32(src_count, tgt_count),
                f32(1, src_count),
                f32(2, src_count),
                f32(1, src_count),
            ),
            in_specs=[SMEM] + [HBM] * 6 + [VMEM] * len(earlier),
            out_specs=(VMEM,) * 7,
            scratch_shapes=[pltpu.VMEM(x.shape, x.dtype) for x in (inputs[0], *inputs[2:])]
            + [product_space, pltpu.SemaphoreType.DMA((6,))],
            compiler_params=params(12),
            cost_estimate=cost(1),
            name=f"prepare_{turn}",
        )(word, *inputs, *earlier)

    earlier = prepare_on(1)
    first, sent = lax.optimization_barrier((earlier[6], sources))
    far_blocks = [crossed(sent, chip, lambda z: z // half, 0) for chip in range(1, chips)]
    held, offset, column, own_z, lse, line, src_sum = prepare_on(0, *earlier[:6], first)
    pair_offset = pair(offset)
    pair_column, near = pl.pallas_call(
        near_kernel,
        out_shape=(f32(tgt_count, LANES), f32(3, src_count)),
        in_specs=[VMEM] * 5,
        out_specs=(VMEM,) * 2,
        scratch_shapes=[product_space],
        compiler_params=params(12),
        cost_estimate=cost(1),
        name="near_rows",
    )(sources, pair_targets, pair_offset, lse, line)
    near_away = pair(near)
    near, *far_blocks = lax.optimization_barrier((near, *far_blocks))
    far_lse = pl.pallas_call(
        functools.partial(far_kernel, far),
        out_shape=f32(far, src_count),
        in_specs=[VMEM] * (far + 4),
        out_specs=VMEM,
        scratch_shapes=[product_space],
        compiler_params=params(12 + far),
        cost_estimate=cost(2 * far),
        name="far_rows",
    )(*far_blocks, held, column, pair_targets, pair_column)
    near = jnp.where(flip == 0, near, near_away)
    payload = jnp.concatenate([near[:1], far_lse, near[1:]])

    payload, pair_sources, *far_blocks = lax.optimization_barrier((payload, pair_sources, *far_blocks))
    def logits(block, *sides):
        return pl.pallas_call(
            functools.partial(logits_kernel, len(sides) // 2),
            out_shape=(f32(src_count, tgt_count),) * (len(sides) // 2),
            in_specs=[VMEM] * (1 + len(sides)),
            out_specs=(VMEM,) * (len(sides) // 2),
            compiler_params=params(12),
            cost_estimate=cost(len(sides) // 2),
            name="logits",
        )(block, *sides)

    zs = [logits(block, held, offset, pair_targets, pair_offset) for block in far_blocks]
    near_zs = pl.pallas_call(
        near_logits_kernel,
        out_shape=(f32(src_count, tgt_count),) * 2,
        in_specs=[SMEM] + [VMEM] * 7,
        out_specs=(VMEM,) * 2,
        compiler_params=params(12),
        cost_estimate=cost(2),
        name="near_logits",
    )(word, sources, pair_sources, own_z, held, offset, pair_targets, pair_offset)
    own_zs, pair_zs = zip(near_zs, *zs)

    def mirror(value, chip):
        return jnp.stack([value[slot ^ chip] for slot in range(chips)])

    other = across(payload, 1)
    beside = along(payload, 1)
    joined = crossed(payload, 1, lambda z: 0, 1)
    far_lines = [across(near[1:], chip) for chip in range(2, chips)]
    lines = jnp.stack([near[1:], other[chips:]] + far_lines, axis=1)
    lse = merge(payload[:chips], mirror(other, 1), beside[:chips], mirror(joined, 1))
    chip = 2
    while chip < chips:
        lse = merge(lse, mirror(across(lse, chip), chip))
        chip *= 2
    step = 2
    while step < half:
        lse = merge(lse, along(lse, step))
        step *= 2
    lse = merge(lse, crossed(lse, 0, lambda z: 1, half))

    def columns(kernel, zs, rows):
        return pl.pallas_call(
            functools.partial(kernel, chips),
            out_shape=f32(rows, LANES),
            in_specs=[VMEM] * (chips + 3),
            out_specs=VMEM,
            scratch_shapes=[pltpu.VMEM((chips, src_count, LANES), jnp.float32)],
            compiler_params=params(8 + 2 * chips),
            cost_estimate=pl.CostEstimate(
                flops=6 * chips * src_count * tgt_count,
                bytes_accessed=2**20,
                transcendentals=chips * src_count * tgt_count,
            ),
            name="columns",
        )(*zs, lse, lines[0], lines[1])

    pair_part = columns(pair_kernel, pair_zs, groups + src_groups)
    lse, pair_part = lax.optimization_barrier((lse, pair_part))
    home = pair(pair_part)
    own_part = columns(own_kernel, own_zs, groups)
    tgt_update, src_potential = pl.pallas_call(
        final_kernel,
        out_shape=(f32(groups, LANES), f32(1, src_count)),
        in_specs=[SMEM] + [VMEM] * 8,
        out_specs=(VMEM,) * 2,
        compiler_params=params(8),
        name="results",
    )(word, own_part, home, lse, line, src_sum, potential, logmass, exponent)
    return (src_potential.reshape(src_count), tgt_update.reshape(tgt_count))


def solution(mesh):
    placed = (
        P(("groups", "blk"), None),
        P(("groups", "blk", "tsplit"), None),
        P(("groups", "blk", "tsplit")),
        P(("groups", "blk")),
        P(("groups", "blk", "tsplit")),
        P(("groups", "blk")),
        P(("groups", "blk", "tsplit")),
    )
    return jax.shard_map(
        shards,
        mesh=mesh,
        in_specs=placed,
        out_specs=(P(("groups", "blk")), P(("groups", "blk", "tsplit"))),
        check_vma=False,
    )
```

```python
import functools
import math

import jax
import jax.numpy as jnp
from jax import lax
from jax.experimental import pallas as pl
from jax.experimental.pallas import tpu as pltpu
from jax.sharding import PartitionSpec as P

EPSILON = 0.5
LOGIT_SCALE = 2.0 / EPSILON
LOG2_E = math.log2(math.e)
LOG_2 = math.log(2.0)
LANES = 128
CHUNK = 256
PIECE = 512
VMEM = pl.BlockSpec(memory_space=pltpu.VMEM)
SMEM = pl.BlockSpec(memory_space=pltpu.SMEM)
HBM = pl.BlockSpec(memory_space=pltpu.HBM)
NT_DIMS = (((1,), (1,)), ((), ()))


def diagonal():
    rows = lax.broadcasted_iota(jnp.int32, (LANES, LANES), 0)
    cols = lax.broadcasted_iota(jnp.int32, (LANES, LANES), 1)
    return rows == cols


def to_lanes(column, eye):
    return jnp.sum(jnp.where(eye, column, 0.0), axis=0, keepdims=True)


def to_column(lanes, eye):
    return jnp.sum(jnp.where(eye, lanes, 0.0), axis=1, keepdims=True)


def merge(*parts):
    peak = functools.reduce(jnp.maximum, parts)
    return peak + jnp.log(sum(jnp.exp(part - peak) for part in parts))


def squares(rows_ref, at):
    rows = rows_ref[at : at + LANES, :].astype(jnp.float32)
    return jnp.sum(rows * rows, axis=1, keepdims=True) / EPSILON


def row_sums(rows, sides, z_ref):
    rows = rows * LOGIT_SCALE
    pieces = [(side, at) for side, (tgt_ref, _) in enumerate(sides) for at in range(0, tgt_ref.shape[0], PIECE)]

    def product(index):
        side, at = pieces[index]
        part = sides[side][0][at : at + PIECE, :]
        z_ref[index % 2] = lax.dot_general(part, rows, NT_DIMS, preferred_element_type=jnp.float32)

    peaks, masses = [], []

    def absorb(index):
        side, at = pieces[index]
        for inner in range(0, PIECE, LANES):
            offset = sides[side][1][at + inner : at + inner + LANES, :]
            offset = jnp.concatenate([offset] * (rows.shape[0] // LANES), axis=1)
            z = z_ref[index % 2, inner : inner + LANES, :] * LOG2_E + offset
            z = z.reshape(LANES // 8, 8, rows.shape[0])
            peaks.append(jnp.max(z, axis=0))
            masses.append(jnp.sum(jnp.exp2(z - peaks[-1]), axis=0))

    product(0)
    for index in range(len(pieces)):
        if index + 1 < len(pieces):
            product(index + 1)
        absorb(index)
    peak = jnp.max(functools.reduce(jnp.maximum, peaks), axis=0, keepdims=True)
    mass = sum(mass * jnp.exp2(high - peak) for high, mass in zip(peaks, masses))
    return peak * LOG_2 + jnp.log(jnp.sum(mass, axis=0, keepdims=True))


def put_offsets(offset_ref, column_ref, eye):
    for at in range(0, offset_ref.shape[1], LANES):
        column = to_column(offset_ref[:, at : at + LANES] * LOG2_E, eye)
        column_ref[at : at + LANES, :] = jnp.broadcast_to(column, (LANES, LANES))


def make_logits(rows, tgt_ref, offset_ref, z_ref):
    rows = rows * LOGIT_SCALE
    for at in range(0, tgt_ref.shape[0], CHUNK):
        cols = slice(at, at + CHUNK)
        dots = lax.dot_general(rows, tgt_ref[cols, :], NT_DIMS, preferred_element_type=jnp.float32)
        z_ref[:, cols] = (dots + offset_ref[:, cols]) * LOG2_E


def logits_kernel(sides, rows_ref, *refs):
    for side in range(sides):
        make_logits(rows_ref[...], refs[2 * side], refs[2 * side + 1], refs[2 * sides + side])


def prepare_kernel(turn, core_ref, *refs):
    inputs, refs = refs[:6], refs[6:]
    earlier, refs = refs[: 7 * (1 - turn)], refs[7 * (1 - turn) :]
    outs, scratch = refs[:7], refs[7:]

    @pl.when(core_ref[0] == turn)
    def work():
        prepare(*inputs, *outs, *scratch)

    if earlier:

        @pl.when(core_ref[0] != turn)
        def hand_on():
            for source, target in zip(earlier, outs):
                target[...] = source[...]


def prepare(
    src_hbm, tgt_hbm, pot_hbm, mass_hbm, slope_hbm, logmass_hbm,
    tgt_ref, offset_ref, column_ref, own_z_ref, lse_ref, line_ref, sum_ref,
    src_ref, pot_ref, mass_ref, slope_ref, logmass_ref, z_ref, sems,
):
    pairs = (
        (tgt_hbm, tgt_ref), (src_hbm, src_ref), (pot_hbm, pot_ref),
        (mass_hbm, mass_ref), (slope_hbm, slope_ref), (logmass_hbm, logmass_ref),
    )
    copies = [pltpu.make_async_copy(source, target, sems.at[at]) for at, (source, target) in enumerate(pairs)]
    for copy in copies:
        copy.start()
    for copy in copies[1:]:
        copy.wait()
    eye = diagonal()
    for group in range(src_ref.shape[0] // LANES):
        cols = slice(group * LANES, (group + 1) * LANES)
        square = to_lanes(squares(src_ref, group * LANES), eye)
        slope = slope_ref[group : group + 1, :]
        logmass = logmass_ref[group : group + 1, :]
        sum_ref[:, cols] = logmass + square
        line_ref[0:1, cols] = slope
        line_ref[1:2, cols] = slope * (logmass + square) + (logmass - square)
    copies[0].wait()
    for group in range(tgt_ref.shape[0] // LANES):
        at = group * LANES
        base = pot_ref[group : group + 1, :] + mass_ref[group : group + 1, :]
        offset_ref[:, at : at + LANES] = base - to_lanes(squares(tgt_ref, at), eye)
    put_offsets(offset_ref, column_ref, eye)
    lse_ref[...] = row_sums(src_ref[...], ((tgt_ref, column_ref),), z_ref)
    make_logits(src_ref[...], tgt_ref, offset_ref, own_z_ref)


def near_kernel(rows_ref, tgt_ref, offset_ref, held_ref, column_ref, lse_ref, z_ref):
    put_offsets(offset_ref, column_ref, diagonal())
    lse_ref[...] = merge(held_ref[...], row_sums(rows_ref[...], ((tgt_ref, column_ref),), z_ref))


def far_kernel(count, *refs):
    own_ref, own_column_ref, pair_ref, pair_column_ref, held_ref, line_ref = refs[count : count + 6]
    out_ref, mirrored_ref, z_ref = refs[count + 6 :]
    slots = count + 1
    for ref in (out_ref, mirrored_ref):
        ref[slots : slots + 2, :] = line_ref[...]
    for slot in range(slots):
        if slot == 0:
            lse = held_ref[...]
        else:
            sides = ((own_ref, own_column_ref), (pair_ref, pair_column_ref))
            lse = row_sums(refs[slot - 1][...], sides, z_ref)
        out_ref[slot : slot + 1, :] = lse
        mirrored_ref[slot ^ 1 : (slot ^ 1) + 1, :] = lse


def sum_columns(z_refs, offset, out_ref, off_ref, peak_ref, mass_ref):
    eye = diagonal()
    slots, src_count = offset.shape
    for slot in range(slots):
        for at in range(0, src_count, LANES):
            column = to_column(offset[slot : slot + 1, at : at + LANES] * LOG2_E, eye)
            off_ref[slot, at : at + LANES, :] = jnp.broadcast_to(column, (LANES, LANES))

    for group in range(out_ref.shape[0]):
        cols = slice(group * LANES, (group + 1) * LANES)
        for slot in range(slots):
            z = (z_refs[slot][:, cols] + off_ref[slot]).reshape(src_count // 8, 8, LANES)
            peak = jnp.max(z, axis=0)
            peak_ref[slot, :, cols] = peak
            mass_ref[slot, :, cols] = jnp.sum(jnp.exp2(z - peak), axis=0)
    peak = jnp.max(functools.reduce(jnp.maximum, [peak_ref[slot] for slot in range(slots)]), axis=0, keepdims=True)
    mass = sum(mass_ref[slot] * jnp.exp2(peak_ref[slot] - peak) for slot in range(slots))
    total = peak * LOG_2 + jnp.log(jnp.sum(mass, axis=0, keepdims=True))
    for group in range(out_ref.shape[0]):
        out_ref[group : group + 1, :] = total[:, group * LANES : (group + 1) * LANES]


def pair_kernel(slots, *refs):
    lse_ref, slope_ref, shift_ref, out_ref, *scratch = refs[slots:]
    sum_columns(refs[:slots], shift_ref[...] - slope_ref[...] * lse_ref[...], out_ref, *scratch)


def own_kernel(turn, slots, *refs):
    z_refs, (lse_ref, slope_ref, shift_ref, core_ref), refs = refs[:slots], refs[slots : slots + 4], refs[slots + 4 :]
    if turn == 0:
        sum_ref, earlier_ref, out_ref, potential_ref, *scratch = refs
        potential_ref[...] = slope_ref[0:1, :] * (sum_ref[...] - lse_ref[0:1, :])
    else:
        out_ref, *scratch = refs

    @pl.when(core_ref[0] == turn)
    def work():
        sum_columns(z_refs, shift_ref[...] - slope_ref[...] * lse_ref[...], out_ref, *scratch)

    if turn == 0:

        @pl.when(core_ref[0] != turn)
        def hand_on():
            out_ref[...] = earlier_ref[...]


def f32(*shape):
    return jax.ShapeDtypeStruct(shape, jnp.float32)


def params(mebibytes):
    return pltpu.CompilerParams(vmem_limit_bytes=mebibytes * 1024 * 1024)


def shards(sources, targets, tgt_potential, src_logmass, tgt_logmass, src_exponent, tgt_exponent):
    src_count, width = sources.shape
    tgt_count = targets.shape[0]
    slabs = lax.axis_size("blk")
    sets = lax.axis_size("tsplit")
    chips = slabs // 2
    far = chips - 1
    groups = tgt_count // LANES
    src_groups = src_count // LANES
    assert chips > 1 and sets > 1 and chips & (chips - 1) == 0 and sets & (sets - 1) == 0

    def pair(value):
        return lax.ppermute(value, "blk", [(i, i ^ 1) for i in range(slabs)])

    def across(value, chip):
        return lax.ppermute(value, "blk", [(i, i ^ (2 * chip)) for i in range(slabs)])

    def along(value, step):
        return lax.ppermute(value, "tsplit", [(i, i ^ step) for i in range(sets)])

    def cost(blocks):
        pairs = blocks * src_count * tgt_count
        return pl.CostEstimate(flops=2 * pairs * width, bytes_accessed=2**20, transcendentals=pairs)

    core = lax.axis_index("blk") & 1
    core_word = core.astype(jnp.int32).reshape(1)
    pair_targets = pair(targets)
    inputs = (
        sources,
        targets,
        tgt_potential.reshape(groups, LANES),
        tgt_logmass.reshape(groups, LANES),
        src_exponent.reshape(src_groups, LANES),
        src_logmass.reshape(src_groups, LANES),
    )
    inputs = [pltpu.with_memory_space_constraint(x, pltpu.HBM) for x in inputs]

    product_space = pltpu.VMEM((2, PIECE, src_count), jnp.float32)

    def prepare_on(turn, *earlier):
        return pl.pallas_call(
            functools.partial(prepare_kernel, turn),
            out_shape=(
                jax.ShapeDtypeStruct(targets.shape, targets.dtype),
                f32(1, tgt_count),
                f32(tgt_count, LANES),
                f32(src_count, tgt_count),
                f32(1, src_count),
                f32(2, src_count),
                f32(1, src_count),
            ),
            in_specs=[SMEM] + [HBM] * 6 + [VMEM] * len(earlier),
            out_specs=(VMEM,) * 7,
            scratch_shapes=[pltpu.VMEM(x.shape, x.dtype) for x in (inputs[0], *inputs[2:])]
            + [product_space, pltpu.SemaphoreType.DMA((6,))],
            compiler_params=params(12),
            cost_estimate=cost(1),
            name=f"prepare_{turn}",
        )(core_word, *inputs, *earlier)

    earlier = prepare_on(1)
    first, sent = lax.optimization_barrier((earlier[6], sources))
    far_blocks = [across(sent, chip) for chip in range(1, chips)]
    held, offset, column, own_z, lse, line, src_sum = prepare_on(0, *earlier[:6], first)
    pair_offset = pair(offset)
    pair_column, lse = pl.pallas_call(
        near_kernel,
        out_shape=(f32(tgt_count, LANES), f32(1, src_count)),
        in_specs=[VMEM] * 4,
        out_specs=(VMEM,) * 2,
        scratch_shapes=[product_space],
        compiler_params=params(12),
        cost_estimate=cost(1),
        name="near_rows",
    )(sources, pair_targets, pair_offset, lse)
    far_lines = [across(line, chip) for chip in range(2, chips)]
    lse, *moved = lax.optimization_barrier((lse, *far_blocks, *far_lines))
    payload, mirrored = pl.pallas_call(
        functools.partial(far_kernel, far),
        out_shape=(f32(chips + 2, src_count),) * 2,
        in_specs=[VMEM] * (far + 6),
        out_specs=(VMEM,) * 2,
        scratch_shapes=[product_space],
        compiler_params=params(12 + far),
        cost_estimate=cost(2 * far),
        name="far_rows",
    )(*moved[:far], held, column, pair_targets, pair_column, lse, line)

    payload, mirrored, *blocks = lax.optimization_barrier((payload, mirrored, sources, *moved[:far]))
    def logits(block, *sides):
        return pl.pallas_call(
            functools.partial(logits_kernel, len(sides) // 2),
            out_shape=(f32(src_count, tgt_count),) * (len(sides) // 2),
            in_specs=[VMEM] * (1 + len(sides)),
            out_specs=(VMEM,) * (len(sides) // 2),
            compiler_params=params(12),
            cost_estimate=cost(len(sides) // 2),
            name="logits",
        )(block, *sides)

    own_zs, pair_zs = [own_z], list(logits(blocks[0], pair_targets, pair_offset))
    for block in blocks[1:]:
        own_z, pair_z = logits(block, held, offset, pair_targets, pair_offset)
        own_zs.append(own_z)
        pair_zs.append(pair_z)

    joined = lax.ppermute(
        mirrored,
        ("blk", "tsplit"),
        [(b * sets + z, (b ^ 2) * sets + (z ^ 1)) for b in range(slabs) for z in range(sets)],
    )
    other = across(mirrored, 1)
    beside = along(payload, 1)
    lines = jnp.stack([line, joined[chips:]] + moved[far:], axis=1)
    lse = merge(payload[:chips], other[:chips], beside[:chips], joined[:chips])
    chip = 2
    while chip < chips:
        there = across(lse, chip)
        lse = merge(lse, jnp.stack([there[slot ^ chip] for slot in range(chips)]))
        chip *= 2
    step = 2
    while step < sets:
        lse = merge(lse, along(lse, step))
        step *= 2

    def columns(kernel, zs, *more, outs=(f32(groups, LANES),)):
        return pl.pallas_call(
            kernel,
            out_shape=outs,
            in_specs=[VMEM] * (chips + 3) + [SMEM] * min(1, len(more)) + [VMEM] * (len(more) - 1),
            out_specs=(VMEM,) * len(outs),
            scratch_shapes=[
                pltpu.VMEM((chips, src_count, LANES), jnp.float32),
                pltpu.VMEM((chips, 8, tgt_count), jnp.float32),
                pltpu.VMEM((chips, 8, tgt_count), jnp.float32),
            ],
            compiler_params=params(8 + 2 * chips),
            cost_estimate=pl.CostEstimate(
                flops=6 * chips * src_count * tgt_count,
                bytes_accessed=2**20,
                transcendentals=chips * src_count * tgt_count,
            ),
            name="columns",
        )(*zs, lse, lines[0], lines[1], *more)

    (pair_part,) = columns(functools.partial(pair_kernel, chips), pair_zs)
    (early_part,) = columns(functools.partial(own_kernel, 1, chips), own_zs, core_word)
    lse, pair_part, early_part = lax.optimization_barrier((lse, pair_part, early_part))
    home = pair(pair_part)
    own_part, src_potential = columns(
        functools.partial(own_kernel, 0, chips),
        own_zs,
        core_word,
        src_sum,
        early_part,
        outs=(f32(groups, LANES), f32(1, src_count)),
    )
    total = merge(own_part, home).reshape(tgt_count)
    tgt_update = tgt_exponent * (2.0 * tgt_logmass + tgt_potential - total)
    return (src_potential.reshape(src_count), tgt_update)


def solution(mesh):
    placed = (
        P(("groups", "blk"), None),
        P(("groups", "blk", "tsplit"), None),
        P(("groups", "blk", "tsplit")),
        P(("groups", "blk")),
        P(("groups", "blk", "tsplit")),
        P(("groups", "blk")),
        P(("groups", "blk", "tsplit")),
    )
    return jax.shard_map(
        shards,
        mesh=mesh,
        in_specs=placed,
        out_specs=(P(("groups", "blk")), P(("groups", "blk", "tsplit"))),
        check_vma=False,
    )
```

```python
import functools
import math

import jax
import jax.numpy as jnp
from jax import lax
from jax.experimental import pallas as pl
from jax.experimental.pallas import tpu as pltpu
from jax.sharding import PartitionSpec as P

EPSILON = 0.5
LOGIT_SCALE = 2.0 / EPSILON
LOG2_E = math.log2(math.e)
LOG_2 = math.log(2.0)
LANES = 128
CHUNK = 256
PIECE = 1024
VMEM = pl.BlockSpec(memory_space=pltpu.VMEM)
SMEM = pl.BlockSpec(memory_space=pltpu.SMEM)
HBM = pl.BlockSpec(memory_space=pltpu.HBM)
NT_DIMS = (((1,), (1,)), ((), ()))


def diagonal():
    rows = lax.broadcasted_iota(jnp.int32, (LANES, LANES), 0)
    cols = lax.broadcasted_iota(jnp.int32, (LANES, LANES), 1)
    return rows == cols


def to_lanes(column, eye):
    return jnp.sum(jnp.where(eye, column, 0.0), axis=0, keepdims=True)


def to_column(lanes, eye):
    return jnp.sum(jnp.where(eye, lanes, 0.0), axis=1, keepdims=True)


def merge(*parts):
    peak = functools.reduce(jnp.maximum, parts)
    return peak + jnp.log(sum(jnp.exp(part - peak) for part in parts))


def squares(rows_ref, at):
    rows = rows_ref[at : at + LANES, :].astype(jnp.float32)
    return jnp.sum(rows * rows, axis=1, keepdims=True) / EPSILON


def row_sums(rows, sides, z_ref):
    rows = rows * LOGIT_SCALE
    pieces = [(side, at) for side, (tgt_ref, _) in enumerate(sides) for at in range(0, tgt_ref.shape[0], PIECE)]

    def product(index):
        side, at = pieces[index]
        part = sides[side][0][at : at + PIECE, :]
        z_ref[index % 2] = lax.dot_general(part, rows, NT_DIMS, preferred_element_type=jnp.float32)

    peaks, masses = [], []

    def absorb(index):
        side, at = pieces[index]
        for inner in range(0, PIECE, LANES):
            offset = sides[side][1][at + inner : at + inner + LANES, :]
            offset = jnp.concatenate([offset] * (rows.shape[0] // LANES), axis=1)
            z = z_ref[index % 2, inner : inner + LANES, :] * LOG2_E + offset
            z = z.reshape(LANES // 8, 8, rows.shape[0])
            peaks.append(jnp.max(z, axis=0))
            masses.append(jnp.sum(jnp.exp2(z - peaks[-1]), axis=0))

    product(0)
    for index in range(len(pieces)):
        if index + 1 < len(pieces):
            product(index + 1)
        absorb(index)
    peak = jnp.max(functools.reduce(jnp.maximum, peaks), axis=0, keepdims=True)
    mass = sum(mass * jnp.exp2(high - peak) for high, mass in zip(peaks, masses))
    return peak * LOG_2 + jnp.log(jnp.sum(mass, axis=0, keepdims=True))


def put_offsets(offset_ref, column_ref, eye):
    for at in range(0, offset_ref.shape[1], LANES):
        column = to_column(offset_ref[:, at : at + LANES] * LOG2_E, eye)
        column_ref[at : at + LANES, :] = jnp.broadcast_to(column, (LANES, LANES))


def make_logits(rows, tgt_ref, offset_ref, z_ref):
    rows = rows * LOGIT_SCALE
    for at in range(0, tgt_ref.shape[0], CHUNK):
        cols = slice(at, at + CHUNK)
        dots = lax.dot_general(rows, tgt_ref[cols, :], NT_DIMS, preferred_element_type=jnp.float32)
        z_ref[:, cols] = (dots + offset_ref[:, cols]) * LOG2_E


def logits_kernel(sides, rows_ref, *refs):
    for side in range(sides):
        make_logits(rows_ref[...], refs[2 * side], refs[2 * side + 1], refs[2 * sides + side])


def prepare_kernel(turn, core_ref, *refs):
    inputs, refs = refs[:6], refs[6:]
    earlier, refs = refs[: 7 * (1 - turn)], refs[7 * (1 - turn) :]
    outs, scratch = refs[:7], refs[7:]

    @pl.when(core_ref[0] == turn)
    def work():
        prepare(*inputs, *outs, *scratch)

    if earlier:

        @pl.when(core_ref[0] != turn)
        def hand_on():
            for source, target in zip(earlier, outs):
                target[...] = source[...]


def prepare(
    src_hbm, tgt_hbm, pot_hbm, mass_hbm, slope_hbm, logmass_hbm,
    tgt_ref, offset_ref, column_ref, own_z_ref, lse_ref, line_ref, sum_ref,
    src_ref, pot_ref, mass_ref, slope_ref, logmass_ref, z_ref, sems,
):
    pairs = (
        (tgt_hbm, tgt_ref), (src_hbm, src_ref), (pot_hbm, pot_ref),
        (mass_hbm, mass_ref), (slope_hbm, slope_ref), (logmass_hbm, logmass_ref),
    )
    copies = [pltpu.make_async_copy(source, target, sems.at[at]) for at, (source, target) in enumerate(pairs)]
    for copy in copies:
        copy.start()
    for copy in copies[1:]:
        copy.wait()
    eye = diagonal()
    for group in range(src_ref.shape[0] // LANES):
        cols = slice(group * LANES, (group + 1) * LANES)
        square = to_lanes(squares(src_ref, group * LANES), eye)
        slope = slope_ref[group : group + 1, :]
        logmass = logmass_ref[group : group + 1, :]
        sum_ref[:, cols] = logmass + square
        line_ref[0:1, cols] = slope
        line_ref[1:2, cols] = slope * (logmass + square) + (logmass - square)
    copies[0].wait()
    for group in range(tgt_ref.shape[0] // LANES):
        at = group * LANES
        base = pot_ref[group : group + 1, :] + mass_ref[group : group + 1, :]
        offset_ref[:, at : at + LANES] = base - to_lanes(squares(tgt_ref, at), eye)
    put_offsets(offset_ref, column_ref, eye)
    lse_ref[...] = row_sums(src_ref[...], ((tgt_ref, column_ref),), z_ref)
    make_logits(src_ref[...], tgt_ref, offset_ref, own_z_ref)


def near_kernel(rows_ref, tgt_ref, offset_ref, held_ref, column_ref, lse_ref, z_ref):
    put_offsets(offset_ref, column_ref, diagonal())
    lse_ref[...] = merge(held_ref[...], row_sums(rows_ref[...], ((tgt_ref, column_ref),), z_ref))


def far_kernel(count, *refs):
    own_ref, own_column_ref, pair_ref, pair_column_ref, held_ref, line_ref = refs[count : count + 6]
    out_ref, z_ref = refs[count + 6 :]
    slots = count + 1
    out_ref[0:1, :] = held_ref[...]
    out_ref[slots : slots + 2, :] = line_ref[...]
    for slot in range(count):
        sides = ((own_ref, own_column_ref), (pair_ref, pair_column_ref))
        out_ref[slot + 1 : slot + 2, :] = row_sums(refs[slot][...], sides, z_ref)


def sum_columns(z_refs, offset, out_ref, off_ref, peak_ref, mass_ref):
    eye = diagonal()
    slots, src_count = offset.shape
    for slot in range(slots):
        for at in range(0, src_count, LANES):
            column = to_column(offset[slot : slot + 1, at : at + LANES] * LOG2_E, eye)
            off_ref[slot, at : at + LANES, :] = jnp.broadcast_to(column, (LANES, LANES))

    for group in range(out_ref.shape[0]):
        cols = slice(group * LANES, (group + 1) * LANES)
        for slot in range(slots):
            z = (z_refs[slot][:, cols] + off_ref[slot]).reshape(src_count // 8, 8, LANES)
            peak = jnp.max(z, axis=0)
            peak_ref[slot, :, cols] = peak
            mass_ref[slot, :, cols] = jnp.sum(jnp.exp2(z - peak), axis=0)
    peak = jnp.max(functools.reduce(jnp.maximum, [peak_ref[slot] for slot in range(slots)]), axis=0, keepdims=True)
    mass = sum(mass_ref[slot] * jnp.exp2(peak_ref[slot] - peak) for slot in range(slots))
    total = peak * LOG_2 + jnp.log(jnp.sum(mass, axis=0, keepdims=True))
    for group in range(out_ref.shape[0]):
        out_ref[group : group + 1, :] = total[:, group * LANES : (group + 1) * LANES]


def pair_kernel(slots, *refs):
    lse_ref, slope_ref, shift_ref, out_ref, *scratch = refs[slots:]
    sum_columns(refs[:slots], shift_ref[...] - slope_ref[...] * lse_ref[...], out_ref, *scratch)


def own_kernel(slots, *refs):
    lse_ref, slope_ref, shift_ref, sum_ref, out_ref, potential_ref, *scratch = refs[slots:]
    lse, slope = lse_ref[...], slope_ref[...]
    potential_ref[...] = slope[0:1, :] * (sum_ref[...] - lse[0:1, :])
    sum_columns(refs[:slots], shift_ref[...] - slope * lse, out_ref, *scratch)


def f32(*shape):
    return jax.ShapeDtypeStruct(shape, jnp.float32)


def params(mebibytes):
    return pltpu.CompilerParams(vmem_limit_bytes=mebibytes * 1024 * 1024)


def shards(sources, targets, tgt_potential, src_logmass, tgt_logmass, src_exponent, tgt_exponent):
    src_count, width = sources.shape
    tgt_count = targets.shape[0]
    slabs = lax.axis_size("blk")
    sets = lax.axis_size("tsplit")
    chips = slabs // 2
    far = chips - 1
    groups = tgt_count // LANES
    src_groups = src_count // LANES
    assert chips > 1 and sets > 1 and chips & (chips - 1) == 0 and sets & (sets - 1) == 0

    def pair(value):
        return lax.ppermute(value, "blk", [(i, i ^ 1) for i in range(slabs)])

    def across(value, chip):
        return lax.ppermute(value, "blk", [(i, i ^ (2 * chip)) for i in range(slabs)])

    def along(value, step):
        return lax.ppermute(value, "tsplit", [(i, i ^ step) for i in range(sets)])

    def cost(blocks):
        pairs = blocks * src_count * tgt_count
        return pl.CostEstimate(flops=2 * pairs * width, bytes_accessed=2**20, transcendentals=pairs)

    core = lax.axis_index("blk") & 1
    core_word = core.astype(jnp.int32).reshape(1)
    pair_targets = pair(targets)
    inputs = (
        sources,
        targets,
        tgt_potential.reshape(groups, LANES),
        tgt_logmass.reshape(groups, LANES),
        src_exponent.reshape(src_groups, LANES),
        src_logmass.reshape(src_groups, LANES),
    )
    inputs = [pltpu.with_memory_space_constraint(x, pltpu.HBM) for x in inputs]

    product_space = pltpu.VMEM((2, PIECE, src_count), jnp.float32)

    def prepare_on(turn, *earlier):
        return pl.pallas_call(
            functools.partial(prepare_kernel, turn),
            out_shape=(
                jax.ShapeDtypeStruct(targets.shape, targets.dtype),
                f32(1, tgt_count),
                f32(tgt_count, LANES),
                f32(src_count, tgt_count),
                f32(1, src_count),
                f32(2, src_count),
                f32(1, src_count),
            ),
            in_specs=[SMEM] + [HBM] * 6 + [VMEM] * len(earlier),
            out_specs=(VMEM,) * 7,
            scratch_shapes=[pltpu.VMEM(x.shape, x.dtype) for x in (inputs[0], *inputs[2:])]
            + [product_space, pltpu.SemaphoreType.DMA((6,))],
            compiler_params=params(12),
            cost_estimate=cost(1),
            name=f"prepare_{turn}",
        )(core_word, *inputs, *earlier)

    earlier = prepare_on(1)
    first, sent = lax.optimization_barrier((earlier[6], sources))
    far_blocks = [across(sent, chip) for chip in range(1, chips)]
    held, offset, column, own_z, lse, line, src_sum = prepare_on(0, *earlier[:6], first)
    pair_offset = pair(offset)
    pair_column, lse = pl.pallas_call(
        near_kernel,
        out_shape=(f32(tgt_count, LANES), f32(1, src_count)),
        in_specs=[VMEM] * 4,
        out_specs=(VMEM,) * 2,
        scratch_shapes=[product_space],
        compiler_params=params(12),
        cost_estimate=cost(1),
        name="near_rows",
    )(sources, pair_targets, pair_offset, lse)
    far_lines = [across(line, chip) for chip in range(2, chips)]
    lse, *moved = lax.optimization_barrier((lse, *far_blocks, *far_lines))
    payload = pl.pallas_call(
        functools.partial(far_kernel, far),
        out_shape=f32(chips + 2, src_count),
        in_specs=[VMEM] * (far + 6),
        out_specs=VMEM,
        scratch_shapes=[product_space],
        compiler_params=params(12 + far),
        cost_estimate=cost(2 * far),
        name="far_rows",
    )(*moved[:far], held, column, pair_targets, pair_column, lse, line)

    payload, *blocks = lax.optimization_barrier((payload, sources, *moved[:far]))
    def logits(block, *sides):
        return pl.pallas_call(
            functools.partial(logits_kernel, len(sides) // 2),
            out_shape=(f32(src_count, tgt_count),) * (len(sides) // 2),
            in_specs=[VMEM] * (1 + len(sides)),
            out_specs=(VMEM,) * (len(sides) // 2),
            compiler_params=params(12),
            cost_estimate=cost(len(sides) // 2),
            name="logits",
        )(block, *sides)

    own_zs, pair_zs = [own_z], list(logits(blocks[0], pair_targets, pair_offset))
    for block in blocks[1:]:
        own_z, pair_z = logits(block, held, offset, pair_targets, pair_offset)
        own_zs.append(own_z)
        pair_zs.append(pair_z)

    def mirror(value, chip):
        return jnp.stack([value[slot ^ chip] for slot in range(chips)])

    other = across(payload, 1)
    beside = along(payload, 1)
    joined = lax.ppermute(
        payload,
        ("blk", "tsplit"),
        [(b * sets + z, (b ^ 2) * sets + (z ^ 1)) for b in range(slabs) for z in range(sets)],
    )
    lines = jnp.stack([line, other[chips:]] + moved[far:], axis=1)
    lse = merge(payload[:chips], mirror(other, 1), beside[:chips], mirror(joined, 1))
    chip = 2
    while chip < chips:
        lse = merge(lse, mirror(across(lse, chip), chip))
        chip *= 2
    step = 2
    while step < sets:
        lse = merge(lse, along(lse, step))
        step *= 2

    def columns(kernel, zs, *more):
        outs = (f32(groups, LANES), f32(1, src_count))[: 1 + len(more)]
        return pl.pallas_call(
            functools.partial(kernel, chips),
            out_shape=outs,
            in_specs=[VMEM] * (chips + 3 + len(more)),
            out_specs=(VMEM,) * len(outs),
            scratch_shapes=[
                pltpu.VMEM((chips, src_count, LANES), jnp.float32),
                pltpu.VMEM((chips, 8, tgt_count), jnp.float32),
                pltpu.VMEM((chips, 8, tgt_count), jnp.float32),
            ],
            compiler_params=params(8 + 2 * chips),
            cost_estimate=pl.CostEstimate(
                flops=6 * chips * src_count * tgt_count,
                bytes_accessed=2**20,
                transcendentals=chips * src_count * tgt_count,
            ),
            name="columns",
        )(*zs, lse, lines[0], lines[1], *more)

    (pair_part,) = columns(pair_kernel, pair_zs)
    lse, pair_part = lax.optimization_barrier((lse, pair_part))
    home = pair(pair_part)
    own_part, src_potential = columns(own_kernel, own_zs, src_sum)
    total = merge(own_part, home).reshape(tgt_count)
    tgt_update = tgt_exponent * (2.0 * tgt_logmass + tgt_potential - total)
    return (src_potential.reshape(src_count), tgt_update)


def solution(mesh):
    placed = (
        P(("groups", "blk"), None),
        P(("groups", "blk", "tsplit"), None),
        P(("groups", "blk", "tsplit")),
        P(("groups", "blk")),
        P(("groups", "blk", "tsplit")),
        P(("groups", "blk")),
        P(("groups", "blk", "tsplit")),
    )
    return jax.shard_map(
        shards,
        mesh=mesh,
        in_specs=placed,
        out_specs=(P(("groups", "blk")), P(("groups", "blk", "tsplit"))),
        check_vma=False,
    )
```

```python
import functools
import math

import jax
import jax.numpy as jnp
from jax import lax
from jax.experimental import pallas as pl
from jax.experimental.pallas import tpu as pltpu
from jax.sharding import PartitionSpec as P

EPSILON = 0.5
LOGIT_SCALE = 2.0 / EPSILON
LOG2_E = math.log2(math.e)
LOG_2 = math.log(2.0)
LANES = 128
CHUNK = 256
PIECE = 256
VMEM = pl.BlockSpec(memory_space=pltpu.VMEM)
SMEM = pl.BlockSpec(memory_space=pltpu.SMEM)
HBM = pl.BlockSpec(memory_space=pltpu.HBM)
NT_DIMS = (((1,), (1,)), ((), ()))


def diagonal():
    rows = lax.broadcasted_iota(jnp.int32, (LANES, LANES), 0)
    cols = lax.broadcasted_iota(jnp.int32, (LANES, LANES), 1)
    return rows == cols


def to_lanes(column, eye):
    return jnp.sum(jnp.where(eye, column, 0.0), axis=0, keepdims=True)


def to_column(lanes, eye):
    return jnp.sum(jnp.where(eye, lanes, 0.0), axis=1, keepdims=True)


def merge(*parts):
    peak = functools.reduce(jnp.maximum, parts)
    return peak + jnp.log(sum(jnp.exp(part - peak) for part in parts))


def squares(rows_ref, at):
    rows = rows_ref[at : at + LANES, :].astype(jnp.float32)
    return jnp.sum(rows * rows, axis=1, keepdims=True) / EPSILON


def row_sums(rows, sides, z_ref):
    rows = rows * LOGIT_SCALE
    pieces = [(side, at) for side, (tgt_ref, _) in enumerate(sides) for at in range(0, tgt_ref.shape[0], PIECE)]

    def product(index):
        side, at = pieces[index]
        part = sides[side][0][at : at + PIECE, :]
        z_ref[index % 2] = lax.dot_general(part, rows, NT_DIMS, preferred_element_type=jnp.float32)

    peaks, masses = [], []

    def absorb(index):
        side, at = pieces[index]
        for inner in range(0, PIECE, LANES):
            offset = sides[side][1][at + inner : at + inner + LANES, :]
            offset = jnp.concatenate([offset] * (rows.shape[0] // LANES), axis=1)
            z = z_ref[index % 2, inner : inner + LANES, :] * LOG2_E + offset
            z = z.reshape(LANES // 8, 8, rows.shape[0])
            peaks.append(jnp.max(z, axis=0))
            masses.append(jnp.sum(jnp.exp2(z - peaks[-1]), axis=0))

    product(0)
    for index in range(len(pieces)):
        if index + 1 < len(pieces):
            product(index + 1)
        absorb(index)
    peak = jnp.max(functools.reduce(jnp.maximum, peaks), axis=0, keepdims=True)
    mass = sum(mass * jnp.exp2(high - peak) for high, mass in zip(peaks, masses))
    return peak * LOG_2 + jnp.log(jnp.sum(mass, axis=0, keepdims=True))


def put_offsets(offset_ref, column_ref, eye):
    for at in range(0, offset_ref.shape[1], LANES):
        column = to_column(offset_ref[:, at : at + LANES] * LOG2_E, eye)
        column_ref[at : at + LANES, :] = jnp.broadcast_to(column, (LANES, LANES))


def make_logits(rows, tgt_ref, offset_ref, z_ref):
    rows = rows * LOGIT_SCALE
    for at in range(0, tgt_ref.shape[0], CHUNK):
        cols = slice(at, at + CHUNK)
        dots = lax.dot_general(rows, tgt_ref[cols, :], NT_DIMS, preferred_element_type=jnp.float32)
        z_ref[:, cols] = (dots + offset_ref[:, cols]) * LOG2_E


def logits_kernel(sides, rows_ref, *refs):
    for side in range(sides):
        make_logits(rows_ref[...], refs[2 * side], refs[2 * side + 1], refs[2 * sides + side])


def prepare_kernel(turn, core_ref, *refs):
    inputs, refs = refs[:6], refs[6:]
    earlier, refs = refs[: 7 * (1 - turn)], refs[7 * (1 - turn) :]
    outs, scratch = refs[:7], refs[7:]

    @pl.when(core_ref[0] == turn)
    def work():
        prepare(*inputs, *outs, *scratch)

    if earlier:

        @pl.when(core_ref[0] != turn)
        def hand_on():
            for source, target in zip(earlier, outs):
                target[...] = source[...]


def prepare(
    src_hbm, tgt_hbm, pot_hbm, mass_hbm, slope_hbm, logmass_hbm,
    tgt_ref, offset_ref, column_ref, own_z_ref, lse_ref, line_ref, sum_ref,
    src_ref, pot_ref, mass_ref, slope_ref, logmass_ref, z_ref, sems,
):
    pairs = (
        (tgt_hbm, tgt_ref), (src_hbm, src_ref), (pot_hbm, pot_ref),
        (mass_hbm, mass_ref), (slope_hbm, slope_ref), (logmass_hbm, logmass_ref),
    )
    copies = [pltpu.make_async_copy(source, target, sems.at[at]) for at, (source, target) in enumerate(pairs)]
    for copy in copies:
        copy.start()
    for copy in copies[1:]:
        copy.wait()
    eye = diagonal()
    for group in range(src_ref.shape[0] // LANES):
        cols = slice(group * LANES, (group + 1) * LANES)
        square = to_lanes(squares(src_ref, group * LANES), eye)
        slope = slope_ref[group : group + 1, :]
        logmass = logmass_ref[group : group + 1, :]
        sum_ref[:, cols] = logmass + square
        line_ref[0:1, cols] = slope
        line_ref[1:2, cols] = slope * (logmass + square) + (logmass - square)
    copies[0].wait()
    for group in range(tgt_ref.shape[0] // LANES):
        at = group * LANES
        base = pot_ref[group : group + 1, :] + mass_ref[group : group + 1, :]
        offset_ref[:, at : at + LANES] = base - to_lanes(squares(tgt_ref, at), eye)
    put_offsets(offset_ref, column_ref, eye)
    lse_ref[...] = row_sums(src_ref[...], ((tgt_ref, column_ref),), z_ref)
    make_logits(src_ref[...], tgt_ref, offset_ref, own_z_ref)


def near_kernel(rows_ref, tgt_ref, offset_ref, held_ref, column_ref, lse_ref, z_ref):
    put_offsets(offset_ref, column_ref, diagonal())
    lse_ref[...] = merge(held_ref[...], row_sums(rows_ref[...], ((tgt_ref, column_ref),), z_ref))


def far_kernel(count, *refs):
    own_ref, own_column_ref, pair_ref, pair_column_ref, held_ref, line_ref = refs[count : count + 6]
    out_ref, z_ref = refs[count + 6 :]
    slots = count + 1
    out_ref[0:1, :] = held_ref[...]
    out_ref[slots : slots + 2, :] = line_ref[...]
    for slot in range(count):
        sides = ((own_ref, own_column_ref), (pair_ref, pair_column_ref))
        out_ref[slot + 1 : slot + 2, :] = row_sums(refs[slot][...], sides, z_ref)


def sum_columns(z_refs, offset, out_ref, off_ref, peak_ref, mass_ref):
    eye = diagonal()
    slots, src_count = offset.shape
    for slot in range(slots):
        for at in range(0, src_count, LANES):
            column = to_column(offset[slot : slot + 1, at : at + LANES] * LOG2_E, eye)
            off_ref[slot, at : at + LANES, :] = jnp.broadcast_to(column, (LANES, LANES))

    for group in range(out_ref.shape[0]):
        cols = slice(group * LANES, (group + 1) * LANES)
        for slot in range(slots):
            z = (z_refs[slot][:, cols] + off_ref[slot]).reshape(src_count // 8, 8, LANES)
            peak = jnp.max(z, axis=0)
            peak_ref[slot, :, cols] = peak
            mass_ref[slot, :, cols] = jnp.sum(jnp.exp2(z - peak), axis=0)
    peak = jnp.max(functools.reduce(jnp.maximum, [peak_ref[slot] for slot in range(slots)]), axis=0, keepdims=True)
    mass = sum(mass_ref[slot] * jnp.exp2(peak_ref[slot] - peak) for slot in range(slots))
    total = peak * LOG_2 + jnp.log(jnp.sum(mass, axis=0, keepdims=True))
    for group in range(out_ref.shape[0]):
        out_ref[group : group + 1, :] = total[:, group * LANES : (group + 1) * LANES]


def pair_kernel(slots, *refs):
    lse_ref, slope_ref, shift_ref, out_ref, *scratch = refs[slots:]
    sum_columns(refs[:slots], shift_ref[...] - slope_ref[...] * lse_ref[...], out_ref, *scratch)


def own_kernel(slots, *refs):
    lse_ref, slope_ref, shift_ref, sum_ref, out_ref, potential_ref, *scratch = refs[slots:]
    lse, slope = lse_ref[...], slope_ref[...]
    potential_ref[...] = slope[0:1, :] * (sum_ref[...] - lse[0:1, :])
    sum_columns(refs[:slots], shift_ref[...] - slope * lse, out_ref, *scratch)


def f32(*shape):
    return jax.ShapeDtypeStruct(shape, jnp.float32)


def params(mebibytes):
    return pltpu.CompilerParams(vmem_limit_bytes=mebibytes * 1024 * 1024)


def shards(sources, targets, tgt_potential, src_logmass, tgt_logmass, src_exponent, tgt_exponent):
    src_count, width = sources.shape
    tgt_count = targets.shape[0]
    slabs = lax.axis_size("blk")
    sets = lax.axis_size("tsplit")
    chips = slabs // 2
    far = chips - 1
    groups = tgt_count // LANES
    src_groups = src_count // LANES
    assert chips > 1 and sets > 1 and chips & (chips - 1) == 0 and sets & (sets - 1) == 0

    def pair(value):
        return lax.ppermute(value, "blk", [(i, i ^ 1) for i in range(slabs)])

    def across(value, chip):
        return lax.ppermute(value, "blk", [(i, i ^ (2 * chip)) for i in range(slabs)])

    def along(value, step):
        return lax.ppermute(value, "tsplit", [(i, i ^ step) for i in range(sets)])

    def cost(blocks):
        pairs = blocks * src_count * tgt_count
        return pl.CostEstimate(flops=2 * pairs * width, bytes_accessed=2**20, transcendentals=pairs)

    core = lax.axis_index("blk") & 1
    core_word = core.astype(jnp.int32).reshape(1)
    pair_targets = pair(targets)
    inputs = (
        sources,
        targets,
        tgt_potential.reshape(groups, LANES),
        tgt_logmass.reshape(groups, LANES),
        src_exponent.reshape(src_groups, LANES),
        src_logmass.reshape(src_groups, LANES),
    )
    inputs = [pltpu.with_memory_space_constraint(x, pltpu.HBM) for x in inputs]

    product_space = pltpu.VMEM((2, PIECE, src_count), jnp.float32)

    def prepare_on(turn, *earlier):
        return pl.pallas_call(
            functools.partial(prepare_kernel, turn),
            out_shape=(
                jax.ShapeDtypeStruct(targets.shape, targets.dtype),
                f32(1, tgt_count),
                f32(tgt_count, LANES),
                f32(src_count, tgt_count),
                f32(1, src_count),
                f32(2, src_count),
                f32(1, src_count),
            ),
            in_specs=[SMEM] + [HBM] * 6 + [VMEM] * len(earlier),
            out_specs=(VMEM,) * 7,
            scratch_shapes=[pltpu.VMEM(x.shape, x.dtype) for x in (inputs[0], *inputs[2:])]
            + [product_space, pltpu.SemaphoreType.DMA((6,))],
            compiler_params=params(12),
            cost_estimate=cost(1),
            name=f"prepare_{turn}",
        )(core_word, *inputs, *earlier)

    earlier = prepare_on(1)
    first, sent = lax.optimization_barrier((earlier[6], sources))
    far_blocks = [across(sent, chip) for chip in range(1, chips)]
    held, offset, column, own_z, lse, line, src_sum = prepare_on(0, *earlier[:6], first)
    pair_offset = pair(offset)
    pair_column, lse = pl.pallas_call(
        near_kernel,
        out_shape=(f32(tgt_count, LANES), f32(1, src_count)),
        in_specs=[VMEM] * 4,
        out_specs=(VMEM,) * 2,
        scratch_shapes=[product_space],
        compiler_params=params(12),
        cost_estimate=cost(1),
        name="near_rows",
    )(sources, pair_targets, pair_offset, lse)
    far_lines = [across(line, chip) for chip in range(2, chips)]
    lse, *moved = lax.optimization_barrier((lse, *far_blocks, *far_lines))
    payload = pl.pallas_call(
        functools.partial(far_kernel, far),
        out_shape=f32(chips + 2, src_count),
        in_specs=[VMEM] * (far + 6),
        out_specs=VMEM,
        scratch_shapes=[product_space],
        compiler_params=params(12 + far),
        cost_estimate=cost(2 * far),
        name="far_rows",
    )(*moved[:far], held, column, pair_targets, pair_column, lse, line)

    payload, *blocks = lax.optimization_barrier((payload, sources, *moved[:far]))
    def logits(block, *sides):
        return pl.pallas_call(
            functools.partial(logits_kernel, len(sides) // 2),
            out_shape=(f32(src_count, tgt_count),) * (len(sides) // 2),
            in_specs=[VMEM] * (1 + len(sides)),
            out_specs=(VMEM,) * (len(sides) // 2),
            compiler_params=params(12),
            cost_estimate=cost(len(sides) // 2),
            name="logits",
        )(block, *sides)

    own_zs, pair_zs = [own_z], list(logits(blocks[0], pair_targets, pair_offset))
    for block in blocks[1:]:
        own_z, pair_z = logits(block, held, offset, pair_targets, pair_offset)
        own_zs.append(own_z)
        pair_zs.append(pair_z)

    def mirror(value, chip):
        return jnp.stack([value[slot ^ chip] for slot in range(chips)])

    other = across(payload, 1)
    beside = along(payload, 1)
    joined = lax.ppermute(
        payload,
        ("blk", "tsplit"),
        [(b * sets + z, (b ^ 2) * sets + (z ^ 1)) for b in range(slabs) for z in range(sets)],
    )
    lines = jnp.stack([line, other[chips:]] + moved[far:], axis=1)
    lse = merge(payload[:chips], mirror(other, 1), beside[:chips], mirror(joined, 1))
    chip = 2
    while chip < chips:
        lse = merge(lse, mirror(across(lse, chip), chip))
        chip *= 2
    step = 2
    while step < sets:
        lse = merge(lse, along(lse, step))
        step *= 2

    def columns(kernel, zs, *more):
        outs = (f32(groups, LANES), f32(1, src_count))[: 1 + len(more)]
        return pl.pallas_call(
            functools.partial(kernel, chips),
            out_shape=outs,
            in_specs=[VMEM] * (chips + 3 + len(more)),
            out_specs=(VMEM,) * len(outs),
            scratch_shapes=[
                pltpu.VMEM((chips, src_count, LANES), jnp.float32),
                pltpu.VMEM((chips, 8, tgt_count), jnp.float32),
                pltpu.VMEM((chips, 8, tgt_count), jnp.float32),
            ],
            compiler_params=params(8 + 2 * chips),
            cost_estimate=pl.CostEstimate(
                flops=6 * chips * src_count * tgt_count,
                bytes_accessed=2**20,
                transcendentals=chips * src_count * tgt_count,
            ),
            name="columns",
        )(*zs, lse, lines[0], lines[1], *more)

    (pair_part,) = columns(pair_kernel, pair_zs)
    lse, pair_part = lax.optimization_barrier((lse, pair_part))
    home = pair(pair_part)
    own_part, src_potential = columns(own_kernel, own_zs, src_sum)
    total = merge(own_part, home).reshape(tgt_count)
    tgt_update = tgt_exponent * (2.0 * tgt_logmass + tgt_potential - total)
    return (src_potential.reshape(src_count), tgt_update)


def solution(mesh):
    placed = (
        P(("groups", "blk"), None),
        P(("groups", "blk", "tsplit"), None),
        P(("groups", "blk", "tsplit")),
        P(("groups", "blk")),
        P(("groups", "blk", "tsplit")),
        P(("groups", "blk")),
        P(("groups", "blk", "tsplit")),
    )
    return jax.shard_map(
        shards,
        mesh=mesh,
        in_specs=placed,
        out_specs=(P(("groups", "blk")), P(("groups", "blk", "tsplit"))),
        check_vma=False,
    )
```

```python
import functools
import math

import jax
import jax.numpy as jnp
from jax import lax
from jax.experimental import pallas as pl
from jax.experimental.pallas import tpu as pltpu
from jax.sharding import PartitionSpec as P

EPSILON = 0.5
LOGIT_SCALE = 2.0 / EPSILON
LOG2_E = math.log2(math.e)
LOG_2 = math.log(2.0)
LANES = 128
CHUNK = 256
PIECE = 256
VMEM = pl.BlockSpec(memory_space=pltpu.VMEM)
SMEM = pl.BlockSpec(memory_space=pltpu.SMEM)
HBM = pl.BlockSpec(memory_space=pltpu.HBM)
NT_DIMS = (((1,), (1,)), ((), ()))


def diagonal():
    rows = lax.broadcasted_iota(jnp.int32, (LANES, LANES), 0)
    cols = lax.broadcasted_iota(jnp.int32, (LANES, LANES), 1)
    return rows == cols


def to_lanes(column, eye):
    return jnp.sum(jnp.where(eye, column, 0.0), axis=0, keepdims=True)


def to_column(lanes, eye):
    return jnp.sum(jnp.where(eye, lanes, 0.0), axis=1, keepdims=True)


def merge(*parts):
    peak = functools.reduce(jnp.maximum, parts)
    return peak + jnp.log(sum(jnp.exp(part - peak) for part in parts))


def squares(rows_ref, at):
    rows = rows_ref[at : at + LANES, :].astype(jnp.float32)
    return jnp.sum(rows * rows, axis=1, keepdims=True) / EPSILON


def row_sums(rows, sides, z_ref):
    rows = rows * LOGIT_SCALE
    pieces = [(side, at) for side, (tgt_ref, _) in enumerate(sides) for at in range(0, tgt_ref.shape[0], PIECE)]

    def product(index):
        side, at = pieces[index]
        part = sides[side][0][at : at + PIECE, :]
        z_ref[index % 2] = lax.dot_general(part, rows, NT_DIMS, preferred_element_type=jnp.float32)

    peaks, masses = [], []

    def absorb(index):
        side, at = pieces[index]
        for inner in range(0, PIECE, LANES):
            offset = sides[side][1][at + inner : at + inner + LANES, :]
            offset = jnp.concatenate([offset] * (rows.shape[0] // LANES), axis=1)
            z = z_ref[index % 2, inner : inner + LANES, :] * LOG2_E + offset
            z = z.reshape(LANES // 8, 8, rows.shape[0])
            peaks.append(jnp.max(z, axis=0))
            masses.append(jnp.sum(jnp.exp2(z - peaks[-1]), axis=0))

    product(0)
    for index in range(len(pieces)):
        if index + 1 < len(pieces):
            product(index + 1)
        absorb(index)
    peak = jnp.max(functools.reduce(jnp.maximum, peaks), axis=0, keepdims=True)
    mass = sum(mass * jnp.exp2(high - peak) for high, mass in zip(peaks, masses))
    return peak * LOG_2 + jnp.log(jnp.sum(mass, axis=0, keepdims=True))


def put_offsets(offset_ref, column_ref, eye):
    for at in range(0, offset_ref.shape[1], LANES):
        column = to_column(offset_ref[:, at : at + LANES] * LOG2_E, eye)
        column_ref[at : at + LANES, :] = jnp.broadcast_to(column, (LANES, LANES))


def make_logits(rows, tgt_ref, offset_ref, z_ref):
    rows = rows * LOGIT_SCALE
    for at in range(0, tgt_ref.shape[0], CHUNK):
        cols = slice(at, at + CHUNK)
        dots = lax.dot_general(rows, tgt_ref[cols, :], NT_DIMS, preferred_element_type=jnp.float32)
        z_ref[:, cols] = (dots + offset_ref[:, cols]) * LOG2_E


def logits_kernel(sides, core_ref, rows_ref, *refs):
    for side, needed in enumerate(sides):
        args = (rows_ref, refs[2 * side], refs[2 * side + 1], refs[2 * len(sides) + side])
        if needed is None:
            make_logits(args[0][...], *args[1:])
        else:
            pl.when(core_ref[0] == needed)(functools.partial(make_logits_of, *args))


def make_logits_of(rows_ref, *refs):
    make_logits(rows_ref[...], *refs)


def prepare_kernel(turn, core_ref, *refs):
    inputs, refs = refs[:6], refs[6:]
    earlier, refs = refs[: 7 * (1 - turn)], refs[7 * (1 - turn) :]
    outs, scratch = refs[:7], refs[7:]

    @pl.when(core_ref[0] == turn)
    def work():
        prepare(*inputs, *outs, *scratch)

    if earlier:

        @pl.when(core_ref[0] != turn)
        def hand_on():
            for source, target in zip(earlier, outs):
                target[...] = source[...]


def prepare(
    src_hbm, tgt_hbm, pot_hbm, mass_hbm, slope_hbm, logmass_hbm,
    tgt_ref, offset_ref, column_ref, own_z_ref, lse_ref, line_ref, sum_ref,
    src_ref, pot_ref, mass_ref, slope_ref, logmass_ref, z_ref, sems,
):
    pairs = (
        (tgt_hbm, tgt_ref), (src_hbm, src_ref), (pot_hbm, pot_ref),
        (mass_hbm, mass_ref), (slope_hbm, slope_ref), (logmass_hbm, logmass_ref),
    )
    copies = [pltpu.make_async_copy(source, target, sems.at[at]) for at, (source, target) in enumerate(pairs)]
    for copy in copies:
        copy.start()
    for copy in copies[1:]:
        copy.wait()
    eye = diagonal()
    for group in range(src_ref.shape[0] // LANES):
        cols = slice(group * LANES, (group + 1) * LANES)
        square = to_lanes(squares(src_ref, group * LANES), eye)
        slope = slope_ref[group : group + 1, :]
        logmass = logmass_ref[group : group + 1, :]
        sum_ref[:, cols] = logmass + square
        line_ref[0:1, cols] = slope
        line_ref[1:2, cols] = slope * (logmass + square) + (logmass - square)
    copies[0].wait()
    for group in range(tgt_ref.shape[0] // LANES):
        at = group * LANES
        base = pot_ref[group : group + 1, :] + mass_ref[group : group + 1, :]
        offset_ref[:, at : at + LANES] = base - to_lanes(squares(tgt_ref, at), eye)
    put_offsets(offset_ref, column_ref, eye)
    lse_ref[...] = row_sums(src_ref[...], ((tgt_ref, column_ref),), z_ref)
    make_logits(src_ref[...], tgt_ref, offset_ref, own_z_ref)


def near_kernel(rows_ref, tgt_ref, offset_ref, held_ref, column_ref, lse_ref, z_ref):
    put_offsets(offset_ref, column_ref, diagonal())
    lse_ref[...] = merge(held_ref[...], row_sums(rows_ref[...], ((tgt_ref, column_ref),), z_ref))


def far_kernel(count, *refs):
    own_ref, own_column_ref, pair_ref, pair_column_ref, held_ref, line_ref = refs[count : count + 6]
    out_ref, z_ref = refs[count + 6 :]
    slots = count + 1
    out_ref[0:1, :] = held_ref[...]
    out_ref[slots : slots + 2, :] = line_ref[...]
    for slot in range(count):
        sides = ((own_ref, own_column_ref), (pair_ref, pair_column_ref))
        out_ref[slot + 1 : slot + 2, :] = row_sums(refs[slot][...], sides, z_ref)


def sum_columns(z_refs, offset, out_ref, off_ref, peak_ref, mass_ref):
    eye = diagonal()
    slots, src_count = offset.shape
    for slot in range(slots):
        for at in range(0, src_count, LANES):
            column = to_column(offset[slot : slot + 1, at : at + LANES] * LOG2_E, eye)
            off_ref[slot, at : at + LANES, :] = jnp.broadcast_to(column, (LANES, LANES))

    for group in range(out_ref.shape[0]):
        cols = slice(group * LANES, (group + 1) * LANES)
        for slot in range(slots):
            z = (z_refs[slot][:, cols] + off_ref[slot]).reshape(src_count // 8, 8, LANES)
            peak = jnp.max(z, axis=0)
            peak_ref[slot, :, cols] = peak
            mass_ref[slot, :, cols] = jnp.sum(jnp.exp2(z - peak), axis=0)
    peak = jnp.max(functools.reduce(jnp.maximum, [peak_ref[slot] for slot in range(slots)]), axis=0, keepdims=True)
    mass = sum(mass_ref[slot] * jnp.exp2(peak_ref[slot] - peak) for slot in range(slots))
    total = peak * LOG_2 + jnp.log(jnp.sum(mass, axis=0, keepdims=True))
    for group in range(out_ref.shape[0]):
        out_ref[group : group + 1, :] = total[:, group * LANES : (group + 1) * LANES]


def pair_kernel(slots, core_ref, *refs):
    lse_ref, slope_ref, shift_ref, out_ref, *scratch = refs[slots:]
    offset = shift_ref[...] - slope_ref[...] * lse_ref[...]
    rows = offset.shape[1] // LANES

    @pl.when(core_ref[0] == 1)
    def work():
        sum_columns(refs[:slots], offset, out_ref.at[: refs[0].shape[1] // LANES], *scratch)

    @pl.when(core_ref[0] == 0)
    def send():
        for row in range(slots * rows):
            at = row % rows * LANES
            out_ref[row : row + 1, :] = offset[row // rows : row // rows + 1, at : at + LANES]


def away_kernel(slots, core_ref, *refs):
    home_ref, out_ref, *scratch = refs[slots:]
    rows = refs[0].shape[0] // LANES

    @pl.when(core_ref[0] == 1)
    def work():
        lines = [
            jnp.concatenate([home_ref[at : at + 1, :] for at in range(slot * rows, (slot + 1) * rows)], axis=1)
            for slot in range(slots)
        ]
        sum_columns(refs[:slots], jnp.concatenate(lines, axis=0), out_ref, *scratch)

    @pl.when(core_ref[0] == 0)
    def take():
        out_ref[...] = home_ref[: out_ref.shape[0], :]


def own_kernel(slots, *refs):
    lse_ref, slope_ref, shift_ref, sum_ref, out_ref, potential_ref, *scratch = refs[slots:]
    lse, slope = lse_ref[...], slope_ref[...]
    potential_ref[...] = slope[0:1, :] * (sum_ref[...] - lse[0:1, :])
    sum_columns(refs[:slots], shift_ref[...] - slope * lse, out_ref, *scratch)


def f32(*shape):
    return jax.ShapeDtypeStruct(shape, jnp.float32)


def params(mebibytes):
    return pltpu.CompilerParams(vmem_limit_bytes=mebibytes * 1024 * 1024)


def shards(sources, targets, tgt_potential, src_logmass, tgt_logmass, src_exponent, tgt_exponent):
    src_count, width = sources.shape
    tgt_count = targets.shape[0]
    slabs = lax.axis_size("blk")
    sets = lax.axis_size("tsplit")
    chips = slabs // 2
    far = chips - 1
    groups = tgt_count // LANES
    src_groups = src_count // LANES
    assert chips > 1 and sets > 1 and chips & (chips - 1) == 0 and sets & (sets - 1) == 0

    def pair(value):
        return lax.ppermute(value, "blk", [(i, i ^ 1) for i in range(slabs)])

    def across(value, chip):
        return lax.ppermute(value, "blk", [(i, i ^ (2 * chip)) for i in range(slabs)])

    def along(value, step):
        return lax.ppermute(value, "tsplit", [(i, i ^ step) for i in range(sets)])

    def cost(blocks):
        pairs = blocks * src_count * tgt_count
        return pl.CostEstimate(flops=2 * pairs * width, bytes_accessed=2**20, transcendentals=pairs)

    core = lax.axis_index("blk") & 1
    core_word = core.astype(jnp.int32).reshape(1)
    pair_targets = pair(targets)
    inputs = (
        sources,
        targets,
        tgt_potential.reshape(groups, LANES),
        tgt_logmass.reshape(groups, LANES),
        src_exponent.reshape(src_groups, LANES),
        src_logmass.reshape(src_groups, LANES),
    )
    inputs = [pltpu.with_memory_space_constraint(x, pltpu.HBM) for x in inputs]

    product_space = pltpu.VMEM((2, PIECE, src_count), jnp.float32)

    def prepare_on(turn, *earlier):
        return pl.pallas_call(
            functools.partial(prepare_kernel, turn),
            out_shape=(
                jax.ShapeDtypeStruct(targets.shape, targets.dtype),
                f32(1, tgt_count),
                f32(tgt_count, LANES),
                f32(src_count, tgt_count),
                f32(1, src_count),
                f32(2, src_count),
                f32(1, src_count),
            ),
            in_specs=[SMEM] + [HBM] * 6 + [VMEM] * len(earlier),
            out_specs=(VMEM,) * 7,
            scratch_shapes=[pltpu.VMEM(x.shape, x.dtype) for x in (inputs[0], *inputs[2:])]
            + [product_space, pltpu.SemaphoreType.DMA((6,))],
            compiler_params=params(12),
            cost_estimate=cost(1),
            name=f"prepare_{turn}",
        )(core_word, *inputs, *earlier)

    earlier = prepare_on(1)
    first, sent = lax.optimization_barrier((earlier[6], sources))
    far_blocks = [across(sent, chip) for chip in range(1, chips)]
    held, offset, column, own_z, lse, line, src_sum = prepare_on(0, *earlier[:6], first)
    pair_offset = pair(offset)
    offset, late_sources = lax.optimization_barrier((offset, sources))
    pair_sources = pair(late_sources)
    pair_column, lse = pl.pallas_call(
        near_kernel,
        out_shape=(f32(tgt_count, LANES), f32(1, src_count)),
        in_specs=[VMEM] * 4,
        out_specs=(VMEM,) * 2,
        scratch_shapes=[product_space],
        compiler_params=params(12),
        cost_estimate=cost(1),
        name="near_rows",
    )(sources, pair_targets, pair_offset, lse)
    far_lines = [across(line, chip) for chip in range(2, chips)]
    lse, *moved = lax.optimization_barrier((lse, *far_blocks, *far_lines))
    payload = pl.pallas_call(
        functools.partial(far_kernel, far),
        out_shape=f32(chips + 2, src_count),
        in_specs=[VMEM] * (far + 6),
        out_specs=VMEM,
        scratch_shapes=[product_space],
        compiler_params=params(12 + far),
        cost_estimate=cost(2 * far),
        name="far_rows",
    )(*moved[:far], held, column, pair_targets, pair_column, lse, line)

    payload, pair_sources, *blocks = lax.optimization_barrier((payload, pair_sources, sources, *moved[:far]))
    def logits(block, *sides):
        return pl.pallas_call(
            functools.partial(logits_kernel, [side[0] for side in sides]),
            out_shape=(f32(src_count, tgt_count),) * len(sides),
            in_specs=[SMEM] + [VMEM] * (1 + 2 * len(sides)),
            out_specs=(VMEM,) * len(sides),
            compiler_params=params(12),
            cost_estimate=cost(len(sides)),
            name="logits",
        )(core_word, block, *[array for side in sides for array in side[1:]])

    own_zs, pair_zs = [own_z], list(logits(blocks[0], (1, pair_targets, pair_offset)))
    for block in blocks[1:]:
        own_z, pair_z = logits(block, (None, held, offset), (1, pair_targets, pair_offset))
        own_zs.append(own_z)
        pair_zs.append(pair_z)
    away_zs = [logits(block, (1, held, offset))[0] for block in [pair_sources] + [pair(block) for block in blocks[1:]]]

    def mirror(value, chip):
        return jnp.stack([value[slot ^ chip] for slot in range(chips)])

    other = across(payload, 1)
    beside = along(payload, 1)
    joined = lax.ppermute(
        payload,
        ("blk", "tsplit"),
        [(b * sets + z, (b ^ 2) * sets + (z ^ 1)) for b in range(slabs) for z in range(sets)],
    )
    lines = jnp.stack([line, joined[chips:]] + moved[far:], axis=1)
    lse = merge(payload[:chips], mirror(other, 1), beside[:chips], mirror(joined, 1))
    chip = 2
    while chip < chips:
        lse = merge(lse, mirror(across(lse, chip), chip))
        chip *= 2
    step = 2
    while step < sets:
        lse = merge(lse, along(lse, step))
        step *= 2

    rows = max(groups, chips * src_groups)

    def columns(kernel, words, vectors, outs):
        return pl.pallas_call(
            functools.partial(kernel, chips),
            out_shape=outs,
            in_specs=[SMEM] * len(words) + [VMEM] * len(vectors),
            out_specs=(VMEM,) * len(outs),
            scratch_shapes=[
                pltpu.VMEM((chips, src_count, LANES), jnp.float32),
                pltpu.VMEM((chips, 8, tgt_count), jnp.float32),
                pltpu.VMEM((chips, 8, tgt_count), jnp.float32),
            ],
            compiler_params=params(8 + 2 * chips),
            cost_estimate=pl.CostEstimate(
                flops=6 * chips * src_count * tgt_count,
                bytes_accessed=2**20,
                transcendentals=chips * src_count * tgt_count,
            ),
            name="columns",
        )(*words, *vectors)

    found = (lse, lines[0], lines[1])
    (sent_part,) = columns(pair_kernel, (core_word,), (*pair_zs, *found), (f32(rows, LANES),))
    lse, sent_part = lax.optimization_barrier((lse, sent_part))
    home = pair(sent_part)
    own_part, src_potential = columns(
        own_kernel, (), (*own_zs, lse, lines[0], lines[1], src_sum), (f32(groups, LANES), f32(1, src_count))
    )
    own_part, home = lax.optimization_barrier((own_part, home))
    (away_part,) = columns(away_kernel, (core_word,), (*away_zs, home), (f32(groups, LANES),))
    total = merge(own_part, away_part).reshape(tgt_count)
    tgt_update = tgt_exponent * (2.0 * tgt_logmass + tgt_potential - total)
    return (src_potential.reshape(src_count), tgt_update)


def solution(mesh):
    placed = (
        P(("groups", "blk"), None),
        P(("groups", "blk", "tsplit"), None),
        P(("groups", "blk", "tsplit")),
        P(("groups", "blk")),
        P(("groups", "blk", "tsplit")),
        P(("groups", "blk")),
        P(("groups", "blk", "tsplit")),
    )
    return jax.shard_map(
        shards,
        mesh=mesh,
        in_specs=placed,
        out_specs=(P(("groups", "blk")), P(("groups", "blk", "tsplit"))),
        check_vma=False,
    )
```

```python
import functools
import math

import jax
import jax.numpy as jnp
from jax import lax
from jax.experimental import pallas as pl
from jax.experimental.pallas import tpu as pltpu
from jax.sharding import PartitionSpec as P

EPSILON = 0.5
LOGIT_SCALE = 2.0 / EPSILON
LOG2_E = math.log2(math.e)
LOG_2 = math.log(2.0)
LANES = 128
CHUNK = 256
PIECE = 256
VMEM = pl.BlockSpec(memory_space=pltpu.VMEM)
SMEM = pl.BlockSpec(memory_space=pltpu.SMEM)
HBM = pl.BlockSpec(memory_space=pltpu.HBM)
NT_DIMS = (((1,), (1,)), ((), ()))


def diagonal():
    rows = lax.broadcasted_iota(jnp.int32, (LANES, LANES), 0)
    cols = lax.broadcasted_iota(jnp.int32, (LANES, LANES), 1)
    return rows == cols


def to_lanes(column, eye):
    return jnp.sum(jnp.where(eye, column, 0.0), axis=0, keepdims=True)


def to_column(lanes, eye):
    return jnp.sum(jnp.where(eye, lanes, 0.0), axis=1, keepdims=True)


def merge(*parts):
    peak = functools.reduce(jnp.maximum, parts)
    return peak + jnp.log(sum(jnp.exp(part - peak) for part in parts))


def squares(rows_ref, at):
    rows = rows_ref[at : at + LANES, :].astype(jnp.float32)
    return jnp.sum(rows * rows, axis=1, keepdims=True) / EPSILON


def row_sums(rows, sides, z_ref):
    rows = rows * LOGIT_SCALE
    pieces = [(side, at) for side, (tgt_ref, _) in enumerate(sides) for at in range(0, tgt_ref.shape[0], PIECE)]

    def product(index):
        side, at = pieces[index]
        part = sides[side][0][at : at + PIECE, :]
        z_ref[index % 2] = lax.dot_general(part, rows, NT_DIMS, preferred_element_type=jnp.float32)

    peaks, masses = [], []

    def absorb(index):
        side, at = pieces[index]
        for inner in range(0, PIECE, LANES):
            offset = sides[side][1][at + inner : at + inner + LANES, :]
            offset = jnp.concatenate([offset] * (rows.shape[0] // LANES), axis=1)
            z = z_ref[index % 2, inner : inner + LANES, :] * LOG2_E + offset
            z = z.reshape(LANES // 8, 8, rows.shape[0])
            peaks.append(jnp.max(z, axis=0))
            masses.append(jnp.sum(jnp.exp2(z - peaks[-1]), axis=0))

    product(0)
    for index in range(len(pieces)):
        if index + 1 < len(pieces):
            product(index + 1)
        absorb(index)
    peak = jnp.max(functools.reduce(jnp.maximum, peaks), axis=0, keepdims=True)
    mass = sum(mass * jnp.exp2(high - peak) for high, mass in zip(peaks, masses))
    return peak * LOG_2 + jnp.log(jnp.sum(mass, axis=0, keepdims=True))


def put_offsets(offset_ref, column_ref, eye):
    for at in range(0, offset_ref.shape[1], LANES):
        column = to_column(offset_ref[:, at : at + LANES] * LOG2_E, eye)
        column_ref[at : at + LANES, :] = jnp.broadcast_to(column, (LANES, LANES))


def make_logits(rows, tgt_ref, offset_ref, z_ref):
    rows = rows * LOGIT_SCALE
    for at in range(0, tgt_ref.shape[0], CHUNK):
        cols = slice(at, at + CHUNK)
        dots = lax.dot_general(rows, tgt_ref[cols, :], NT_DIMS, preferred_element_type=jnp.float32)
        z_ref[:, cols] = (dots + offset_ref[:, cols]) * LOG2_E


def logits_kernel(sides, rows_ref, *refs):
    for side in range(sides):
        make_logits(rows_ref[...], refs[2 * side], refs[2 * side + 1], refs[2 * sides + side])


def prepare_kernel(turn, core_ref, *refs):
    inputs, refs = refs[:6], refs[6:]
    earlier, refs = refs[: 7 * (1 - turn)], refs[7 * (1 - turn) :]
    outs, scratch = refs[:7], refs[7:]

    @pl.when(core_ref[0] == turn)
    def work():
        prepare(*inputs, *outs, *scratch)

    if earlier:

        @pl.when(core_ref[0] != turn)
        def hand_on():
            for source, target in zip(earlier, outs):
                target[...] = source[...]


def prepare(
    src_hbm, tgt_hbm, pot_hbm, mass_hbm, slope_hbm, logmass_hbm,
    tgt_ref, offset_ref, column_ref, own_z_ref, lse_ref, line_ref, sum_ref,
    src_ref, pot_ref, mass_ref, slope_ref, logmass_ref, z_ref, sems,
):
    pairs = (
        (tgt_hbm, tgt_ref), (src_hbm, src_ref), (pot_hbm, pot_ref),
        (mass_hbm, mass_ref), (slope_hbm, slope_ref), (logmass_hbm, logmass_ref),
    )
    copies = [pltpu.make_async_copy(source, target, sems.at[at]) for at, (source, target) in enumerate(pairs)]
    for copy in copies:
        copy.start()
    for copy in copies[1:]:
        copy.wait()
    eye = diagonal()
    for group in range(src_ref.shape[0] // LANES):
        cols = slice(group * LANES, (group + 1) * LANES)
        square = to_lanes(squares(src_ref, group * LANES), eye)
        slope = slope_ref[group : group + 1, :]
        logmass = logmass_ref[group : group + 1, :]
        sum_ref[:, cols] = logmass + square
        line_ref[0:1, cols] = slope
        line_ref[1:2, cols] = slope * (logmass + square) + (logmass - square)
    copies[0].wait()
    for group in range(tgt_ref.shape[0] // LANES):
        at = group * LANES
        base = pot_ref[group : group + 1, :] + mass_ref[group : group + 1, :]
        offset_ref[:, at : at + LANES] = base - to_lanes(squares(tgt_ref, at), eye)
    put_offsets(offset_ref, column_ref, eye)
    lse_ref[...] = row_sums(src_ref[...], ((tgt_ref, column_ref),), z_ref)
    make_logits(src_ref[...], tgt_ref, offset_ref, own_z_ref)


def near_kernel(rows_ref, tgt_ref, offset_ref, held_ref, column_ref, lse_ref, z_ref):
    put_offsets(offset_ref, column_ref, diagonal())
    lse_ref[...] = merge(held_ref[...], row_sums(rows_ref[...], ((tgt_ref, column_ref),), z_ref))


def far_kernel(count, *refs):
    own_ref, own_column_ref, pair_ref, pair_column_ref, held_ref, line_ref = refs[count : count + 6]
    out_ref, z_ref = refs[count + 6 :]
    slots = count + 1
    out_ref[0:1, :] = held_ref[...]
    out_ref[slots : slots + 2, :] = line_ref[...]
    for slot in range(count):
        sides = ((own_ref, own_column_ref), (pair_ref, pair_column_ref))
        out_ref[slot + 1 : slot + 2, :] = row_sums(refs[slot][...], sides, z_ref)


def sum_columns(z_refs, offset, out_ref, off_ref, peak_ref, mass_ref):
    eye = diagonal()
    slots, src_count = offset.shape
    for slot in range(slots):
        for at in range(0, src_count, LANES):
            column = to_column(offset[slot : slot + 1, at : at + LANES] * LOG2_E, eye)
            off_ref[slot, at : at + LANES, :] = jnp.broadcast_to(column, (LANES, LANES))

    for group in range(out_ref.shape[0]):
        cols = slice(group * LANES, (group + 1) * LANES)
        for slot in range(slots):
            z = (z_refs[slot][:, cols] + off_ref[slot]).reshape(src_count // 8, 8, LANES)
            peak = jnp.max(z, axis=0)
            peak_ref[slot, :, cols] = peak
            mass_ref[slot, :, cols] = jnp.sum(jnp.exp2(z - peak), axis=0)
    peak = jnp.max(functools.reduce(jnp.maximum, [peak_ref[slot] for slot in range(slots)]), axis=0, keepdims=True)
    mass = sum(mass_ref[slot] * jnp.exp2(peak_ref[slot] - peak) for slot in range(slots))
    total = peak * LOG_2 + jnp.log(jnp.sum(mass, axis=0, keepdims=True))
    for group in range(out_ref.shape[0]):
        out_ref[group : group + 1, :] = total[:, group * LANES : (group + 1) * LANES]


def pair_kernel(slots, *refs):
    lse_ref, there_ref, slope_ref, shift_ref, out_ref, *scratch = refs[slots:]
    lse = merge(lse_ref[...], there_ref[...])
    sum_columns(refs[:slots], shift_ref[...] - slope_ref[...] * lse, out_ref, *scratch)


def own_kernel(turn, slots, *refs):
    z_refs, (lse_ref, there_ref, slope_ref, shift_ref, core_ref), refs = refs[:slots], refs[slots : slots + 5], refs[slots + 5 :]
    lse = merge(lse_ref[...], there_ref[...])
    if turn == 0:
        sum_ref, earlier_ref, out_ref, potential_ref, *scratch = refs
        potential_ref[...] = slope_ref[0:1, :] * (sum_ref[...] - lse[0:1, :])
    else:
        out_ref, *scratch = refs

    @pl.when(core_ref[0] == turn)
    def work():
        sum_columns(z_refs, shift_ref[...] - slope_ref[...] * lse, out_ref, *scratch)

    if turn == 0:

        @pl.when(core_ref[0] != turn)
        def hand_on():
            out_ref[...] = earlier_ref[...]


def f32(*shape):
    return jax.ShapeDtypeStruct(shape, jnp.float32)


def params(mebibytes):
    return pltpu.CompilerParams(vmem_limit_bytes=mebibytes * 1024 * 1024)


def shards(sources, targets, tgt_potential, src_logmass, tgt_logmass, src_exponent, tgt_exponent):
    src_count, width = sources.shape
    tgt_count = targets.shape[0]
    slabs = lax.axis_size("blk")
    sets = lax.axis_size("tsplit")
    chips = slabs // 2
    far = chips - 1
    groups = tgt_count // LANES
    src_groups = src_count // LANES
    assert chips > 1 and sets > 2 and chips & (chips - 1) == 0 and sets & (sets - 1) == 0

    def pair(value):
        return lax.ppermute(value, "blk", [(i, i ^ 1) for i in range(slabs)])

    def across(value, chip):
        return lax.ppermute(value, "blk", [(i, i ^ (2 * chip)) for i in range(slabs)])

    def along(value, step):
        return lax.ppermute(value, "tsplit", [(i, i ^ step) for i in range(sets)])

    def cost(blocks):
        pairs = blocks * src_count * tgt_count
        return pl.CostEstimate(flops=2 * pairs * width, bytes_accessed=2**20, transcendentals=pairs)

    core = lax.axis_index("blk") & 1
    core_word = core.astype(jnp.int32).reshape(1)
    pair_targets = pair(targets)
    inputs = (
        sources,
        targets,
        tgt_potential.reshape(groups, LANES),
        tgt_logmass.reshape(groups, LANES),
        src_exponent.reshape(src_groups, LANES),
        src_logmass.reshape(src_groups, LANES),
    )
    inputs = [pltpu.with_memory_space_constraint(x, pltpu.HBM) for x in inputs]

    product_space = pltpu.VMEM((2, PIECE, src_count), jnp.float32)

    def prepare_on(turn, *earlier):
        return pl.pallas_call(
            functools.partial(prepare_kernel, turn),
            out_shape=(
                jax.ShapeDtypeStruct(targets.shape, targets.dtype),
                f32(1, tgt_count),
                f32(tgt_count, LANES),
                f32(src_count, tgt_count),
                f32(1, src_count),
                f32(2, src_count),
                f32(1, src_count),
            ),
            in_specs=[SMEM] + [HBM] * 6 + [VMEM] * len(earlier),
            out_specs=(VMEM,) * 7,
            scratch_shapes=[pltpu.VMEM(x.shape, x.dtype) for x in (inputs[0], *inputs[2:])]
            + [product_space, pltpu.SemaphoreType.DMA((6,))],
            compiler_params=params(12),
            cost_estimate=cost(1),
            name=f"prepare_{turn}",
        )(core_word, *inputs, *earlier)

    earlier = prepare_on(1)
    first, sent = lax.optimization_barrier((earlier[6], sources))
    far_blocks = [across(sent, chip) for chip in range(1, chips)]
    held, offset, column, own_z, lse, line, src_sum = prepare_on(0, *earlier[:6], first)
    pair_offset = pair(offset)
    pair_column, lse = pl.pallas_call(
        near_kernel,
        out_shape=(f32(tgt_count, LANES), f32(1, src_count)),
        in_specs=[VMEM] * 4,
        out_specs=(VMEM,) * 2,
        scratch_shapes=[product_space],
        compiler_params=params(12),
        cost_estimate=cost(1),
        name="near_rows",
    )(sources, pair_targets, pair_offset, lse)
    far_lines = [across(line, chip) for chip in range(2, chips)]
    lse, *moved = lax.optimization_barrier((lse, *far_blocks, *far_lines))
    payload = pl.pallas_call(
        functools.partial(far_kernel, far),
        out_shape=f32(chips + 2, src_count),
        in_specs=[VMEM] * (far + 6),
        out_specs=VMEM,
        scratch_shapes=[product_space],
        compiler_params=params(12 + far),
        cost_estimate=cost(2 * far),
        name="far_rows",
    )(*moved[:far], held, column, pair_targets, pair_column, lse, line)

    payload, *blocks = lax.optimization_barrier((payload, sources, *moved[:far]))
    def logits(block, *sides):
        return pl.pallas_call(
            functools.partial(logits_kernel, len(sides) // 2),
            out_shape=(f32(src_count, tgt_count),) * (len(sides) // 2),
            in_specs=[VMEM] * (1 + len(sides)),
            out_specs=(VMEM,) * (len(sides) // 2),
            compiler_params=params(12),
            cost_estimate=cost(len(sides) // 2),
            name="logits",
        )(block, *sides)

    own_zs, pair_zs = [own_z], list(logits(blocks[0], pair_targets, pair_offset))
    for block in blocks[1:]:
        own_z, pair_z = logits(block, held, offset, pair_targets, pair_offset)
        own_zs.append(own_z)
        pair_zs.append(pair_z)

    def mirror(value, chip):
        return jnp.stack([value[slot ^ chip] for slot in range(chips)])

    other = across(payload, 1)
    beside = along(payload, 1)
    joined = lax.ppermute(
        payload,
        ("blk", "tsplit"),
        [(b * sets + z, (b ^ 2) * sets + (z ^ 1)) for b in range(slabs) for z in range(sets)],
    )
    lines = jnp.stack([line, other[chips:]] + moved[far:], axis=1)
    lse = merge(payload[:chips], mirror(other, 1), beside[:chips], mirror(joined, 1))
    chip = 2
    while chip < chips:
        lse = merge(lse, mirror(across(lse, chip), chip))
        chip *= 2
    step = 2
    while 2 * step < sets:
        lse = merge(lse, along(lse, step))
        step *= 2
    there = along(lse, step)

    def columns(kernel, zs, *more, outs=(f32(groups, LANES),)):
        return pl.pallas_call(
            kernel,
            out_shape=outs,
            in_specs=[VMEM] * (chips + 4) + [SMEM] * min(1, len(more)) + [VMEM] * (len(more) - 1),
            out_specs=(VMEM,) * len(outs),
            scratch_shapes=[
                pltpu.VMEM((chips, src_count, LANES), jnp.float32),
                pltpu.VMEM((chips, 8, tgt_count), jnp.float32),
                pltpu.VMEM((chips, 8, tgt_count), jnp.float32),
            ],
            compiler_params=params(8 + 2 * chips),
            cost_estimate=pl.CostEstimate(
                flops=6 * chips * src_count * tgt_count,
                bytes_accessed=2**20,
                transcendentals=chips * src_count * tgt_count,
            ),
            name="columns",
        )(*zs, lse, there, lines[0], lines[1], *more)

    (pair_part,) = columns(functools.partial(pair_kernel, chips), pair_zs)
    (early_part,) = columns(functools.partial(own_kernel, 1, chips), own_zs, core_word)
    there, pair_part, early_part = lax.optimization_barrier((there, pair_part, early_part))
    home = pair(pair_part)
    own_part, src_potential = columns(
        functools.partial(own_kernel, 0, chips),
        own_zs,
        core_word,
        src_sum,
        early_part,
        outs=(f32(groups, LANES), f32(1, src_count)),
    )
    total = merge(own_part, home).reshape(tgt_count)
    tgt_update = tgt_exponent * (2.0 * tgt_logmass + tgt_potential - total)
    return (src_potential.reshape(src_count), tgt_update)


def solution(mesh):
    placed = (
        P(("groups", "blk"), None),
        P(("groups", "blk", "tsplit"), None),
        P(("groups", "blk", "tsplit")),
        P(("groups", "blk")),
        P(("groups", "blk", "tsplit")),
        P(("groups", "blk")),
        P(("groups", "blk", "tsplit")),
    )
    return jax.shard_map(
        shards,
        mesh=mesh,
        in_specs=placed,
        out_specs=(P(("groups", "blk")), P(("groups", "blk", "tsplit"))),
        check_vma=False,
    )
```

```python
import functools
import math

import jax
import jax.numpy as jnp
from jax import lax
from jax.experimental import pallas as pl
from jax.experimental.pallas import tpu as pltpu
from jax.sharding import PartitionSpec as P

EPSILON = 0.5
LOGIT_SCALE = 2.0 / EPSILON
LOG2_E = math.log2(math.e)
LOG_2 = math.log(2.0)
LANES = 128
CHUNK = 256
PIECE = 128
VMEM = pl.BlockSpec(memory_space=pltpu.VMEM)
SMEM = pl.BlockSpec(memory_space=pltpu.SMEM)
HBM = pl.BlockSpec(memory_space=pltpu.HBM)
NT_DIMS = (((1,), (1,)), ((), ()))


def diagonal():
    rows = lax.broadcasted_iota(jnp.int32, (LANES, LANES), 0)
    cols = lax.broadcasted_iota(jnp.int32, (LANES, LANES), 1)
    return rows == cols


def to_lanes(column, eye):
    return jnp.sum(jnp.where(eye, column, 0.0), axis=0, keepdims=True)


def to_column(lanes, eye):
    return jnp.sum(jnp.where(eye, lanes, 0.0), axis=1, keepdims=True)


def merge(*parts):
    peak = functools.reduce(jnp.maximum, parts)
    return peak + jnp.log(sum(jnp.exp(part - peak) for part in parts))


def squares(rows_ref, at):
    rows = rows_ref[at : at + LANES, :].astype(jnp.float32)
    return jnp.sum(rows * rows, axis=1, keepdims=True) / EPSILON


def row_sums(rows, sides, z_ref):
    rows = rows * LOGIT_SCALE
    pieces = [(side, at) for side, (tgt_ref, _) in enumerate(sides) for at in range(0, tgt_ref.shape[0], PIECE)]

    def product(index):
        side, at = pieces[index]
        part = sides[side][0][at : at + PIECE, :]
        z_ref[index % 2] = lax.dot_general(part, rows, NT_DIMS, preferred_element_type=jnp.float32)

    peaks, masses = [], []

    def absorb(index):
        side, at = pieces[index]
        for inner in range(0, PIECE, LANES):
            offset = sides[side][1][at + inner : at + inner + LANES, :]
            offset = jnp.concatenate([offset] * (rows.shape[0] // LANES), axis=1)
            z = z_ref[index % 2, inner : inner + LANES, :] * LOG2_E + offset
            z = z.reshape(LANES // 8, 8, rows.shape[0])
            peaks.append(jnp.max(z, axis=0))
            masses.append(jnp.sum(jnp.exp2(z - peaks[-1]), axis=0))

    product(0)
    for index in range(len(pieces)):
        if index + 1 < len(pieces):
            product(index + 1)
        absorb(index)
    peak = jnp.max(functools.reduce(jnp.maximum, peaks), axis=0, keepdims=True)
    mass = sum(mass * jnp.exp2(high - peak) for high, mass in zip(peaks, masses))
    return peak * LOG_2 + jnp.log(jnp.sum(mass, axis=0, keepdims=True))


def put_offsets(offset_ref, column_ref, eye):
    for at in range(0, offset_ref.shape[1], LANES):
        column = to_column(offset_ref[:, at : at + LANES] * LOG2_E, eye)
        column_ref[at : at + LANES, :] = jnp.broadcast_to(column, (LANES, LANES))


def make_logits(rows, tgt_ref, offset_ref, z_ref):
    rows = rows * LOGIT_SCALE
    for at in range(0, tgt_ref.shape[0], CHUNK):
        cols = slice(at, at + CHUNK)
        dots = lax.dot_general(rows, tgt_ref[cols, :], NT_DIMS, preferred_element_type=jnp.float32)
        z_ref[:, cols] = (dots + offset_ref[:, cols]) * LOG2_E


def logits_kernel(sides, rows_ref, *refs):
    for side in range(sides):
        make_logits(rows_ref[...], refs[2 * side], refs[2 * side + 1], refs[2 * sides + side])


def prepare_kernel(turn, core_ref, *refs):
    inputs, refs = refs[:6], refs[6:]
    earlier, refs = refs[: 7 * (1 - turn)], refs[7 * (1 - turn) :]
    outs, scratch = refs[:7], refs[7:]

    @pl.when(core_ref[0] == turn)
    def work():
        prepare(*inputs, *outs, *scratch)

    if earlier:

        @pl.when(core_ref[0] != turn)
        def hand_on():
            for source, target in zip(earlier, outs):
                target[...] = source[...]


def prepare(
    src_hbm, tgt_hbm, pot_hbm, mass_hbm, slope_hbm, logmass_hbm,
    tgt_ref, offset_ref, column_ref, own_z_ref, lse_ref, line_ref, sum_ref,
    src_ref, pot_ref, mass_ref, slope_ref, logmass_ref, z_ref, sems,
):
    pairs = (
        (tgt_hbm, tgt_ref), (src_hbm, src_ref), (pot_hbm, pot_ref),
        (mass_hbm, mass_ref), (slope_hbm, slope_ref), (logmass_hbm, logmass_ref),
    )
    copies = [pltpu.make_async_copy(source, target, sems.at[at]) for at, (source, target) in enumerate(pairs)]
    for copy in copies:
        copy.start()
    for copy in copies[1:]:
        copy.wait()
    eye = diagonal()
    for group in range(src_ref.shape[0] // LANES):
        cols = slice(group * LANES, (group + 1) * LANES)
        square = to_lanes(squares(src_ref, group * LANES), eye)
        slope = slope_ref[group : group + 1, :]
        logmass = logmass_ref[group : group + 1, :]
        sum_ref[:, cols] = logmass + square
        line_ref[0:1, cols] = slope
        line_ref[1:2, cols] = slope * (logmass + square) + (logmass - square)
    copies[0].wait()
    for group in range(tgt_ref.shape[0] // LANES):
        at = group * LANES
        base = pot_ref[group : group + 1, :] + mass_ref[group : group + 1, :]
        offset_ref[:, at : at + LANES] = base - to_lanes(squares(tgt_ref, at), eye)
    put_offsets(offset_ref, column_ref, eye)
    lse_ref[...] = row_sums(src_ref[...], ((tgt_ref, column_ref),), z_ref)
    make_logits(src_ref[...], tgt_ref, offset_ref, own_z_ref)


def near_kernel(rows_ref, tgt_ref, offset_ref, held_ref, column_ref, lse_ref, z_ref):
    put_offsets(offset_ref, column_ref, diagonal())
    lse_ref[...] = merge(held_ref[...], row_sums(rows_ref[...], ((tgt_ref, column_ref),), z_ref))


def far_kernel(count, *refs):
    own_ref, own_column_ref, pair_ref, pair_column_ref, held_ref, line_ref = refs[count : count + 6]
    out_ref, z_ref = refs[count + 6 :]
    slots = count + 1
    out_ref[0:1, :] = held_ref[...]
    out_ref[slots : slots + 2, :] = line_ref[...]
    for slot in range(count):
        sides = ((own_ref, own_column_ref), (pair_ref, pair_column_ref))
        out_ref[slot + 1 : slot + 2, :] = row_sums(refs[slot][...], sides, z_ref)


def sum_columns(z_refs, offset, out_ref, off_ref, peak_ref, mass_ref):
    eye = diagonal()
    slots, src_count = offset.shape
    for slot in range(slots):
        for at in range(0, src_count, LANES):
            column = to_column(offset[slot : slot + 1, at : at + LANES] * LOG2_E, eye)
            off_ref[slot, at : at + LANES, :] = jnp.broadcast_to(column, (LANES, LANES))

    for group in range(out_ref.shape[0]):
        cols = slice(group * LANES, (group + 1) * LANES)
        for slot in range(slots):
            z = (z_refs[slot][:, cols] + off_ref[slot]).reshape(src_count // 8, 8, LANES)
            peak = jnp.max(z, axis=0)
            peak_ref[slot, :, cols] = peak
            mass_ref[slot, :, cols] = jnp.sum(jnp.exp2(z - peak), axis=0)
    peak = jnp.max(functools.reduce(jnp.maximum, [peak_ref[slot] for slot in range(slots)]), axis=0, keepdims=True)
    mass = sum(mass_ref[slot] * jnp.exp2(peak_ref[slot] - peak) for slot in range(slots))
    total = peak * LOG_2 + jnp.log(jnp.sum(mass, axis=0, keepdims=True))
    for group in range(out_ref.shape[0]):
        out_ref[group : group + 1, :] = total[:, group * LANES : (group + 1) * LANES]


def pair_kernel(slots, *refs):
    lse_ref, there_ref, slope_ref, shift_ref, out_ref, *scratch = refs[slots:]
    lse = merge(lse_ref[...], there_ref[...])
    sum_columns(refs[:slots], shift_ref[...] - slope_ref[...] * lse, out_ref, *scratch)


def own_kernel(turn, slots, *refs):
    z_refs, (lse_ref, there_ref, slope_ref, shift_ref, core_ref), refs = refs[:slots], refs[slots : slots + 5], refs[slots + 5 :]
    lse = merge(lse_ref[...], there_ref[...])
    if turn == 0:
        sum_ref, earlier_ref, out_ref, potential_ref, *scratch = refs
        potential_ref[...] = slope_ref[0:1, :] * (sum_ref[...] - lse[0:1, :])
    else:
        out_ref, *scratch = refs

    @pl.when(core_ref[0] == turn)
    def work():
        sum_columns(z_refs, shift_ref[...] - slope_ref[...] * lse, out_ref, *scratch)

    if turn == 0:

        @pl.when(core_ref[0] != turn)
        def hand_on():
            out_ref[...] = earlier_ref[...]


def f32(*shape):
    return jax.ShapeDtypeStruct(shape, jnp.float32)


def params(mebibytes):
    return pltpu.CompilerParams(vmem_limit_bytes=mebibytes * 1024 * 1024)


def shards(sources, targets, tgt_potential, src_logmass, tgt_logmass, src_exponent, tgt_exponent):
    src_count, width = sources.shape
    tgt_count = targets.shape[0]
    slabs = lax.axis_size("blk")
    sets = lax.axis_size("tsplit")
    chips = slabs // 2
    far = chips - 1
    groups = tgt_count // LANES
    src_groups = src_count // LANES
    assert chips > 1 and sets > 2 and chips & (chips - 1) == 0 and sets & (sets - 1) == 0

    def pair(value):
        return lax.ppermute(value, "blk", [(i, i ^ 1) for i in range(slabs)])

    def across(value, chip):
        return lax.ppermute(value, "blk", [(i, i ^ (2 * chip)) for i in range(slabs)])

    def along(value, step):
        return lax.ppermute(value, "tsplit", [(i, i ^ step) for i in range(sets)])

    def cost(blocks):
        pairs = blocks * src_count * tgt_count
        return pl.CostEstimate(flops=2 * pairs * width, bytes_accessed=2**20, transcendentals=pairs)

    core = lax.axis_index("blk") & 1
    core_word = core.astype(jnp.int32).reshape(1)
    pair_targets = pair(targets)
    inputs = (
        sources,
        targets,
        tgt_potential.reshape(groups, LANES),
        tgt_logmass.reshape(groups, LANES),
        src_exponent.reshape(src_groups, LANES),
        src_logmass.reshape(src_groups, LANES),
    )
    inputs = [pltpu.with_memory_space_constraint(x, pltpu.HBM) for x in inputs]

    product_space = pltpu.VMEM((2, PIECE, src_count), jnp.float32)

    def prepare_on(turn, *earlier):
        return pl.pallas_call(
            functools.partial(prepare_kernel, turn),
            out_shape=(
                jax.ShapeDtypeStruct(targets.shape, targets.dtype),
                f32(1, tgt_count),
                f32(tgt_count, LANES),
                f32(src_count, tgt_count),
                f32(1, src_count),
                f32(2, src_count),
                f32(1, src_count),
            ),
            in_specs=[SMEM] + [HBM] * 6 + [VMEM] * len(earlier),
            out_specs=(VMEM,) * 7,
            scratch_shapes=[pltpu.VMEM(x.shape, x.dtype) for x in (inputs[0], *inputs[2:])]
            + [product_space, pltpu.SemaphoreType.DMA((6,))],
            compiler_params=params(12),
            cost_estimate=cost(1),
            name=f"prepare_{turn}",
        )(core_word, *inputs, *earlier)

    earlier = prepare_on(1)
    first, sent = lax.optimization_barrier((earlier[6], sources))
    far_blocks = [across(sent, chip) for chip in range(1, chips)]
    held, offset, column, own_z, lse, line, src_sum = prepare_on(0, *earlier[:6], first)
    pair_offset = pair(offset)
    pair_column, lse = pl.pallas_call(
        near_kernel,
        out_shape=(f32(tgt_count, LANES), f32(1, src_count)),
        in_specs=[VMEM] * 4,
        out_specs=(VMEM,) * 2,
        scratch_shapes=[product_space],
        compiler_params=params(12),
        cost_estimate=cost(1),
        name="near_rows",
    )(sources, pair_targets, pair_offset, lse)
    far_lines = [across(line, chip) for chip in range(2, chips)]
    lse, *moved = lax.optimization_barrier((lse, *far_blocks, *far_lines))
    payload = pl.pallas_call(
        functools.partial(far_kernel, far),
        out_shape=f32(chips + 2, src_count),
        in_specs=[VMEM] * (far + 6),
        out_specs=VMEM,
        scratch_shapes=[product_space],
        compiler_params=params(12 + far),
        cost_estimate=cost(2 * far),
        name="far_rows",
    )(*moved[:far], held, column, pair_targets, pair_column, lse, line)

    payload, *blocks = lax.optimization_barrier((payload, sources, *moved[:far]))
    def logits(block, *sides):
        return pl.pallas_call(
            functools.partial(logits_kernel, len(sides) // 2),
            out_shape=(f32(src_count, tgt_count),) * (len(sides) // 2),
            in_specs=[VMEM] * (1 + len(sides)),
            out_specs=(VMEM,) * (len(sides) // 2),
            compiler_params=params(12),
            cost_estimate=cost(len(sides) // 2),
            name="logits",
        )(block, *sides)

    own_zs, pair_zs = [own_z], list(logits(blocks[0], pair_targets, pair_offset))
    for block in blocks[1:]:
        own_z, pair_z = logits(block, held, offset, pair_targets, pair_offset)
        own_zs.append(own_z)
        pair_zs.append(pair_z)

    def mirror(value, chip):
        return jnp.stack([value[slot ^ chip] for slot in range(chips)])

    other = across(payload, 1)
    beside = along(payload, 1)
    joined = lax.ppermute(
        payload,
        ("blk", "tsplit"),
        [(b * sets + z, (b ^ 2) * sets + (z ^ 1)) for b in range(slabs) for z in range(sets)],
    )
    lines = jnp.stack([line, other[chips:]] + moved[far:], axis=1)
    lse = merge(payload[:chips], mirror(other, 1), beside[:chips], mirror(joined, 1))
    chip = 2
    while chip < chips:
        lse = merge(lse, mirror(across(lse, chip), chip))
        chip *= 2
    step = 2
    while 2 * step < sets:
        lse = merge(lse, along(lse, step))
        step *= 2
    there = along(lse, step)

    def columns(kernel, zs, *more, outs=(f32(groups, LANES),)):
        return pl.pallas_call(
            kernel,
            out_shape=outs,
            in_specs=[VMEM] * (chips + 4) + [SMEM] * min(1, len(more)) + [VMEM] * (len(more) - 1),
            out_specs=(VMEM,) * len(outs),
            scratch_shapes=[
                pltpu.VMEM((chips, src_count, LANES), jnp.float32),
                pltpu.VMEM((chips, 8, tgt_count), jnp.float32),
                pltpu.VMEM((chips, 8, tgt_count), jnp.float32),
            ],
            compiler_params=params(8 + 2 * chips),
            cost_estimate=pl.CostEstimate(
                flops=6 * chips * src_count * tgt_count,
                bytes_accessed=2**20,
                transcendentals=chips * src_count * tgt_count,
            ),
            name="columns",
        )(*zs, lse, there, lines[0], lines[1], *more)

    (pair_part,) = columns(functools.partial(pair_kernel, chips), pair_zs)
    (early_part,) = columns(functools.partial(own_kernel, 1, chips), own_zs, core_word)
    there, pair_part, early_part = lax.optimization_barrier((there, pair_part, early_part))
    home = pair(pair_part)
    own_part, src_potential = columns(
        functools.partial(own_kernel, 0, chips),
        own_zs,
        core_word,
        src_sum,
        early_part,
        outs=(f32(groups, LANES), f32(1, src_count)),
    )
    total = merge(own_part, home).reshape(tgt_count)
    tgt_update = tgt_exponent * (2.0 * tgt_logmass + tgt_potential - total)
    return (src_potential.reshape(src_count), tgt_update)


def solution(mesh):
    placed = (
        P(("groups", "blk"), None),
        P(("groups", "blk", "tsplit"), None),
        P(("groups", "blk", "tsplit")),
        P(("groups", "blk")),
        P(("groups", "blk", "tsplit")),
        P(("groups", "blk")),
        P(("groups", "blk", "tsplit")),
    )
    return jax.shard_map(
        shards,
        mesh=mesh,
        in_specs=placed,
        out_specs=(P(("groups", "blk")), P(("groups", "blk", "tsplit"))),
        check_vma=False,
    )
```

```python
import functools
import math

import jax
import jax.numpy as jnp
from jax import lax
from jax.experimental import pallas as pl
from jax.experimental.pallas import tpu as pltpu
from jax.sharding import PartitionSpec as P

EPSILON = 0.5
LOGIT_SCALE = 2.0 / EPSILON
LOG2_E = math.log2(math.e)
LOG_2 = math.log(2.0)
LANES = 128
CHUNK = 256
PIECE = 256
VMEM = pl.BlockSpec(memory_space=pltpu.VMEM)
SMEM = pl.BlockSpec(memory_space=pltpu.SMEM)
HBM = pl.BlockSpec(memory_space=pltpu.HBM)
NT_DIMS = (((1,), (1,)), ((), ()))


def diagonal():
    rows = lax.broadcasted_iota(jnp.int32, (LANES, LANES), 0)
    cols = lax.broadcasted_iota(jnp.int32, (LANES, LANES), 1)
    return rows == cols


def to_lanes(column, eye):
    return jnp.sum(jnp.where(eye, column, 0.0), axis=0, keepdims=True)


def to_column(lanes, eye):
    return jnp.sum(jnp.where(eye, lanes, 0.0), axis=1, keepdims=True)


def merge(*parts):
    peak = functools.reduce(jnp.maximum, parts)
    return peak + jnp.log(sum(jnp.exp(part - peak) for part in parts))


def squares(rows_ref, at):
    rows = rows_ref[at : at + LANES, :].astype(jnp.float32)
    return jnp.sum(rows * rows, axis=1, keepdims=True) / EPSILON


def row_sums(rows, sides, z_ref):
    rows = rows * LOGIT_SCALE
    pieces = [(side, at) for side, (tgt_ref, _) in enumerate(sides) for at in range(0, tgt_ref.shape[0], PIECE)]

    def product(index):
        side, at = pieces[index]
        part = sides[side][0][at : at + PIECE, :]
        z_ref[index % 2] = lax.dot_general(part, rows, NT_DIMS, preferred_element_type=jnp.float32)

    peaks, masses = [], []

    def absorb(index):
        side, at = pieces[index]
        for inner in range(0, PIECE, LANES):
            offset = sides[side][1][at + inner : at + inner + LANES, :]
            offset = jnp.concatenate([offset] * (rows.shape[0] // LANES), axis=1)
            z = z_ref[index % 2, inner : inner + LANES, :] * LOG2_E + offset
            z = z.reshape(LANES // 8, 8, rows.shape[0])
            peaks.append(jnp.max(z, axis=0))
            masses.append(jnp.sum(jnp.exp2(z - peaks[-1]), axis=0))

    product(0)
    for index in range(len(pieces)):
        if index + 1 < len(pieces):
            product(index + 1)
        absorb(index)
    peak = jnp.max(functools.reduce(jnp.maximum, peaks), axis=0, keepdims=True)
    mass = sum(mass * jnp.exp2(high - peak) for high, mass in zip(peaks, masses))
    return peak * LOG_2 + jnp.log(jnp.sum(mass, axis=0, keepdims=True))


def put_offsets(offset_ref, column_ref, eye):
    for at in range(0, offset_ref.shape[1], LANES):
        column = to_column(offset_ref[:, at : at + LANES] * LOG2_E, eye)
        column_ref[at : at + LANES, :] = jnp.broadcast_to(column, (LANES, LANES))


def make_logits(rows, tgt_ref, offset_ref, z_ref):
    rows = rows * LOGIT_SCALE
    for at in range(0, tgt_ref.shape[0], CHUNK):
        cols = slice(at, at + CHUNK)
        dots = lax.dot_general(rows, tgt_ref[cols, :], NT_DIMS, preferred_element_type=jnp.float32)
        z_ref[:, cols] = (dots + offset_ref[:, cols]) * LOG2_E


def logits_kernel(sides, rows_ref, *refs):
    for side in range(sides):
        make_logits(rows_ref[...], refs[2 * side], refs[2 * side + 1], refs[2 * sides + side])


def prepare_kernel(turn, core_ref, *refs):
    inputs, refs = refs[:6], refs[6:]
    earlier, refs = refs[: 7 * (1 - turn)], refs[7 * (1 - turn) :]
    outs, scratch = refs[:7], refs[7:]

    @pl.when(core_ref[0] == turn)
    def work():
        prepare(*inputs, *outs, *scratch)

    if earlier:

        @pl.when(core_ref[0] != turn)
        def hand_on():
            for source, target in zip(earlier, outs):
                target[...] = source[...]


def prepare(
    src_hbm, tgt_hbm, pot_hbm, mass_hbm, slope_hbm, logmass_hbm,
    tgt_ref, offset_ref, column_ref, own_z_ref, lse_ref, line_ref, sum_ref,
    src_ref, pot_ref, mass_ref, slope_ref, logmass_ref, z_ref, sems,
):
    pairs = (
        (tgt_hbm, tgt_ref), (src_hbm, src_ref), (pot_hbm, pot_ref),
        (mass_hbm, mass_ref), (slope_hbm, slope_ref), (logmass_hbm, logmass_ref),
    )
    copies = [pltpu.make_async_copy(source, target, sems.at[at]) for at, (source, target) in enumerate(pairs)]
    for copy in copies:
        copy.start()
    for copy in copies[1:]:
        copy.wait()
    eye = diagonal()
    for group in range(src_ref.shape[0] // LANES):
        cols = slice(group * LANES, (group + 1) * LANES)
        square = to_lanes(squares(src_ref, group * LANES), eye)
        slope = slope_ref[group : group + 1, :]
        logmass = logmass_ref[group : group + 1, :]
        sum_ref[:, cols] = logmass + square
        line_ref[0:1, cols] = slope
        line_ref[1:2, cols] = slope * (logmass + square) + (logmass - square)
    copies[0].wait()
    for group in range(tgt_ref.shape[0] // LANES):
        at = group * LANES
        base = pot_ref[group : group + 1, :] + mass_ref[group : group + 1, :]
        offset_ref[:, at : at + LANES] = base - to_lanes(squares(tgt_ref, at), eye)
    put_offsets(offset_ref, column_ref, eye)
    lse_ref[...] = row_sums(src_ref[...], ((tgt_ref, column_ref),), z_ref)
    make_logits(src_ref[...], tgt_ref, offset_ref, own_z_ref)


def near_kernel(rows_ref, tgt_ref, offset_ref, held_ref, column_ref, lse_ref, z_ref):
    put_offsets(offset_ref, column_ref, diagonal())
    lse_ref[...] = merge(held_ref[...], row_sums(rows_ref[...], ((tgt_ref, column_ref),), z_ref))


def far_kernel(count, *refs):
    own_ref, own_column_ref, pair_ref, pair_column_ref, held_ref, line_ref = refs[count : count + 6]
    out_ref, z_ref = refs[count + 6 :]
    slots = count + 1
    out_ref[0:1, :] = held_ref[...]
    out_ref[slots : slots + 2, :] = line_ref[...]
    for slot in range(count):
        sides = ((own_ref, own_column_ref), (pair_ref, pair_column_ref))
        out_ref[slot + 1 : slot + 2, :] = row_sums(refs[slot][...], sides, z_ref)


def sum_columns(z_refs, offset, out_ref, off_ref, peak_ref, mass_ref):
    eye = diagonal()
    slots, src_count = offset.shape
    for slot in range(slots):
        for at in range(0, src_count, LANES):
            column = to_column(offset[slot : slot + 1, at : at + LANES] * LOG2_E, eye)
            off_ref[slot, at : at + LANES, :] = jnp.broadcast_to(column, (LANES, LANES))

    for group in range(out_ref.shape[0]):
        cols = slice(group * LANES, (group + 1) * LANES)
        for slot in range(slots):
            z = (z_refs[slot][:, cols] + off_ref[slot]).reshape(src_count // 8, 8, LANES)
            peak = jnp.max(z, axis=0)
            peak_ref[slot, :, cols] = peak
            mass_ref[slot, :, cols] = jnp.sum(jnp.exp2(z - peak), axis=0)
    peak = jnp.max(functools.reduce(jnp.maximum, [peak_ref[slot] for slot in range(slots)]), axis=0, keepdims=True)
    mass = sum(mass_ref[slot] * jnp.exp2(peak_ref[slot] - peak) for slot in range(slots))
    total = peak * LOG_2 + jnp.log(jnp.sum(mass, axis=0, keepdims=True))
    for group in range(out_ref.shape[0]):
        out_ref[group : group + 1, :] = total[:, group * LANES : (group + 1) * LANES]


def pair_kernel(slots, *refs):
    lse_ref, there_ref, slope_ref, shift_ref, out_ref, *scratch = refs[slots:]
    lse = merge(lse_ref[...], there_ref[...])
    sum_columns(refs[:slots], shift_ref[...] - slope_ref[...] * lse, out_ref, *scratch)


def own_kernel(turn, slots, *refs):
    z_refs, (lse_ref, there_ref, slope_ref, shift_ref, core_ref), refs = refs[:slots], refs[slots : slots + 5], refs[slots + 5 :]
    lse = merge(lse_ref[...], there_ref[...])
    if turn == 0:
        sum_ref, earlier_ref, out_ref, potential_ref, *scratch = refs
        potential_ref[...] = slope_ref[0:1, :] * (sum_ref[...] - lse[0:1, :])
    else:
        out_ref, *scratch = refs

    @pl.when(core_ref[0] == turn)
    def work():
        sum_columns(z_refs, shift_ref[...] - slope_ref[...] * lse, out_ref, *scratch)

    if turn == 0:

        @pl.when(core_ref[0] != turn)
        def hand_on():
            out_ref[...] = earlier_ref[...]


def f32(*shape):
    return jax.ShapeDtypeStruct(shape, jnp.float32)


def params(mebibytes):
    return pltpu.CompilerParams(vmem_limit_bytes=mebibytes * 1024 * 1024)


def shards(sources, targets, tgt_potential, src_logmass, tgt_logmass, src_exponent, tgt_exponent):
    src_count, width = sources.shape
    tgt_count = targets.shape[0]
    slabs = lax.axis_size("blk")
    sets = lax.axis_size("tsplit")
    chips = slabs // 2
    far = chips - 1
    groups = tgt_count // LANES
    src_groups = src_count // LANES
    assert chips > 1 and sets > 2 and chips & (chips - 1) == 0 and sets & (sets - 1) == 0

    def pair(value):
        return lax.ppermute(value, "blk", [(i, i ^ 1) for i in range(slabs)])

    def across(value, chip):
        return lax.ppermute(value, "blk", [(i, i ^ (2 * chip)) for i in range(slabs)])

    def along(value, step):
        return lax.ppermute(value, "tsplit", [(i, i ^ step) for i in range(sets)])

    def cost(blocks):
        pairs = blocks * src_count * tgt_count
        return pl.CostEstimate(flops=2 * pairs * width, bytes_accessed=2**20, transcendentals=pairs)

    core = lax.axis_index("blk") & 1
    core_word = core.astype(jnp.int32).reshape(1)
    pair_targets = pair(targets)
    inputs = (
        sources,
        targets,
        tgt_potential.reshape(groups, LANES),
        tgt_logmass.reshape(groups, LANES),
        src_exponent.reshape(src_groups, LANES),
        src_logmass.reshape(src_groups, LANES),
    )
    inputs = [pltpu.with_memory_space_constraint(x, pltpu.HBM) for x in inputs]

    product_space = pltpu.VMEM((2, PIECE, src_count), jnp.float32)

    def prepare_on(turn, *earlier):
        return pl.pallas_call(
            functools.partial(prepare_kernel, turn),
            out_shape=(
                jax.ShapeDtypeStruct(targets.shape, targets.dtype),
                f32(1, tgt_count),
                f32(tgt_count, LANES),
                f32(src_count, tgt_count),
                f32(1, src_count),
                f32(2, src_count),
                f32(1, src_count),
            ),
            in_specs=[SMEM] + [HBM] * 6 + [VMEM] * len(earlier),
            out_specs=(VMEM,) * 7,
            scratch_shapes=[pltpu.VMEM(x.shape, x.dtype) for x in (inputs[0], *inputs[2:])]
            + [product_space, pltpu.SemaphoreType.DMA((6,))],
            compiler_params=params(12),
            cost_estimate=cost(1),
            name=f"prepare_{turn}",
        )(core_word, *inputs, *earlier)

    earlier = prepare_on(1)
    first, sent = lax.optimization_barrier((earlier[6], sources))
    far_blocks = [across(sent, chip) for chip in range(1, chips)]
    held, offset, column, own_z, lse, line, src_sum = prepare_on(0, *earlier[:6], first)
    pair_offset = pair(offset)
    pair_column, lse = pl.pallas_call(
        near_kernel,
        out_shape=(f32(tgt_count, LANES), f32(1, src_count)),
        in_specs=[VMEM] * 4,
        out_specs=(VMEM,) * 2,
        scratch_shapes=[product_space],
        compiler_params=params(12),
        cost_estimate=cost(1),
        name="near_rows",
    )(sources, pair_targets, pair_offset, lse)
    far_lines = [across(line, chip) for chip in range(2, chips)]
    lse, *moved = lax.optimization_barrier((lse, *far_blocks, *far_lines))
    payload = pl.pallas_call(
        functools.partial(far_kernel, far),
        out_shape=f32(chips + 2, src_count),
        in_specs=[VMEM] * (far + 6),
        out_specs=VMEM,
        scratch_shapes=[product_space],
        compiler_params=params(12 + far),
        cost_estimate=cost(2 * far),
        name="far_rows",
    )(*moved[:far], held, column, pair_targets, pair_column, lse, line)

    payload, *blocks = lax.optimization_barrier((payload, sources, *moved[:far]))
    def logits(block, *sides):
        return pl.pallas_call(
            functools.partial(logits_kernel, len(sides) // 2),
            out_shape=(f32(src_count, tgt_count),) * (len(sides) // 2),
            in_specs=[VMEM] * (1 + len(sides)),
            out_specs=(VMEM,) * (len(sides) // 2),
            compiler_params=params(12),
            cost_estimate=cost(len(sides) // 2),
            name="logits",
        )(block, *sides)

    own_zs, pair_zs = [own_z], list(logits(blocks[0], pair_targets, pair_offset))
    for block in blocks[1:]:
        own_z, pair_z = logits(block, held, offset, pair_targets, pair_offset)
        own_zs.append(own_z)
        pair_zs.append(pair_z)

    def mirror(value, chip):
        return jnp.stack([value[slot ^ chip] for slot in range(chips)])

    lse = merge(payload[:chips], along(payload, sets // 2)[:chips])
    step = 2
    while 2 * step < sets:
        lse = merge(lse, along(lse, step))
        step *= 2
    chip = 2
    while chip < chips:
        lse = merge(lse, mirror(across(lse, chip), chip))
        chip *= 2
    payload = jnp.concatenate([lse, line])
    payload, *zs = lax.optimization_barrier((payload, *own_zs, *pair_zs))
    own_zs, pair_zs = zs[:chips], zs[chips:]
    other = across(payload, 1)
    beside = along(payload, 1)
    joined = lax.ppermute(
        payload,
        ("blk", "tsplit"),
        [(b * sets + z, (b ^ 2) * sets + (z ^ 1)) for b in range(slabs) for z in range(sets)],
    )
    lines = jnp.stack([line, joined[chips:]] + moved[far:], axis=1)
    lse = merge(lse, beside[:chips], mirror(joined, 1))
    there = mirror(other, 1)

    def columns(kernel, zs, *more, outs=(f32(groups, LANES),)):
        return pl.pallas_call(
            kernel,
            out_shape=outs,
            in_specs=[VMEM] * (chips + 4) + [SMEM] * min(1, len(more)) + [VMEM] * (len(more) - 1),
            out_specs=(VMEM,) * len(outs),
            scratch_shapes=[
                pltpu.VMEM((chips, src_count, LANES), jnp.float32),
                pltpu.VMEM((chips, 8, tgt_count), jnp.float32),
                pltpu.VMEM((chips, 8, tgt_count), jnp.float32),
            ],
            compiler_params=params(8 + 2 * chips),
            cost_estimate=pl.CostEstimate(
                flops=6 * chips * src_count * tgt_count,
                bytes_accessed=2**20,
                transcendentals=chips * src_count * tgt_count,
            ),
            name="columns",
        )(*zs, lse, there, lines[0], lines[1], *more)

    (pair_part,) = columns(functools.partial(pair_kernel, chips), pair_zs)
    (early_part,) = columns(functools.partial(own_kernel, 1, chips), own_zs, core_word)
    there, pair_part, early_part = lax.optimization_barrier((there, pair_part, early_part))
    home = pair(pair_part)
    own_part, src_potential = columns(
        functools.partial(own_kernel, 0, chips),
        own_zs,
        core_word,
        src_sum,
        early_part,
        outs=(f32(groups, LANES), f32(1, src_count)),
    )
    total = merge(own_part, home).reshape(tgt_count)
    tgt_update = tgt_exponent * (2.0 * tgt_logmass + tgt_potential - total)
    return (src_potential.reshape(src_count), tgt_update)


def solution(mesh):
    placed = (
        P(("groups", "blk"), None),
        P(("groups", "blk", "tsplit"), None),
        P(("groups", "blk", "tsplit")),
        P(("groups", "blk")),
        P(("groups", "blk", "tsplit")),
        P(("groups", "blk")),
        P(("groups", "blk", "tsplit")),
    )
    return jax.shard_map(
        shards,
        mesh=mesh,
        in_specs=placed,
        out_specs=(P(("groups", "blk")), P(("groups", "blk", "tsplit"))),
        check_vma=False,
    )
```

```python
import functools
import math

import jax
import jax.numpy as jnp
from jax import lax
from jax.experimental import pallas as pl
from jax.experimental.pallas import tpu as pltpu
from jax.sharding import PartitionSpec as P

EPSILON = 0.5
LOGIT_SCALE = 2.0 / EPSILON
LOG2_E = math.log2(math.e)
LOG_2 = math.log(2.0)
LANES = 128
CHUNK = 256
PIECE = 256
VMEM = pl.BlockSpec(memory_space=pltpu.VMEM)
SMEM = pl.BlockSpec(memory_space=pltpu.SMEM)
HBM = pl.BlockSpec(memory_space=pltpu.HBM)
NT_DIMS = (((1,), (1,)), ((), ()))


def diagonal():
    rows = lax.broadcasted_iota(jnp.int32, (LANES, LANES), 0)
    cols = lax.broadcasted_iota(jnp.int32, (LANES, LANES), 1)
    return rows == cols


def to_lanes(column, eye):
    return jnp.sum(jnp.where(eye, column, 0.0), axis=0, keepdims=True)


def to_column(lanes, eye):
    return jnp.sum(jnp.where(eye, lanes, 0.0), axis=1, keepdims=True)


def merge(*parts):
    peak = functools.reduce(jnp.maximum, parts)
    return peak + jnp.log(sum(jnp.exp(part - peak) for part in parts))


def squares(rows_ref, at):
    rows = rows_ref[at : at + LANES, :].astype(jnp.float32)
    return jnp.sum(rows * rows, axis=1, keepdims=True) / EPSILON


def row_sums(rows, sides, z_ref):
    rows = rows * LOGIT_SCALE
    pieces = [(side, at) for side, (tgt_ref, _) in enumerate(sides) for at in range(0, tgt_ref.shape[0], PIECE)]

    def product(index):
        side, at = pieces[index]
        part = sides[side][0][at : at + PIECE, :]
        z_ref[index % 2] = lax.dot_general(part, rows, NT_DIMS, preferred_element_type=jnp.float32)

    peaks, masses = [], []

    def absorb(index):
        side, at = pieces[index]
        for inner in range(0, PIECE, LANES):
            offset = sides[side][1][at + inner : at + inner + LANES, :]
            offset = jnp.concatenate([offset] * (rows.shape[0] // LANES), axis=1)
            z = z_ref[index % 2, inner : inner + LANES, :] * LOG2_E + offset
            z = z.reshape(LANES // 8, 8, rows.shape[0])
            peaks.append(jnp.max(z, axis=0))
            masses.append(jnp.sum(jnp.exp2(z - peaks[-1]), axis=0))

    product(0)
    for index in range(len(pieces)):
        if index + 1 < len(pieces):
            product(index + 1)
        absorb(index)
    peak = jnp.max(functools.reduce(jnp.maximum, peaks), axis=0, keepdims=True)
    mass = sum(mass * jnp.exp2(high - peak) for high, mass in zip(peaks, masses))
    return peak * LOG_2 + jnp.log(jnp.sum(mass, axis=0, keepdims=True))


def put_offsets(offset_ref, column_ref, eye):
    for at in range(0, offset_ref.shape[1], LANES):
        column = to_column(offset_ref[:, at : at + LANES] * LOG2_E, eye)
        column_ref[at : at + LANES, :] = jnp.broadcast_to(column, (LANES, LANES))


def make_logits(rows, tgt_ref, offset_ref, z_ref):
    rows = rows * LOGIT_SCALE
    for at in range(0, tgt_ref.shape[0], CHUNK):
        cols = slice(at, at + CHUNK)
        dots = lax.dot_general(rows, tgt_ref[cols, :], NT_DIMS, preferred_element_type=jnp.float32)
        z_ref[:, cols] = (dots + offset_ref[:, cols]) * LOG2_E


def logits_kernel(sides, rows_ref, *refs):
    for side in range(sides):
        make_logits(rows_ref[...], refs[2 * side], refs[2 * side + 1], refs[2 * sides + side])


def prepare_kernel(turn, core_ref, *refs):
    inputs, refs = refs[:6], refs[6:]
    earlier, refs = refs[: 7 * (1 - turn)], refs[7 * (1 - turn) :]
    outs, scratch = refs[:7], refs[7:]

    @pl.when(core_ref[0] == turn)
    def work():
        prepare(*inputs, *outs, *scratch)

    if earlier:

        @pl.when(core_ref[0] != turn)
        def hand_on():
            for source, target in zip(earlier, outs):
                target[...] = source[...]


def prepare(
    src_hbm, tgt_hbm, pot_hbm, mass_hbm, slope_hbm, logmass_hbm,
    tgt_ref, offset_ref, column_ref, own_z_ref, lse_ref, line_ref, sum_ref,
    src_ref, pot_ref, mass_ref, slope_ref, logmass_ref, z_ref, sems,
):
    pairs = (
        (tgt_hbm, tgt_ref), (src_hbm, src_ref), (pot_hbm, pot_ref),
        (mass_hbm, mass_ref), (slope_hbm, slope_ref), (logmass_hbm, logmass_ref),
    )
    copies = [pltpu.make_async_copy(source, target, sems.at[at]) for at, (source, target) in enumerate(pairs)]
    for copy in copies:
        copy.start()
    for copy in copies[1:]:
        copy.wait()
    eye = diagonal()
    for group in range(src_ref.shape[0] // LANES):
        cols = slice(group * LANES, (group + 1) * LANES)
        square = to_lanes(squares(src_ref, group * LANES), eye)
        slope = slope_ref[group : group + 1, :]
        logmass = logmass_ref[group : group + 1, :]
        sum_ref[:, cols] = logmass + square
        line_ref[0:1, cols] = slope
        line_ref[1:2, cols] = slope * (logmass + square) + (logmass - square)
    copies[0].wait()
    for group in range(tgt_ref.shape[0] // LANES):
        at = group * LANES
        base = pot_ref[group : group + 1, :] + mass_ref[group : group + 1, :]
        offset_ref[:, at : at + LANES] = base - to_lanes(squares(tgt_ref, at), eye)
    put_offsets(offset_ref, column_ref, eye)
    lse_ref[...] = row_sums(src_ref[...], ((tgt_ref, column_ref),), z_ref)
    make_logits(src_ref[...], tgt_ref, offset_ref, own_z_ref)


def near_kernel(rows_ref, tgt_ref, offset_ref, held_ref, column_ref, lse_ref, z_ref):
    put_offsets(offset_ref, column_ref, diagonal())
    lse_ref[...] = merge(held_ref[...], row_sums(rows_ref[...], ((tgt_ref, column_ref),), z_ref))


def far_kernel(count, *refs):
    own_ref, own_column_ref, pair_ref, pair_column_ref, held_ref, line_ref = refs[count : count + 6]
    out_ref, mirrored_ref, z_ref = refs[count + 6 :]
    slots = count + 1
    for ref in (out_ref, mirrored_ref):
        ref[slots : slots + 2, :] = line_ref[...]
    for slot in range(slots):
        if slot == 0:
            lse = held_ref[...]
        else:
            sides = ((own_ref, own_column_ref), (pair_ref, pair_column_ref))
            lse = row_sums(refs[slot - 1][...], sides, z_ref)
        out_ref[slot : slot + 1, :] = lse
        mirrored_ref[slot ^ 1 : (slot ^ 1) + 1, :] = lse


def sum_columns(z_refs, offset, out_ref, off_ref, peak_ref, mass_ref):
    eye = diagonal()
    slots, src_count = offset.shape
    for slot in range(slots):
        for at in range(0, src_count, LANES):
            column = to_column(offset[slot : slot + 1, at : at + LANES] * LOG2_E, eye)
            off_ref[slot, at : at + LANES, :] = jnp.broadcast_to(column, (LANES, LANES))

    for group in range(out_ref.shape[0]):
        cols = slice(group * LANES, (group + 1) * LANES)
        for slot in range(slots):
            z = (z_refs[slot][:, cols] + off_ref[slot]).reshape(src_count // 8, 8, LANES)
            peak = jnp.max(z, axis=0)
            peak_ref[slot, :, cols] = peak
            mass_ref[slot, :, cols] = jnp.sum(jnp.exp2(z - peak), axis=0)
    peak = jnp.max(functools.reduce(jnp.maximum, [peak_ref[slot] for slot in range(slots)]), axis=0, keepdims=True)
    mass = sum(mass_ref[slot] * jnp.exp2(peak_ref[slot] - peak) for slot in range(slots))
    total = peak * LOG_2 + jnp.log(jnp.sum(mass, axis=0, keepdims=True))
    for group in range(out_ref.shape[0]):
        out_ref[group : group + 1, :] = total[:, group * LANES : (group + 1) * LANES]


def pair_kernel(slots, *refs):
    lse_ref, there_ref, slope_ref, shift_ref, out_ref, *scratch = refs[slots:]
    lse = merge(lse_ref[...], there_ref[...])
    sum_columns(refs[:slots], shift_ref[...] - slope_ref[...] * lse, out_ref, *scratch)


def own_kernel(turn, slots, *refs):
    z_refs, (lse_ref, there_ref, slope_ref, shift_ref, core_ref), refs = refs[:slots], refs[slots : slots + 5], refs[slots + 5 :]
    lse = merge(lse_ref[...], there_ref[...])
    if turn == 0:
        sum_ref, earlier_ref, out_ref, potential_ref, *scratch = refs
        potential_ref[...] = slope_ref[0:1, :] * (sum_ref[...] - lse[0:1, :])
    else:
        out_ref, *scratch = refs

    @pl.when(core_ref[0] == turn)
    def work():
        sum_columns(z_refs, shift_ref[...] - slope_ref[...] * lse, out_ref, *scratch)

    if turn == 0:

        @pl.when(core_ref[0] != turn)
        def hand_on():
            out_ref[...] = earlier_ref[...]


def f32(*shape):
    return jax.ShapeDtypeStruct(shape, jnp.float32)


def params(mebibytes):
    return pltpu.CompilerParams(vmem_limit_bytes=mebibytes * 1024 * 1024)


def shards(sources, targets, tgt_potential, src_logmass, tgt_logmass, src_exponent, tgt_exponent):
    src_count, width = sources.shape
    tgt_count = targets.shape[0]
    slabs = lax.axis_size("blk")
    sets = lax.axis_size("tsplit")
    chips = slabs // 2
    far = chips - 1
    groups = tgt_count // LANES
    src_groups = src_count // LANES
    assert chips > 1 and sets > 2 and chips & (chips - 1) == 0 and sets & (sets - 1) == 0

    def pair(value):
        return lax.ppermute(value, "blk", [(i, i ^ 1) for i in range(slabs)])

    def across(value, chip):
        return lax.ppermute(value, "blk", [(i, i ^ (2 * chip)) for i in range(slabs)])

    def along(value, step):
        return lax.ppermute(value, "tsplit", [(i, i ^ step) for i in range(sets)])

    def cost(blocks):
        pairs = blocks * src_count * tgt_count
        return pl.CostEstimate(flops=2 * pairs * width, bytes_accessed=2**20, transcendentals=pairs)

    core = lax.axis_index("blk") & 1
    core_word = core.astype(jnp.int32).reshape(1)
    pair_targets = pair(targets)
    inputs = (
        sources,
        targets,
        tgt_potential.reshape(groups, LANES),
        tgt_logmass.reshape(groups, LANES),
        src_exponent.reshape(src_groups, LANES),
        src_logmass.reshape(src_groups, LANES),
    )
    inputs = [pltpu.with_memory_space_constraint(x, pltpu.HBM) for x in inputs]

    product_space = pltpu.VMEM((2, PIECE, src_count), jnp.float32)

    def prepare_on(turn, *earlier):
        return pl.pallas_call(
            functools.partial(prepare_kernel, turn),
            out_shape=(
                jax.ShapeDtypeStruct(targets.shape, targets.dtype),
                f32(1, tgt_count),
                f32(tgt_count, LANES),
                f32(src_count, tgt_count),
                f32(1, src_count),
                f32(2, src_count),
                f32(1, src_count),
            ),
            in_specs=[SMEM] + [HBM] * 6 + [VMEM] * len(earlier),
            out_specs=(VMEM,) * 7,
            scratch_shapes=[pltpu.VMEM(x.shape, x.dtype) for x in (inputs[0], *inputs[2:])]
            + [product_space, pltpu.SemaphoreType.DMA((6,))],
            compiler_params=params(12),
            cost_estimate=cost(1),
            name=f"prepare_{turn}",
        )(core_word, *inputs, *earlier)

    earlier = prepare_on(1)
    first, sent = lax.optimization_barrier((earlier[6], sources))
    far_blocks = [across(sent, chip) for chip in range(1, chips)]
    held, offset, column, own_z, lse, line, src_sum = prepare_on(0, *earlier[:6], first)
    pair_offset = pair(offset)
    pair_column, lse = pl.pallas_call(
        near_kernel,
        out_shape=(f32(tgt_count, LANES), f32(1, src_count)),
        in_specs=[VMEM] * 4,
        out_specs=(VMEM,) * 2,
        scratch_shapes=[product_space],
        compiler_params=params(12),
        cost_estimate=cost(1),
        name="near_rows",
    )(sources, pair_targets, pair_offset, lse)
    far_lines = [across(line, chip) for chip in range(2, chips)]
    lse, *moved = lax.optimization_barrier((lse, *far_blocks, *far_lines))
    payload, mirrored = pl.pallas_call(
        functools.partial(far_kernel, far),
        out_shape=(f32(chips + 2, src_count),) * 2,
        in_specs=[VMEM] * (far + 6),
        out_specs=(VMEM,) * 2,
        scratch_shapes=[product_space],
        compiler_params=params(12 + far),
        cost_estimate=cost(2 * far),
        name="far_rows",
    )(*moved[:far], held, column, pair_targets, pair_column, lse, line)

    payload, mirrored, *blocks = lax.optimization_barrier((payload, mirrored, sources, *moved[:far]))
    def logits(block, *sides):
        return pl.pallas_call(
            functools.partial(logits_kernel, len(sides) // 2),
            out_shape=(f32(src_count, tgt_count),) * (len(sides) // 2),
            in_specs=[VMEM] * (1 + len(sides)),
            out_specs=(VMEM,) * (len(sides) // 2),
            compiler_params=params(12),
            cost_estimate=cost(len(sides) // 2),
            name="logits",
        )(block, *sides)

    own_zs, pair_zs = [own_z], list(logits(blocks[0], pair_targets, pair_offset))
    for block in blocks[1:]:
        own_z, pair_z = logits(block, held, offset, pair_targets, pair_offset)
        own_zs.append(own_z)
        pair_zs.append(pair_z)

    def mirror(value, chip):
        return jnp.stack([value[slot ^ chip] for slot in range(chips)])

    other = across(mirrored, 1)
    beside = along(payload, 1)
    joined = lax.ppermute(
        payload,
        ("blk", "tsplit"),
        [(b * sets + z, (b ^ 2) * sets + (z ^ 1)) for b in range(slabs) for z in range(sets)],
    )
    lines = jnp.stack([line, joined[chips:]] + moved[far:], axis=1)
    lse = merge(payload[:chips], other[:chips], beside[:chips], mirror(joined, 1))
    chip = 2
    while chip < chips:
        lse = merge(lse, mirror(across(lse, chip), chip))
        chip *= 2
    step = 2
    while 2 * step < sets:
        lse = merge(lse, along(lse, step))
        step *= 2
    there = along(lse, step)

    def columns(kernel, zs, *more, outs=(f32(groups, LANES),)):
        return pl.pallas_call(
            kernel,
            out_shape=outs,
            in_specs=[VMEM] * (chips + 4) + [SMEM] * min(1, len(more)) + [VMEM] * (len(more) - 1),
            out_specs=(VMEM,) * len(outs),
            scratch_shapes=[
                pltpu.VMEM((chips, src_count, LANES), jnp.float32),
                pltpu.VMEM((chips, 8, tgt_count), jnp.float32),
                pltpu.VMEM((chips, 8, tgt_count), jnp.float32),
            ],
            compiler_params=params(8 + 2 * chips),
            cost_estimate=pl.CostEstimate(
                flops=6 * chips * src_count * tgt_count,
                bytes_accessed=2**20,
                transcendentals=chips * src_count * tgt_count,
            ),
            name="columns",
        )(*zs, lse, there, lines[0], lines[1], *more)

    (pair_part,) = columns(functools.partial(pair_kernel, chips), pair_zs)
    (early_part,) = columns(functools.partial(own_kernel, 1, chips), own_zs, core_word)
    there, pair_part, early_part = lax.optimization_barrier((there, pair_part, early_part))
    home = pair(pair_part)
    own_part, src_potential = columns(
        functools.partial(own_kernel, 0, chips),
        own_zs,
        core_word,
        src_sum,
        early_part,
        outs=(f32(groups, LANES), f32(1, src_count)),
    )
    total = merge(own_part, home).reshape(tgt_count)
    tgt_update = tgt_exponent * (2.0 * tgt_logmass + tgt_potential - total)
    return (src_potential.reshape(src_count), tgt_update)


def solution(mesh):
    placed = (
        P(("groups", "blk"), None),
        P(("groups", "blk", "tsplit"), None),
        P(("groups", "blk", "tsplit")),
        P(("groups", "blk")),
        P(("groups", "blk", "tsplit")),
        P(("groups", "blk")),
        P(("groups", "blk", "tsplit")),
    )
    return jax.shard_map(
        shards,
        mesh=mesh,
        in_specs=placed,
        out_specs=(P(("groups", "blk")), P(("groups", "blk", "tsplit"))),
        check_vma=False,
    )
```

```python
import functools
import math

import jax
import jax.numpy as jnp
from jax import lax
from jax.experimental import pallas as pl
from jax.experimental.pallas import tpu as pltpu
from jax.sharding import PartitionSpec as P

EPSILON = 0.5
LOGIT_SCALE = 2.0 / EPSILON
LOG2_E = math.log2(math.e)
LOG_2 = math.log(2.0)
LANES = 128
CHUNK = 256
PIECE = 256
VMEM = pl.BlockSpec(memory_space=pltpu.VMEM)
SMEM = pl.BlockSpec(memory_space=pltpu.SMEM)
HBM = pl.BlockSpec(memory_space=pltpu.HBM)
NT_DIMS = (((1,), (1,)), ((), ()))


def diagonal():
    rows = lax.broadcasted_iota(jnp.int32, (LANES, LANES), 0)
    cols = lax.broadcasted_iota(jnp.int32, (LANES, LANES), 1)
    return rows == cols


def to_lanes(column, eye):
    return jnp.sum(jnp.where(eye, column, 0.0), axis=0, keepdims=True)


def to_column(lanes, eye):
    return jnp.sum(jnp.where(eye, lanes, 0.0), axis=1, keepdims=True)


def merge(*parts):
    peak = functools.reduce(jnp.maximum, parts)
    return peak + jnp.log(sum(jnp.exp(part - peak) for part in parts))


def squares(rows_ref, at):
    rows = rows_ref[at : at + LANES, :].astype(jnp.float32)
    return jnp.sum(rows * rows, axis=1, keepdims=True) / EPSILON


def row_sums(rows, sides, z_ref):
    rows = rows * LOGIT_SCALE
    pieces = [(side, at) for side, (tgt_ref, _) in enumerate(sides) for at in range(0, tgt_ref.shape[0], PIECE)]

    def product(index):
        side, at = pieces[index]
        part = sides[side][0][at : at + PIECE, :]
        z_ref[index % 2] = lax.dot_general(part, rows, NT_DIMS, preferred_element_type=jnp.float32)

    peaks, masses = [], []

    def absorb(index):
        side, at = pieces[index]
        for inner in range(0, PIECE, LANES):
            offset = sides[side][1][at + inner : at + inner + LANES, :]
            offset = jnp.concatenate([offset] * (rows.shape[0] // LANES), axis=1)
            z = z_ref[index % 2, inner : inner + LANES, :] * LOG2_E + offset
            z = z.reshape(LANES // 8, 8, rows.shape[0])
            peaks.append(jnp.max(z, axis=0))
            masses.append(jnp.sum(jnp.exp2(z - peaks[-1]), axis=0))

    product(0)
    for index in range(len(pieces)):
        if index + 1 < len(pieces):
            product(index + 1)
        absorb(index)
    peak = jnp.max(functools.reduce(jnp.maximum, peaks), axis=0, keepdims=True)
    mass = sum(mass * jnp.exp2(high - peak) for high, mass in zip(peaks, masses))
    return peak * LOG_2 + jnp.log(jnp.sum(mass, axis=0, keepdims=True))


def put_offsets(offset_ref, column_ref, eye):
    for at in range(0, offset_ref.shape[1], LANES):
        column = to_column(offset_ref[:, at : at + LANES] * LOG2_E, eye)
        column_ref[at : at + LANES, :] = jnp.broadcast_to(column, (LANES, LANES))


def make_logits(rows, tgt_ref, offset_ref, z_ref):
    rows = rows * LOGIT_SCALE
    for at in range(0, tgt_ref.shape[0], CHUNK):
        cols = slice(at, at + CHUNK)
        dots = lax.dot_general(rows, tgt_ref[cols, :], NT_DIMS, preferred_element_type=jnp.float32)
        z_ref[:, cols] = (dots + offset_ref[:, cols]) * LOG2_E


def logits_kernel(sides, rows_ref, *refs):
    for side in range(sides):
        make_logits(rows_ref[...], refs[2 * side], refs[2 * side + 1], refs[2 * sides + side])


def prepare_kernel(turn, core_ref, *refs):
    inputs, refs = refs[:6], refs[6:]
    earlier, refs = refs[: 7 * (1 - turn)], refs[7 * (1 - turn) :]
    outs, scratch = refs[:7], refs[7:]

    @pl.when(core_ref[0] == turn)
    def work():
        prepare(*inputs, *outs, *scratch)

    if earlier:

        @pl.when(core_ref[0] != turn)
        def hand_on():
            for source, target in zip(earlier, outs):
                target[...] = source[...]


def prepare(
    src_hbm, tgt_hbm, pot_hbm, mass_hbm, slope_hbm, logmass_hbm,
    tgt_ref, offset_ref, column_ref, own_z_ref, lse_ref, line_ref, sum_ref,
    src_ref, pot_ref, mass_ref, slope_ref, logmass_ref, z_ref, sems,
):
    pairs = (
        (tgt_hbm, tgt_ref), (src_hbm, src_ref), (pot_hbm, pot_ref),
        (mass_hbm, mass_ref), (slope_hbm, slope_ref), (logmass_hbm, logmass_ref),
    )
    copies = [pltpu.make_async_copy(source, target, sems.at[at]) for at, (source, target) in enumerate(pairs)]
    for copy in copies:
        copy.start()
    for copy in copies[1:]:
        copy.wait()
    eye = diagonal()
    for group in range(src_ref.shape[0] // LANES):
        cols = slice(group * LANES, (group + 1) * LANES)
        square = to_lanes(squares(src_ref, group * LANES), eye)
        slope = slope_ref[group : group + 1, :]
        logmass = logmass_ref[group : group + 1, :]
        sum_ref[:, cols] = logmass + square
        line_ref[0:1, cols] = slope
        line_ref[1:2, cols] = slope * (logmass + square) + (logmass - square)
    copies[0].wait()
    for group in range(tgt_ref.shape[0] // LANES):
        at = group * LANES
        base = pot_ref[group : group + 1, :] + mass_ref[group : group + 1, :]
        offset_ref[:, at : at + LANES] = base - to_lanes(squares(tgt_ref, at), eye)
    put_offsets(offset_ref, column_ref, eye)
    lse_ref[...] = row_sums(src_ref[...], ((tgt_ref, column_ref),), z_ref)
    make_logits(src_ref[...], tgt_ref, offset_ref, own_z_ref)


def near_kernel(rows_ref, tgt_ref, offset_ref, held_ref, column_ref, lse_ref, z_ref):
    put_offsets(offset_ref, column_ref, diagonal())
    lse_ref[...] = merge(held_ref[...], row_sums(rows_ref[...], ((tgt_ref, column_ref),), z_ref))


def far_kernel(count, *refs):
    own_ref, own_column_ref, pair_ref, pair_column_ref, held_ref, line_ref = refs[count : count + 6]
    out_ref, z_ref = refs[count + 6 :]
    slots = count + 1
    out_ref[0:1, :] = held_ref[...]
    out_ref[slots : slots + 2, :] = line_ref[...]
    for slot in range(count):
        sides = ((own_ref, own_column_ref), (pair_ref, pair_column_ref))
        out_ref[slot + 1 : slot + 2, :] = row_sums(refs[slot][...], sides, z_ref)


def sum_columns(z_refs, offset, out_ref, off_ref, peak_ref, mass_ref):
    eye = diagonal()
    slots, src_count = offset.shape
    for slot in range(slots):
        for at in range(0, src_count, LANES):
            column = to_column(offset[slot : slot + 1, at : at + LANES] * LOG2_E, eye)
            off_ref[slot, at : at + LANES, :] = jnp.broadcast_to(column, (LANES, LANES))

    parts = [(slot, at) for slot in range(slots) for at in range(0, src_count, LANES)]
    for left in range(0, z_refs[0].shape[1], CHUNK):
        cols = slice(left, left + CHUNK)
        for part, (slot, at) in enumerate(parts):
            rows = slice(at, at + LANES)
            offsets = jnp.concatenate([off_ref[slot, rows, :]] * (CHUNK // LANES), axis=1)
            z = (z_refs[slot][rows, cols] + offsets).reshape(LANES // 8, 8, CHUNK)
            peak = jnp.max(z, axis=0)
            peak_ref[part, :, cols] = peak
            mass_ref[part, :, cols] = jnp.sum(jnp.exp2(z - peak), axis=0)
    every = range(len(parts))
    peak = jnp.max(functools.reduce(jnp.maximum, [peak_ref[part] for part in every]), axis=0, keepdims=True)
    mass = sum(mass_ref[part] * jnp.exp2(peak_ref[part] - peak) for part in every)
    total = peak * LOG_2 + jnp.log(jnp.sum(mass, axis=0, keepdims=True))
    for group in range(out_ref.shape[0]):
        out_ref[group : group + 1, :] = total[:, group * LANES : (group + 1) * LANES]


def pair_kernel(slots, *refs):
    lse_ref, there_ref, slope_ref, shift_ref, out_ref, *scratch = refs[slots:]
    lse = merge(lse_ref[...], there_ref[...])
    sum_columns(refs[:slots], shift_ref[...] - slope_ref[...] * lse, out_ref, *scratch)


def own_kernel(turn, slots, *refs):
    z_refs, (lse_ref, there_ref, slope_ref, shift_ref, core_ref), refs = refs[:slots], refs[slots : slots + 5], refs[slots + 5 :]
    lse = merge(lse_ref[...], there_ref[...])
    if turn == 0:
        sum_ref, earlier_ref, out_ref, potential_ref, *scratch = refs
        potential_ref[...] = slope_ref[0:1, :] * (sum_ref[...] - lse[0:1, :])
    else:
        out_ref, *scratch = refs

    @pl.when(core_ref[0] == turn)
    def work():
        sum_columns(z_refs, shift_ref[...] - slope_ref[...] * lse, out_ref, *scratch)

    if turn == 0:

        @pl.when(core_ref[0] != turn)
        def hand_on():
            out_ref[...] = earlier_ref[...]


def f32(*shape):
    return jax.ShapeDtypeStruct(shape, jnp.float32)


def params(mebibytes):
    return pltpu.CompilerParams(vmem_limit_bytes=mebibytes * 1024 * 1024)


def shards(sources, targets, tgt_potential, src_logmass, tgt_logmass, src_exponent, tgt_exponent):
    src_count, width = sources.shape
    tgt_count = targets.shape[0]
    slabs = lax.axis_size("blk")
    sets = lax.axis_size("tsplit")
    chips = slabs // 2
    far = chips - 1
    groups = tgt_count // LANES
    src_groups = src_count // LANES
    assert chips > 1 and sets > 2 and chips & (chips - 1) == 0 and sets & (sets - 1) == 0

    def pair(value):
        return lax.ppermute(value, "blk", [(i, i ^ 1) for i in range(slabs)])

    def across(value, chip):
        return lax.ppermute(value, "blk", [(i, i ^ (2 * chip)) for i in range(slabs)])

    def along(value, step):
        return lax.ppermute(value, "tsplit", [(i, i ^ step) for i in range(sets)])

    def cost(blocks):
        pairs = blocks * src_count * tgt_count
        return pl.CostEstimate(flops=2 * pairs * width, bytes_accessed=2**20, transcendentals=pairs)

    core = lax.axis_index("blk") & 1
    core_word = core.astype(jnp.int32).reshape(1)
    pair_targets = pair(targets)
    inputs = (
        sources,
        targets,
        tgt_potential.reshape(groups, LANES),
        tgt_logmass.reshape(groups, LANES),
        src_exponent.reshape(src_groups, LANES),
        src_logmass.reshape(src_groups, LANES),
    )
    inputs = [pltpu.with_memory_space_constraint(x, pltpu.HBM) for x in inputs]

    product_space = pltpu.VMEM((2, PIECE, src_count), jnp.float32)

    def prepare_on(turn, *earlier):
        return pl.pallas_call(
            functools.partial(prepare_kernel, turn),
            out_shape=(
                jax.ShapeDtypeStruct(targets.shape, targets.dtype),
                f32(1, tgt_count),
                f32(tgt_count, LANES),
                f32(src_count, tgt_count),
                f32(1, src_count),
                f32(2, src_count),
                f32(1, src_count),
            ),
            in_specs=[SMEM] + [HBM] * 6 + [VMEM] * len(earlier),
            out_specs=(VMEM,) * 7,
            scratch_shapes=[pltpu.VMEM(x.shape, x.dtype) for x in (inputs[0], *inputs[2:])]
            + [product_space, pltpu.SemaphoreType.DMA((6,))],
            compiler_params=params(12),
            cost_estimate=cost(1),
            name=f"prepare_{turn}",
        )(core_word, *inputs, *earlier)

    earlier = prepare_on(1)
    first, sent = lax.optimization_barrier((earlier[6], sources))
    far_blocks = [across(sent, chip) for chip in range(1, chips)]
    held, offset, column, own_z, lse, line, src_sum = prepare_on(0, *earlier[:6], first)
    pair_offset = pair(offset)
    pair_column, lse = pl.pallas_call(
        near_kernel,
        out_shape=(f32(tgt_count, LANES), f32(1, src_count)),
        in_specs=[VMEM] * 4,
        out_specs=(VMEM,) * 2,
        scratch_shapes=[product_space],
        compiler_params=params(12),
        cost_estimate=cost(1),
        name="near_rows",
    )(sources, pair_targets, pair_offset, lse)
    far_lines = [across(line, chip) for chip in range(2, chips)]
    lse, *moved = lax.optimization_barrier((lse, *far_blocks, *far_lines))
    payload = pl.pallas_call(
        functools.partial(far_kernel, far),
        out_shape=f32(chips + 2, src_count),
        in_specs=[VMEM] * (far + 6),
        out_specs=VMEM,
        scratch_shapes=[product_space],
        compiler_params=params(12 + far),
        cost_estimate=cost(2 * far),
        name="far_rows",
    )(*moved[:far], held, column, pair_targets, pair_column, lse, line)

    payload, *blocks = lax.optimization_barrier((payload, sources, *moved[:far]))
    def logits(block, *sides):
        return pl.pallas_call(
            functools.partial(logits_kernel, len(sides) // 2),
            out_shape=(f32(src_count, tgt_count),) * (len(sides) // 2),
            in_specs=[VMEM] * (1 + len(sides)),
            out_specs=(VMEM,) * (len(sides) // 2),
            compiler_params=params(12),
            cost_estimate=cost(len(sides) // 2),
            name="logits",
        )(block, *sides)

    own_zs, pair_zs = [own_z], list(logits(blocks[0], pair_targets, pair_offset))
    for block in blocks[1:]:
        own_z, pair_z = logits(block, held, offset, pair_targets, pair_offset)
        own_zs.append(own_z)
        pair_zs.append(pair_z)

    def mirror(value, chip):
        return jnp.stack([value[slot ^ chip] for slot in range(chips)])

    other = across(payload, 1)
    beside = along(payload, 1)
    joined = lax.ppermute(
        payload,
        ("blk", "tsplit"),
        [(b * sets + z, (b ^ 2) * sets + (z ^ 1)) for b in range(slabs) for z in range(sets)],
    )
    lines = jnp.stack([line, other[chips:]] + moved[far:], axis=1)
    lse = merge(payload[:chips], mirror(other, 1), beside[:chips], mirror(joined, 1))
    chip = 2
    while chip < chips:
        lse = merge(lse, mirror(across(lse, chip), chip))
        chip *= 2
    step = 2
    while 2 * step < sets:
        lse = merge(lse, along(lse, step))
        step *= 2
    there = along(lse, step)

    def columns(kernel, zs, *more, outs=(f32(groups, LANES),)):
        return pl.pallas_call(
            kernel,
            out_shape=outs,
            in_specs=[VMEM] * (chips + 4) + [SMEM] * min(1, len(more)) + [VMEM] * (len(more) - 1),
            out_specs=(VMEM,) * len(outs),
            scratch_shapes=[
                pltpu.VMEM((chips, src_count, LANES), jnp.float32),
                pltpu.VMEM((chips * src_groups, 8, tgt_count), jnp.float32),
                pltpu.VMEM((chips * src_groups, 8, tgt_count), jnp.float32),
            ],
            compiler_params=params(8 + 2 * chips),
            cost_estimate=pl.CostEstimate(
                flops=6 * chips * src_count * tgt_count,
                bytes_accessed=2**20,
                transcendentals=chips * src_count * tgt_count,
            ),
            name="columns",
        )(*zs, lse, there, lines[0], lines[1], *more)

    (pair_part,) = columns(functools.partial(pair_kernel, chips), pair_zs)
    (early_part,) = columns(functools.partial(own_kernel, 1, chips), own_zs, core_word)
    there, pair_part, early_part = lax.optimization_barrier((there, pair_part, early_part))
    home = pair(pair_part)
    own_part, src_potential = columns(
        functools.partial(own_kernel, 0, chips),
        own_zs,
        core_word,
        src_sum,
        early_part,
        outs=(f32(groups, LANES), f32(1, src_count)),
    )
    total = merge(own_part, home).reshape(tgt_count)
    tgt_update = tgt_exponent * (2.0 * tgt_logmass + tgt_potential - total)
    return (src_potential.reshape(src_count), tgt_update)


def solution(mesh):
    placed = (
        P(("groups", "blk"), None),
        P(("groups", "blk", "tsplit"), None),
        P(("groups", "blk", "tsplit")),
        P(("groups", "blk")),
        P(("groups", "blk", "tsplit")),
        P(("groups", "blk")),
        P(("groups", "blk", "tsplit")),
    )
    return jax.shard_map(
        shards,
        mesh=mesh,
        in_specs=placed,
        out_specs=(P(("groups", "blk")), P(("groups", "blk", "tsplit"))),
        check_vma=False,
    )
```

```python
import functools
import math

import jax
import jax.numpy as jnp
from jax import lax
from jax.experimental import pallas as pl
from jax.experimental.pallas import tpu as pltpu
from jax.sharding import PartitionSpec as P

EPSILON = 0.5
LOGIT_SCALE = 2.0 / EPSILON
LOG2_E = math.log2(math.e)
LOG_2 = math.log(2.0)
LANES = 128
CHUNK = 256
PIECE = 256
VMEM = pl.BlockSpec(memory_space=pltpu.VMEM)
SMEM = pl.BlockSpec(memory_space=pltpu.SMEM)
HBM = pl.BlockSpec(memory_space=pltpu.HBM)
NT_DIMS = (((1,), (1,)), ((), ()))


def diagonal():
    rows = lax.broadcasted_iota(jnp.int32, (LANES, LANES), 0)
    cols = lax.broadcasted_iota(jnp.int32, (LANES, LANES), 1)
    return rows == cols


def to_lanes(column, eye):
    return jnp.sum(jnp.where(eye, column, 0.0), axis=0, keepdims=True)


def to_column(lanes, eye):
    return jnp.sum(jnp.where(eye, lanes, 0.0), axis=1, keepdims=True)


def merge(*parts):
    peak = functools.reduce(jnp.maximum, parts)
    return peak + jnp.log(sum(jnp.exp(part - peak) for part in parts))


def squares(rows_ref, at):
    rows = rows_ref[at : at + LANES, :].astype(jnp.float32)
    return jnp.sum(rows * rows, axis=1, keepdims=True) / EPSILON


def row_sums(rows, sides, z_ref):
    rows = rows * LOGIT_SCALE
    pieces = [(side, at) for side, (tgt_ref, _) in enumerate(sides) for at in range(0, tgt_ref.shape[0], PIECE)]

    def product(index):
        side, at = pieces[index]
        part = sides[side][0][at : at + PIECE, :]
        z_ref[index % 2] = lax.dot_general(part, rows, NT_DIMS, preferred_element_type=jnp.float32)

    peaks, masses = [], []

    def absorb(index):
        side, at = pieces[index]
        for inner in range(0, PIECE, LANES):
            offset = sides[side][1][at + inner : at + inner + LANES, :]
            offset = jnp.concatenate([offset] * (rows.shape[0] // LANES), axis=1)
            z = z_ref[index % 2, inner : inner + LANES, :] * LOG2_E + offset
            z = z.reshape(LANES // 8, 8, rows.shape[0])
            peaks.append(jnp.max(z, axis=0))
            masses.append(jnp.sum(jnp.exp2(z - peaks[-1]), axis=0))

    product(0)
    for index in range(len(pieces)):
        if index + 1 < len(pieces):
            product(index + 1)
        absorb(index)
    peak = jnp.max(functools.reduce(jnp.maximum, peaks), axis=0, keepdims=True)
    mass = sum(mass * jnp.exp2(high - peak) for high, mass in zip(peaks, masses))
    return peak * LOG_2 + jnp.log(jnp.sum(mass, axis=0, keepdims=True))


def put_offsets(offset_ref, column_ref, eye):
    for at in range(0, offset_ref.shape[1], LANES):
        column = to_column(offset_ref[:, at : at + LANES] * LOG2_E, eye)
        column_ref[at : at + LANES, :] = jnp.broadcast_to(column, (LANES, LANES))


def make_logits(rows, tgt_ref, offset_ref, z_ref):
    rows = rows * LOGIT_SCALE
    for at in range(0, tgt_ref.shape[0], CHUNK):
        cols = slice(at, at + CHUNK)
        dots = lax.dot_general(rows, tgt_ref[cols, :], NT_DIMS, preferred_element_type=jnp.float32)
        z_ref[:, cols] = (dots + offset_ref[:, cols]) * LOG2_E


def logits_kernel(sides, rows_ref, *refs):
    for side in range(sides):
        make_logits(rows_ref[...], refs[2 * side], refs[2 * side + 1], refs[2 * sides + side])


def prepare_kernel(turn, core_ref, *refs):
    inputs, refs = refs[:6], refs[6:]
    earlier, refs = refs[: 7 * (1 - turn)], refs[7 * (1 - turn) :]
    outs, scratch = refs[:7], refs[7:]

    @pl.when(core_ref[0] == turn)
    def work():
        prepare(*inputs, *outs, *scratch)

    if earlier:

        @pl.when(core_ref[0] != turn)
        def hand_on():
            for source, target in zip(earlier, outs):
                target[...] = source[...]


def prepare(
    src_hbm, tgt_hbm, pot_hbm, mass_hbm, slope_hbm, logmass_hbm,
    tgt_ref, offset_ref, column_ref, own_z_ref, lse_ref, line_ref, sum_ref,
    src_ref, pot_ref, mass_ref, slope_ref, logmass_ref, z_ref, sems,
):
    pairs = (
        (tgt_hbm, tgt_ref), (src_hbm, src_ref), (pot_hbm, pot_ref),
        (mass_hbm, mass_ref), (slope_hbm, slope_ref), (logmass_hbm, logmass_ref),
    )
    copies = [pltpu.make_async_copy(source, target, sems.at[at]) for at, (source, target) in enumerate(pairs)]
    for copy in copies:
        copy.start()
    for copy in copies[1:]:
        copy.wait()
    eye = diagonal()
    for group in range(src_ref.shape[0] // LANES):
        cols = slice(group * LANES, (group + 1) * LANES)
        square = to_lanes(squares(src_ref, group * LANES), eye)
        slope = slope_ref[group : group + 1, :]
        logmass = logmass_ref[group : group + 1, :]
        sum_ref[:, cols] = logmass + square
        line_ref[0:1, cols] = slope
        line_ref[1:2, cols] = slope * (logmass + square) + (logmass - square)
    copies[0].wait()
    for group in range(tgt_ref.shape[0] // LANES):
        at = group * LANES
        base = pot_ref[group : group + 1, :] + mass_ref[group : group + 1, :]
        offset_ref[:, at : at + LANES] = base - to_lanes(squares(tgt_ref, at), eye)
    put_offsets(offset_ref, column_ref, eye)
    lse_ref[...] = row_sums(src_ref[...], ((tgt_ref, column_ref),), z_ref)
    make_logits(src_ref[...], tgt_ref, offset_ref, own_z_ref)


def near_kernel(rows_ref, tgt_ref, offset_ref, held_ref, column_ref, lse_ref, z_ref):
    put_offsets(offset_ref, column_ref, diagonal())
    lse_ref[...] = merge(held_ref[...], row_sums(rows_ref[...], ((tgt_ref, column_ref),), z_ref))


def far_kernel(count, *refs):
    own_ref, own_column_ref, pair_ref, pair_column_ref, held_ref, line_ref = refs[count : count + 6]
    out_ref, z_ref = refs[count + 6 :]
    slots = count + 1
    out_ref[0:1, :] = held_ref[...]
    out_ref[slots : slots + 2, :] = line_ref[...]
    for slot in range(count):
        sides = ((own_ref, own_column_ref), (pair_ref, pair_column_ref))
        out_ref[slot + 1 : slot + 2, :] = row_sums(refs[slot][...], sides, z_ref)


def sum_columns(z_refs, offset, out_ref, off_ref, peak_ref, mass_ref):
    slots, src_count = offset.shape
    for slot in range(slots):
        for at in range(0, src_count, LANES):
            row = jnp.broadcast_to(offset[slot : slot + 1, at : at + LANES] * LOG2_E, (LANES, LANES))
            off_ref[slot, at : at + LANES, :] = jnp.transpose(row)

    parts = [(slot, at) for slot in range(slots) for at in range(0, src_count, LANES)]
    for left in range(0, z_refs[0].shape[1], CHUNK):
        cols = slice(left, left + CHUNK)
        for part, (slot, at) in enumerate(parts):
            rows = slice(at, at + LANES)
            offsets = jnp.concatenate([off_ref[slot, rows, :]] * (CHUNK // LANES), axis=1)
            z = (z_refs[slot][rows, cols] + offsets).reshape(LANES // 8, 8, CHUNK)
            peak = jnp.max(z, axis=0)
            peak_ref[part, :, cols] = peak
            mass_ref[part, :, cols] = jnp.sum(jnp.exp2(z - peak), axis=0)
    every = range(len(parts))
    peak = jnp.max(functools.reduce(jnp.maximum, [peak_ref[part] for part in every]), axis=0, keepdims=True)
    mass = sum(mass_ref[part] * jnp.exp2(peak_ref[part] - peak) for part in every)
    total = peak * LOG_2 + jnp.log(jnp.sum(mass, axis=0, keepdims=True))
    for group in range(out_ref.shape[0]):
        out_ref[group : group + 1, :] = total[:, group * LANES : (group + 1) * LANES]


def pair_kernel(slots, *refs):
    lse_ref, there_ref, slope_ref, shift_ref, out_ref, *scratch = refs[slots:]
    lse = merge(lse_ref[...], there_ref[...])
    sum_columns(refs[:slots], shift_ref[...] - slope_ref[...] * lse, out_ref, *scratch)


def own_kernel(turn, slots, *refs):
    z_refs, (lse_ref, there_ref, slope_ref, shift_ref, core_ref), refs = refs[:slots], refs[slots : slots + 5], refs[slots + 5 :]
    lse = merge(lse_ref[...], there_ref[...])
    if turn == 0:
        sum_ref, earlier_ref, out_ref, potential_ref, *scratch = refs
        potential_ref[...] = slope_ref[0:1, :] * (sum_ref[...] - lse[0:1, :])
    else:
        out_ref, *scratch = refs

    @pl.when(core_ref[0] == turn)
    def work():
        sum_columns(z_refs, shift_ref[...] - slope_ref[...] * lse, out_ref, *scratch)

    if turn == 0:

        @pl.when(core_ref[0] != turn)
        def hand_on():
            out_ref[...] = earlier_ref[...]


def f32(*shape):
    return jax.ShapeDtypeStruct(shape, jnp.float32)


def params(mebibytes):
    return pltpu.CompilerParams(vmem_limit_bytes=mebibytes * 1024 * 1024)


def shards(sources, targets, tgt_potential, src_logmass, tgt_logmass, src_exponent, tgt_exponent):
    src_count, width = sources.shape
    tgt_count = targets.shape[0]
    slabs = lax.axis_size("blk")
    sets = lax.axis_size("tsplit")
    chips = slabs // 2
    far = chips - 1
    groups = tgt_count // LANES
    src_groups = src_count // LANES
    assert chips > 1 and sets > 2 and chips & (chips - 1) == 0 and sets & (sets - 1) == 0

    def pair(value):
        return lax.ppermute(value, "blk", [(i, i ^ 1) for i in range(slabs)])

    def across(value, chip):
        return lax.ppermute(value, "blk", [(i, i ^ (2 * chip)) for i in range(slabs)])

    def along(value, step):
        return lax.ppermute(value, "tsplit", [(i, i ^ step) for i in range(sets)])

    def cost(blocks):
        pairs = blocks * src_count * tgt_count
        return pl.CostEstimate(flops=2 * pairs * width, bytes_accessed=2**20, transcendentals=pairs)

    core = lax.axis_index("blk") & 1
    core_word = core.astype(jnp.int32).reshape(1)
    pair_targets = pair(targets)
    inputs = (
        sources,
        targets,
        tgt_potential.reshape(groups, LANES),
        tgt_logmass.reshape(groups, LANES),
        src_exponent.reshape(src_groups, LANES),
        src_logmass.reshape(src_groups, LANES),
    )
    inputs = [pltpu.with_memory_space_constraint(x, pltpu.HBM) for x in inputs]

    product_space = pltpu.VMEM((2, PIECE, src_count), jnp.float32)

    def prepare_on(turn, *earlier):
        return pl.pallas_call(
            functools.partial(prepare_kernel, turn),
            out_shape=(
                jax.ShapeDtypeStruct(targets.shape, targets.dtype),
                f32(1, tgt_count),
                f32(tgt_count, LANES),
                f32(src_count, tgt_count),
                f32(1, src_count),
                f32(2, src_count),
                f32(1, src_count),
            ),
            in_specs=[SMEM] + [HBM] * 6 + [VMEM] * len(earlier),
            out_specs=(VMEM,) * 7,
            scratch_shapes=[pltpu.VMEM(x.shape, x.dtype) for x in (inputs[0], *inputs[2:])]
            + [product_space, pltpu.SemaphoreType.DMA((6,))],
            compiler_params=params(12),
            cost_estimate=cost(1),
            name=f"prepare_{turn}",
        )(core_word, *inputs, *earlier)

    earlier = prepare_on(1)
    first, sent = lax.optimization_barrier((earlier[6], sources))
    far_blocks = [across(sent, chip) for chip in range(1, chips)]
    held, offset, column, own_z, lse, line, src_sum = prepare_on(0, *earlier[:6], first)
    pair_offset = pair(offset)
    pair_column, lse = pl.pallas_call(
        near_kernel,
        out_shape=(f32(tgt_count, LANES), f32(1, src_count)),
        in_specs=[VMEM] * 4,
        out_specs=(VMEM,) * 2,
        scratch_shapes=[product_space],
        compiler_params=params(12),
        cost_estimate=cost(1),
        name="near_rows",
    )(sources, pair_targets, pair_offset, lse)
    far_lines = [across(line, chip) for chip in range(2, chips)]
    lse, *moved = lax.optimization_barrier((lse, *far_blocks, *far_lines))
    payload = pl.pallas_call(
        functools.partial(far_kernel, far),
        out_shape=f32(chips + 2, src_count),
        in_specs=[VMEM] * (far + 6),
        out_specs=VMEM,
        scratch_shapes=[product_space],
        compiler_params=params(12 + far),
        cost_estimate=cost(2 * far),
        name="far_rows",
    )(*moved[:far], held, column, pair_targets, pair_column, lse, line)

    payload, *blocks = lax.optimization_barrier((payload, sources, *moved[:far]))
    def logits(block, *sides):
        return pl.pallas_call(
            functools.partial(logits_kernel, len(sides) // 2),
            out_shape=(f32(src_count, tgt_count),) * (len(sides) // 2),
            in_specs=[VMEM] * (1 + len(sides)),
            out_specs=(VMEM,) * (len(sides) // 2),
            compiler_params=params(12),
            cost_estimate=cost(len(sides) // 2),
            name="logits",
        )(block, *sides)

    own_zs, pair_zs = [own_z], list(logits(blocks[0], pair_targets, pair_offset))
    for block in blocks[1:]:
        own_z, pair_z = logits(block, held, offset, pair_targets, pair_offset)
        own_zs.append(own_z)
        pair_zs.append(pair_z)

    def mirror(value, chip):
        return jnp.stack([value[slot ^ chip] for slot in range(chips)])

    other = across(payload, 1)
    beside = along(payload, 1)
    joined = lax.ppermute(
        payload,
        ("blk", "tsplit"),
        [(b * sets + z, (b ^ 2) * sets + (z ^ 1)) for b in range(slabs) for z in range(sets)],
    )
    lines = jnp.stack([line, other[chips:]] + moved[far:], axis=1)
    lse = merge(payload[:chips], mirror(other, 1), beside[:chips], mirror(joined, 1))
    chip = 2
    while chip < chips:
        lse = merge(lse, mirror(across(lse, chip), chip))
        chip *= 2
    step = 2
    while 2 * step < sets:
        lse = merge(lse, along(lse, step))
        step *= 2
    there = along(lse, step)

    def columns(kernel, zs, *more, outs=(f32(groups, LANES),)):
        return pl.pallas_call(
            kernel,
            out_shape=outs,
            in_specs=[VMEM] * (chips + 4) + [SMEM] * min(1, len(more)) + [VMEM] * (len(more) - 1),
            out_specs=(VMEM,) * len(outs),
            scratch_shapes=[
                pltpu.VMEM((chips, src_count, LANES), jnp.float32),
                pltpu.VMEM((chips * src_groups, 8, tgt_count), jnp.float32),
                pltpu.VMEM((chips * src_groups, 8, tgt_count), jnp.float32),
            ],
            compiler_params=params(8 + 2 * chips),
            cost_estimate=pl.CostEstimate(
                flops=6 * chips * src_count * tgt_count,
                bytes_accessed=2**20,
                transcendentals=chips * src_count * tgt_count,
            ),
            name="columns",
        )(*zs, lse, there, lines[0], lines[1], *more)

    (pair_part,) = columns(functools.partial(pair_kernel, chips), pair_zs)
    (early_part,) = columns(functools.partial(own_kernel, 1, chips), own_zs, core_word)
    there, pair_part, early_part = lax.optimization_barrier((there, pair_part, early_part))
    home = pair(pair_part)
    own_part, src_potential = columns(
        functools.partial(own_kernel, 0, chips),
        own_zs,
        core_word,
        src_sum,
        early_part,
        outs=(f32(groups, LANES), f32(1, src_count)),
    )
    total = merge(own_part, home).reshape(tgt_count)
    tgt_update = tgt_exponent * (2.0 * tgt_logmass + tgt_potential - total)
    return (src_potential.reshape(src_count), tgt_update)


def solution(mesh):
    placed = (
        P(("groups", "blk"), None),
        P(("groups", "blk", "tsplit"), None),
        P(("groups", "blk", "tsplit")),
        P(("groups", "blk")),
        P(("groups", "blk", "tsplit")),
        P(("groups", "blk")),
        P(("groups", "blk", "tsplit")),
    )
    return jax.shard_map(
        shards,
        mesh=mesh,
        in_specs=placed,
        out_specs=(P(("groups", "blk")), P(("groups", "blk", "tsplit"))),
        check_vma=False,
    )
```
